32 devices in a mesh: fsdp: 16 (over z, x, core), dp: 2 (over y).
Axes of the slice: x: 2, y: 2, z: 4, core: 2. Of those that a mesh axis runs over, the one named last changes fastest.
Arguments:
- inputs: bfloat16 [32, 1024, 1024], P(('fsdp', 'dp')), may hold values from -6 to 6
- encoder: bfloat16 [32, 1024, 1024], P(('fsdp', 'dp')), may hold values from -6 to 6
- grad_out: bfloat16 [32, 1024, 1024], P(('fsdp', 'dp')), may hold values from -6 to 6
- target_mask: int32 [32, 1024], P(('fsdp', 'dp')), may hold values from 0 to 1, as said below
- source_lengths: int32 [32], P(('fsdp', 'dp')), may hold values from 16 to 1024, as said below
- step: int32 [1], replicated, may hold values from 250 to 999
- attn_in: bfloat16 [1024, 6144], P('fsdp'), may hold values from -0.1875 to 0.1875
- attn_out: bfloat16 [1024, 2048], P('fsdp'), may hold values from -0.75 to 0.75
- ffn_in: bfloat16 [1024, 4096], P('fsdp'), may hold values from -0.1875 to 0.1875
- ffn_in_bias: float32 [4096], replicated, may hold values from -1.75 to 1.75
- ffn_out: bfloat16 [4096, 1024], P('fsdp'), may hold values from -0.09375 to 0.09375
- ffn_out_bias: float32 [1024], replicated, may hold values from -1.75 to 1.75
- attn_bias: float32 [6, 1024], replicated, may hold values from -1.75 to 1.75
- norm_gain: float32 [3, 1024], replicated, may hold values from 0.5 to 1.5
- norm_shift: float32 [3, 1024], replicated, may hold values from -1.75 to 1.75
- adapter_down: bfloat16 [1024, 512], replicated, may hold values from -0.1875 to 0.1875
- adapter_down_bias: float32 [512], replicated, may hold values from -1.75 to 1.75
- adapter_up: bfloat16 [512, 1024], replicated, may hold values from -0.25 to 0.25
- adapter_up_bias: float32 [1024], replicated, may hold values from -1.75 to 1.75
- adapter_gain: float32 [1024], replicated, may hold values from 0.5 to 1.5
- adapter_shift: float32 [1024], replicated, may hold values from -1.75 to 1.75
Outputs:
- layer_out: bfloat16 [32, 1024, 1024], P(('fsdp', 'dp'))
- grad_input: float32 [32, 1024, 1024], P(('fsdp', 'dp'))
- grad_encoder: float32 [32, 1024, 1024], P(('fsdp', 'dp'))
- grad_down: float32 [1024, 512], replicated
- grad_down_bias: float32 [512], replicated
- grad_up: float32 [512, 1024], replicated
- grad_up_bias: float32 [1024], replicated
- grad_gain: float32 [1024], replicated
- grad_shift: float32 [1024], replicated
The draws below stay inside these ranges and needn't reach their ends.
Inputs may be any that keep to these rules, and one draw needn't show every extreme that they name: `target_mask`: each row is 1 on its first positions and 0 after them, with at least half of 1024 ones; the first sequence is all ones and the second has exactly half of 1024 ones. `source_lengths`: the first sequence has 1024, the last the least value.
All inputs are finite; a program needn't handle non-finite values.
Results may differ from the reference program's by a relative error of at most 0.023.
Values may be sent and summed in bfloat16 or wider, within the bound.
No kernel may reach another device: no remote copies, remote signals or barrier semaphores. Data moves between devices by JAX's collectives and lax.ppermute only.
A program may use at most 256 MiB of HBM per device.

```python
import jax
import jax.numpy as jnp
from jax import lax

D = 1024
HEADS = 16
FF = 4096
A = 512
LEN = 1024
SRC = 1024
RAMP = 1000
BATCH = 32


def draw_target_mask(key, part):
    cutoff = jax.random.randint(key, (BATCH,), 0, LEN // 2)
    lengths = LEN - cutoff
    lengths = lengths.at[0].set(LEN).at[1].set(LEN // 2)
    places = jnp.arange(LEN, dtype=jnp.int32)
    return (places[None, :] < lengths[:, None]).astype(jnp.int32)


def draw_source_lengths(key, part):
    key_power = jax.random.fold_in(key, 11)
    key_trim = jax.random.fold_in(key, 23)
    power = jax.random.randint(key_power, (BATCH,), 0, 6)
    base_len = SRC // jnp.left_shift(jnp.int32(1), power)
    trimmed = jax.random.randint(key_trim, (BATCH,), 0, base_len // 2 + 1)
    lengths = base_len - trimmed
    lengths = lengths.at[0].set(SRC).at[BATCH - 1].set(max(1, SRC // 64))
    return lengths.astype(jnp.int32)


def block_scale(own_key, shape, shards, low, high):
    def one(axis_at, shards_of):
        heights = jax.random.uniform(jax.random.fold_in(jax.random.fold_in(own_key, 6), axis_at), (shards_of,), jnp.float32, low / len(shards), high / len(shards))
        return jnp.repeat(jnp.exp(heights), shape[axis_at] // shards_of).reshape((-1,) + (1,) * (len(shape) - axis_at - 1))

    level = one(*shards[0])
    for cut in shards[1:]:
        level = level * one(*cut)
    return level


def normal_values(stream_key, dims, scale, limit, pieces=(), held_as=jnp.bfloat16):
    level = block_scale(stream_key, dims, pieces, -0.22, 0.18) if pieces else 1.0
    values = jax.random.normal(stream_key, dims, jnp.float32) * scale * level
    return jnp.minimum(jnp.maximum(values, -limit), limit).astype(held_as)


def setup_inputs(seed: int = 0) -> dict:
    key_of = jax.random.split(jax.random.key(seed), 22)
    inputs = normal_values(key_of[0], (BATCH, LEN, D), 1.0, 6.0, ((0, 32),))
    encoder = normal_values(key_of[1], (BATCH, SRC, D), 1.0, 6.0, ((0, 32),))
    grad_out = normal_values(key_of[2], (BATCH, LEN, D), 1.0, 6.0, ((0, 32),))
    target_mask = draw_target_mask(jax.random.fold_in(key_of[21], 71), 0)
    source_lengths = draw_source_lengths(jax.random.fold_in(key_of[21], 71), 0)
    step = jax.random.randint(key_of[5], (1,), RAMP // 4, RAMP).astype(jnp.int32)
    attn_in = normal_values(key_of[6], (D, 6 * D), D ** -0.5, 0.1875, ((0, 16),))
    attn_out = normal_values(key_of[7], (D, 2 * D), (D // 16) ** -0.5, 0.75, ((0, 16),))
    ffn_in = normal_values(key_of[8], (D, FF), D ** -0.5, 0.1875, ((0, 16),))
    ffn_in_bias = normal_values(key_of[9], (FF,), 0.3, 1.75, (), jnp.float32)
    ffn_out = normal_values(key_of[10], (FF, D), FF ** -0.5, 0.09375, ((0, 16),))
    ffn_out_bias = normal_values(key_of[11], (D,), 0.3, 1.75, (), jnp.float32)
    attn_bias = normal_values(key_of[12], (6, D), 0.3, 1.75, (), jnp.float32)
    norm_gain = jnp.clip(1.0 + 0.1 * jax.random.normal(key_of[13], (3, D), jnp.float32), 0.5, 1.5)
    norm_shift = normal_values(key_of[14], (3, D), 0.3, 1.75, (), jnp.float32)
    adapter_down = normal_values(key_of[15], (D, A), D ** -0.5, 0.1875)
    adapter_down_bias = normal_values(key_of[16], (A,), 0.3, 1.75, (), jnp.float32)
    adapter_up = normal_values(key_of[17], (A, D), A ** -0.5, 0.25)
    adapter_up_bias = normal_values(key_of[18], (D,), 0.3, 1.75, (), jnp.float32)
    adapter_gain = jnp.clip(1.0 + 0.1 * jax.random.normal(key_of[19], (D,), jnp.float32), 0.5, 1.5)
    adapter_shift = normal_values(key_of[20], (D,), 0.3, 1.75, (), jnp.float32)
    return {"inputs": inputs, "encoder": encoder, "grad_out": grad_out, "target_mask": target_mask, "source_lengths": source_lengths, "step": step, "attn_in": attn_in, "attn_out": attn_out, "ffn_in": ffn_in, "ffn_in_bias": ffn_in_bias, "ffn_out": ffn_out, "ffn_out_bias": ffn_out_bias, "attn_bias": attn_bias, "norm_gain": norm_gain, "norm_shift": norm_shift, "adapter_down": adapter_down, "adapter_down_bias": adapter_down_bias, "adapter_up": adapter_up, "adapter_up_bias": adapter_up_bias, "adapter_gain": adapter_gain, "adapter_shift": adapter_shift}


@jax.custom_vjp
def low(v):
    return lax.optimization_barrier(v.astype(jnp.bfloat16)).astype(jnp.float32)

@jax.custom_vjp
def low_back(v):
    return v

def low_keep(v):
    return (low(v), None)

def low_pass(kept, grad):
    return (grad,)

def back_keep(v):
    return (v, None)

def back_low(kept, grad):
    return (low(grad),)
low.defvjp(low_keep, low_pass)
low_back.defvjp(back_keep, back_low)

def rounded_both(value):
    return low(low_back(value))

def project(left, right):
    return jnp.dot(left, right, precision=lax.Precision.HIGHEST)

def norm_rows(values, gain, shift):
    center = values - lax.optimization_barrier(jnp.mean(values, -1, keepdims=True))
    spread = lax.optimization_barrier(jnp.mean(center * center, -1, keepdims=True))
    return center * lax.rsqrt(spread + 1e-05) * gain + shift

def attend(queries, key_rows, value_rows, allowed):
    length, width = queries.shape
    head_size = width // HEADS
    query_heads = queries.reshape(length, HEADS, head_size)
    key_heads = key_rows.reshape(key_rows.shape[0], HEADS, head_size)
    value_heads = value_rows.reshape(value_rows.shape[0], HEADS, head_size)
    scores = jnp.einsum('qhe,khe->hqk', query_heads, key_heads, precision=lax.Precision.HIGHEST) * head_size ** (-0.5)
    scores = low_back(scores)
    scores = jnp.where(allowed[None], scores, -1e+30)
    row_max = lax.optimization_barrier(jnp.max(scores, -1, keepdims=True))
    expo = jnp.exp(scores - row_max)
    probs = rounded_both(expo / lax.optimization_barrier(jnp.sum(expo, -1, keepdims=True)))
    context = jnp.einsum('hqk,khe->qhe', probs, value_heads, precision=lax.Precision.HIGHEST)
    return rounded_both(context.reshape(length, width))

def reference(inputs, encoder, grad_out, target_mask, source_lengths, step, attn_in, attn_out, ffn_in, ffn_in_bias, ffn_out, ffn_out_bias, attn_bias, norm_gain, norm_shift, adapter_down, adapter_down_bias, adapter_up, adapter_up_bias, adapter_gain, adapter_shift):
    width = D
    w_in = attn_in.astype(jnp.float32)
    w_out = attn_out.astype(jnp.float32)
    w_first = ffn_in.astype(jnp.float32)
    w_second = ffn_out.astype(jnp.float32)
    first_bias = ffn_in_bias.astype(jnp.float32)
    second_bias = ffn_out_bias.astype(jnp.float32)
    biases = attn_bias.astype(jnp.float32)
    gains = norm_gain.astype(jnp.float32)
    shifts = norm_shift.astype(jnp.float32)
    ramp = 4.0 * step[0].astype(jnp.float32) / RAMP
    trainable = (adapter_down.astype(jnp.float32), adapter_down_bias.astype(jnp.float32), adapter_up.astype(jnp.float32), adapter_up_bias.astype(jnp.float32), adapter_gain.astype(jnp.float32), adapter_shift.astype(jnp.float32))
    positions = jnp.arange(LEN, dtype=jnp.int32)
    slots = jnp.arange(SRC, dtype=jnp.int32)

    def one_sequence(totals, items):
        seq_in, seq_enc, seq_grad, seq_mask, seq_len = items
        self_allowed = (positions[None, :] <= positions[:, None]) & (seq_mask.astype(jnp.int32)[None, :] > 0)
        cross_allowed = jnp.broadcast_to(slots[None, :] < seq_len.astype(jnp.int32), (LEN, SRC))

        def forward(tokens, states, params):
            down_w, down_b, up_w, up_b, gain_a, shift_a = params
            self_q = rounded_both(project(tokens, w_in[:, 0:width]) + biases[0])
            self_k = rounded_both(project(tokens, w_in[:, width:2 * width]))
            self_v = rounded_both(project(tokens, w_in[:, 2 * width:3 * width]) + biases[1])
            self_ctx = attend(self_q, self_k, self_v, self_allowed)
            attn_one = low_back(project(self_ctx, w_out[:, 0:width]) + biases[2])
            hidden1 = norm_rows(tokens + attn_one, gains[0], shifts[0])
            cross_q = rounded_both(project(low(hidden1), w_in[:, 3 * width:4 * width]) + biases[3])
            cross_k = rounded_both(project(states, w_in[:, 4 * width:5 * width]))
            cross_v = rounded_both(project(states, w_in[:, 5 * width:6 * width]) + biases[4])
            cross_ctx = attend(cross_q, cross_k, cross_v, cross_allowed)
            attn_two = low_back(project(cross_ctx, w_out[:, width:2 * width]) + biases[5])
            hidden2 = norm_rows(hidden1 + attn_two, gains[1], shifts[1])
            pre = low_back(project(low(hidden2), w_first) + first_bias)
            act = rounded_both(jax.nn.gelu(pre, approximate=False))
            ffn_part = low_back(project(act, w_second) + second_bias)
            adapt_in = low(norm_rows(hidden2, gain_a, shift_a))
            lower = low_back(project(adapt_in, down_w) + down_b)
            adapt_act = rounded_both(jax.nn.silu(lower))
            branch = low_back(project(adapt_act, up_w) + up_b)
            return norm_rows(hidden2 + ffn_part + ramp * branch, gains[2], shifts[2])
        result, pull = jax.vjp(forward, seq_in.astype(jnp.float32), seq_enc.astype(jnp.float32), trainable)
        grad_tokens, grad_states, grad_params = pull(seq_grad.astype(jnp.float32))
        totals = jax.tree.map(lambda left, right: left + right.astype(jnp.float32), totals, grad_params)
        return (totals, (result.astype(jnp.bfloat16), grad_tokens.astype(jnp.float32), grad_states.astype(jnp.float32)))
    zeros = jax.tree.map(lambda value: jnp.zeros(value.shape, jnp.float32), trainable)
    totals, outputs = lax.scan(one_sequence, zeros, (inputs, encoder, grad_out, target_mask, source_lengths))
    layer_out, grad_input, grad_encoder = outputs
    factor = (BATCH * LEN) ** (-0.5)
    totals = jax.tree.map(lambda total: total * factor, totals)
    return (layer_out, grad_input, grad_encoder, totals[0], totals[1], totals[2], totals[3], totals[4], totals[5])
```

```python
import functools
import math

import jax
import jax.numpy as jnp
from jax import lax
from jax.experimental import pallas as pl
from jax.experimental.pallas import tpu as pltpu
from jax.sharding import PartitionSpec as P

HEADS = 16
RAMP = 1000
EPS = 1e-05
F32 = jnp.float32
BF16 = jnp.bfloat16
VMEM_LIMIT = 58 * 2**20


def dot(left, right, left_dim, right_dim):
    return lax.dot_general(
        left, right, (((left_dim,), (right_dim,)), ((), ())), preferred_element_type=F32
    )


def call(kernel, name, grid, in_specs, out_specs, out_shape, flops, moved, exps=0, scratch=()):
    return pl.pallas_call(
        kernel,
        name=name,
        grid=grid,
        in_specs=in_specs,
        out_specs=out_specs,
        out_shape=out_shape,
        scratch_shapes=scratch,
        compiler_params=pltpu.CompilerParams(vmem_limit_bytes=VMEM_LIMIT),
        cost_estimate=pl.CostEstimate(
            flops=int(flops), bytes_accessed=int(moved), transcendentals=int(exps)
        ),
    )


def whole(shape):
    return pl.BlockSpec(shape, lambda *_: (0,) * len(shape))


def rows_block(rows, width):
    return pl.BlockSpec((rows, width), lambda i: (i, 0))


def normalize(values):
    center = values - jnp.mean(values, -1, keepdims=True)
    scale = lax.rsqrt(jnp.mean(center * center, -1, keepdims=True) + EPS)
    return center * scale, scale


def normalize_back(normal, scale, grad):
    return scale * (
        grad
        - jnp.mean(grad, -1, keepdims=True)
        - normal * jnp.mean(grad * normal, -1, keepdims=True)
    )


def split_three(values):
    high = values.astype(BF16).astype(F32)
    middle = (values - high).astype(BF16).astype(F32)
    return high, middle, values - high - middle


def key_extra(live):
    lane = jnp.arange(128) % 64
    bias = jnp.where(live, 0.0, -1e30)[:, None]
    ones = jnp.where((lane >= 1) & (lane <= 3), 1.0, 0.0)[None]
    return jnp.where(lane[None] == 0, bias, ones).astype(BF16)


def attend_forward_kernel(causal, chunk, ahead, q_ref, k_ref, v_ref, extra_ref, out_ref, lse_ref):
    rows, width = q_ref.shape
    keys, half = k_ref.shape[0], width // 2
    lane = lax.broadcasted_iota(jnp.int32, (rows, width), 1)
    key_lane = lax.broadcasted_iota(jnp.int32, (keys, width), 1)
    queries = q_ref[...] * jnp.asarray(half**-0.5, BF16)
    picks = jnp.where(lane % half == 0, 1.0, 0.0).astype(BF16)
    key_rows, extra, value_rows = k_ref[...], extra_ref[...], v_ref[...]
    one = jnp.asarray(1.0, BF16)
    head_q = [jnp.where(lane < half, queries, picks), jnp.where(lane < half, picks, queries)]
    head_k = [
        jnp.where(key_lane < half, key_rows, extra),
        jnp.where(key_lane < half, extra, key_rows),
    ]
    head_v = [
        jnp.where(key_lane < half, value_rows, one),
        jnp.where(key_lane < half, one, value_rows),
    ]

    def scores(at, head):
        low, high = at * chunk, (at + 1) * chunk
        live = high if causal else keys
        found = dot(head_q[head][low:high], head_k[head][:live], 1, 1)
        if not causal:
            return found
        query_at = lax.broadcasted_iota(jnp.int32, (chunk, chunk), 0)
        key_at = lax.broadcasted_iota(jnp.int32, (chunk, chunk), 1)
        edge = jnp.where(key_at <= query_at, found[:, low:high], -1e30)
        return jnp.concatenate([found[:, :low], edge], 1) if low else edge

    def mix(head, found):
        top = jnp.max(found, 1, keepdims=True)
        expo = jnp.exp(found - top).astype(BF16)
        mixed = dot(expo, head_v[head][: found.shape[1]], 1, 0)
        return mixed / pltpu.roll(mixed, half, 1), top + jnp.log(mixed)

    units = [(at, head) for at in range(rows // chunk) for head in range(2)]
    done, waiting = {}, []
    for unit in units:
        waiting.append((unit, scores(*unit)))
        if len(waiting) > ahead:
            first, found = waiting.pop(0)
            done[first] = mix(first[1], found)
    for first, found in waiting:
        done[first] = mix(first[1], found)
    left = lane[:chunk] < half
    place = lane[:chunk] % half
    for at in range(rows // chunk):
        low, high = at * chunk, (at + 1) * chunk
        out_ref[low:high, :] = jnp.where(left, done[at, 0][0], done[at, 1][0]).astype(BF16)
        parts = split_three(-jnp.where(left, done[at, 1][1], done[at, 0][1]))
        packed = jnp.where(place == 0, 1.0, 0.0)
        for index, part in enumerate(parts):
            packed = jnp.where(place == index + 1, part, packed)
        lse_ref[low:high, :] = packed.astype(BF16)


def attend_backward_kernel(
    causal, chunk, q_ref, k_ref, v_ref, out_ref, grad_ref, lse_ref, extra_ref,
    dq_ref, dk_ref, dv_ref, p_scr, s_scr,
):
    rows, width = q_ref.shape
    keys, half = k_ref.shape[0], width // 2
    scale = half**-0.5
    count = rows // chunk
    lane = lax.broadcasted_iota(jnp.int32, (rows, width), 1)
    key_lane = lax.broadcasted_iota(jnp.int32, (keys, width), 1)
    queries = q_ref[...] * jnp.asarray(scale, BF16)
    lse, extra = lse_ref[...], extra_ref[...]
    key_rows, value_rows, grads = k_ref[...], v_ref[...], grad_ref[...]
    place = key_lane % half
    ones = jnp.where((place >= 1) & (place <= 3), 1.0, 0.0).astype(BF16)
    products = grads.astype(F32) * out_ref[...].astype(F32)
    queries_t, grads_t = queries.T, grads.T
    grad_q = [[None] * count, [None] * count]
    grad_k_t, grad_v_t = [], []
    for head in range(2):
        mine = (lane < half) if head == 0 else (lane >= half)
        key_mine = (key_lane < half) if head == 0 else (key_lane >= half)
        base = half if head == 0 else 0
        head_q = jnp.where(mine, queries, lse)
        head_k = jnp.where(key_mine, key_rows, extra)
        head_v = jnp.where(key_mine, value_rows, ones)
        head_g = grads.astype(F32)
        dots = split_three(-jnp.sum(jnp.where(mine, products, 0.0), 1, keepdims=True))
        head_g = jnp.where(mine, head_g, 0.0)
        for index, part in enumerate(dots):
            head_g = jnp.where(lane == base + index + 1, part, head_g)
        head_g = head_g.astype(BF16)
        span = slice(head * half, (head + 1) * half)
        for at in range(count):
            low, high = at * chunk, (at + 1) * chunk
            live = high if causal else keys
            probs = jnp.exp(dot(head_q[low:high], head_k[:live], 1, 1))
            if causal:
                query_at = lax.broadcasted_iota(jnp.int32, (chunk, chunk), 0)
                key_at = lax.broadcasted_iota(jnp.int32, (chunk, chunk), 1)
                edge = jnp.where(key_at <= query_at, probs[:, low:high], 0.0)
                probs = jnp.concatenate([probs[:, :low], edge], 1) if low else edge
            grad_s = (probs * dot(head_g[low:high], head_v[:live], 1, 1)).astype(BF16)
            p_scr[head, low:high, :live] = probs.astype(BF16)
            s_scr[head, low:high, :live] = grad_s
            grad_q[head][at] = dot(grad_s, key_rows[:live], 1, 0)
        if causal:
            for total, source, saved in (
                (grad_v_t, grads_t, p_scr),
                (grad_k_t, queries_t, s_scr),
            ):
                total.append(
                    jnp.concatenate(
                        [
                            dot(
                                source[span, at * chunk :],
                                saved[head, at * chunk :, at * chunk : (at + 1) * chunk],
                                1,
                                0,
                            )
                            for at in range(count)
                        ],
                        1,
                    )
                )
        else:
            grad_v_t.append(dot(grads_t[span], p_scr[head], 1, 0))
            grad_k_t.append(dot(queries_t[span], s_scr[head], 1, 0))
    for at in range(count):
        low, high = at * chunk, (at + 1) * chunk
        both = jnp.where(lane[low:high] < half, grad_q[0][at], grad_q[1][at])
        dq_ref[low:high, :] = (both * scale).astype(BF16)
    dk_ref[...] = jnp.concatenate(grad_k_t, 0).T.astype(BF16)
    dv_ref[...] = jnp.concatenate(grad_v_t, 0).T.astype(BF16)


def attend_forward(queries, q_at, key_rows, k_at, value_rows, v_at, extra, width, causal):
    rows, keys = queries.shape[0], key_rows.shape[0]

    def pair(count, first):
        return pl.BlockSpec((count, 128), lambda i: (0, i + first))

    return call(
        functools.partial(attend_forward_kernel, causal, 256, 2),
        "self_forward" if causal else "cross_forward",
        (width // 128,),
        [pair(rows, q_at), pair(keys, k_at), pair(keys, v_at), whole((keys, 128))],
        [pair(rows, 0), pair(rows, 0)],
        [jax.ShapeDtypeStruct((rows, width), BF16)] * 2,
        4 * rows * keys * width,
        12 * rows * width,
        rows * keys * HEADS,
    )(queries, key_rows, value_rows, extra)


def attend_backward(
    queries, q_at, key_rows, k_at, value_rows, v_at, mixed, grads, lse, extra, width, causal
):
    rows, keys = queries.shape[0], key_rows.shape[0]

    def pair(count, first):
        return pl.BlockSpec((count, 128), lambda i: (0, i + first))

    return call(
        functools.partial(attend_backward_kernel, causal, 256),
        "self_backward" if causal else "cross_backward",
        (width // 128,),
        [pair(rows, q_at), pair(keys, k_at), pair(keys, v_at)]
        + [pair(rows, 0)] * 3
        + [whole((keys, 128))],
        [pair(rows, 0), pair(keys, 0), pair(keys, 0)],
        [
            jax.ShapeDtypeStruct((rows, width), BF16),
            jax.ShapeDtypeStruct((keys, width), BF16),
            jax.ShapeDtypeStruct((keys, width), BF16),
        ],
        10 * rows * keys * width,
        18 * rows * width,
        rows * keys * HEADS,
        [pltpu.VMEM((2, rows, keys), BF16)] * 2,
    )(queries, key_rows, value_rows, mixed, grads, lse, extra)


def project_kernel(x_ref, w_ref, bias_ref, out_ref):
    out_ref[...] = (dot(x_ref[...], w_ref[...], 1, 0) + bias_ref[...]).astype(BF16)


def project(values, weight, first, columns, bias, name):
    rows, depth = values.shape
    step = 512
    return call(
        project_kernel,
        name,
        (columns // step,),
        [
            whole((rows, depth)),
            pl.BlockSpec((depth, step), lambda i: (0, i + first // step)),
            pl.BlockSpec((1, step), lambda i: (0, i)),
        ],
        pl.BlockSpec((rows, step), lambda i: (0, i)),
        jax.ShapeDtypeStruct((rows, columns), BF16),
        2 * rows * depth * columns,
        2 * (rows * depth + depth * columns + rows * columns),
    )(values, weight, bias)


def post_self_kernel(
    x_ref, ctx_ref, wo_ref, wq_ref, bo_ref, gain_ref, shift_ref, bq_ref, normal_ref, scale_ref, q_ref
):
    part = 256
    spans = [slice(at, at + part) for at in range(0, x_ref.shape[0], part)]
    sums = [
        x_ref[span].astype(F32) + dot(ctx_ref[span], wo_ref[...], 1, 0) + bo_ref[...]
        for span in spans
    ]
    for span, total in zip(spans, sums):
        normal, scale = normalize(total)
        normal_ref[span] = normal
        scale_ref[span] = jnp.broadcast_to(scale, (part, 128))
        hidden = (normal * gain_ref[...] + shift_ref[...]).astype(BF16)
        q_ref[span] = (dot(hidden, wq_ref[...], 1, 0) + bq_ref[...]).astype(BF16)


def post_self(values, context, weights, wo_at, wq_at, out_bias, gain, shift, q_bias):
    rows, width = values.shape
    step = 512
    vector = whole((1, width))
    return call(
        post_self_kernel,
        "post_self",
        (rows // step,),
        [
            rows_block(step, width),
            rows_block(step, width),
            pl.BlockSpec((width, width), lambda i: (0, wo_at)),
            pl.BlockSpec((width, width), lambda i: (0, wq_at)),
        ]
        + [vector] * 4,
        [rows_block(step, width), rows_block(step, 128), rows_block(step, width)],
        [
            jax.ShapeDtypeStruct((rows, width), F32),
            jax.ShapeDtypeStruct((rows, 128), F32),
            jax.ShapeDtypeStruct((rows, width), BF16),
        ],
        4 * rows * width * width,
        rows * width * 10 + 4 * width * width,
    )(values, context, weights, weights, out_bias, gain, shift, q_bias)


def post_cross_kernel(
    n1_ref, ctx_ref, wo_ref, bo_ref, gain_ref, shift_ref, gain2_ref, shift2_ref,
    normal_ref, scale_ref, hidden_ref,
):
    part = 256
    spans = [slice(at, at + part) for at in range(0, n1_ref.shape[0], part)]
    sums = [
        n1_ref[span] * gain_ref[...]
        + shift_ref[...]
        + dot(ctx_ref[span], wo_ref[...], 1, 0)
        + bo_ref[...]
        for span in spans
    ]
    for span, total in zip(spans, sums):
        normal, scale = normalize(total)
        normal_ref[span] = normal
        scale_ref[span] = jnp.broadcast_to(scale, (part, 128))
        hidden_ref[span] = (normal * gain2_ref[...] + shift2_ref[...]).astype(BF16)


def post_cross(normal, context, weights, wo_at, out_bias, gain, shift, gain2, shift2):
    rows, width = normal.shape
    step = 512
    vector = whole((1, width))
    return call(
        post_cross_kernel,
        "post_cross",
        (rows // step,),
        [
            rows_block(step, width),
            rows_block(step, width),
            pl.BlockSpec((width, width), lambda i: (0, wo_at)),
        ]
        + [vector] * 5,
        [rows_block(step, width), rows_block(step, 128), rows_block(step, width)],
        [
            jax.ShapeDtypeStruct((rows, width), F32),
            jax.ShapeDtypeStruct((rows, 128), F32),
            jax.ShapeDtypeStruct((rows, width), BF16),
        ],
        2 * rows * width * width,
        rows * width * 12 + 2 * width * width,
    )(normal, context, weights, out_bias, gain, shift, gain2, shift2)


def second_block(w_ref, held, width):
    pieces = []
    for at in range(0, w_ref.shape[0], held):
        for group in range(w_ref.shape[1] // width):
            pieces.append(w_ref[at : at + held, group * width : (group + 1) * width])
    return jnp.concatenate(pieces, 0)


def ffn_forward_kernel(held, h_ref, w1_ref, w2_ref, b1_ref, b2_ref, out_ref, slope_ref):
    rows, width = h_ref.shape
    part = 256
    second = second_block(w2_ref, held, width)

    @pl.when(pl.program_id(0) == 0)
    def _():
        out_ref[...] = jnp.broadcast_to(b2_ref[...], out_ref.shape)

    def first(at):
        return dot(h_ref[at : at + part], w1_ref[...], 1, 0) + b1_ref[...]

    def finish(at, pre):
        phi = 0.5 + 0.5 * lax.erf(pre * (0.5**0.5))
        act = (pre * phi).astype(BF16)
        slope = phi + pre * (jnp.exp(pre * pre * -0.5) * (1.0 / math.sqrt(2.0 * math.pi)))
        slope_ref[at : at + part] = slope.astype(BF16)
        out_ref[at : at + part] += dot(act, second, 1, 0)

    waiting = None
    for at in range(0, rows, part):
        pre = first(at)
        if waiting is not None:
            finish(*waiting)
        waiting = (at, pre)
    finish(*waiting)


def ffn_forward(hidden, weights, w2_at, w1_at, first_bias, second_bias, held):
    rows, width = hidden.shape
    wide = first_bias.shape[1]
    step = 512
    groups = wide // width
    return call(
        functools.partial(ffn_forward_kernel, held),
        "ffn_forward",
        (wide // step,),
        [
            whole((rows, width)),
            pl.BlockSpec((width, step), lambda i: (0, i + w1_at // step)),
            pl.BlockSpec((step // groups, wide), lambda i: (i, w2_at // wide)),
            pl.BlockSpec((1, step), lambda i: (0, i)),
            whole((1, width)),
        ],
        [whole((rows, width)), pl.BlockSpec((rows, step), lambda i: (0, i))],
        [jax.ShapeDtypeStruct((rows, width), F32), jax.ShapeDtypeStruct((rows, wide), BF16)],
        4 * rows * width * wide,
        6 * rows * width + 4 * width * wide + 2 * rows * wide,
        2 * rows * wide,
    )(hidden, weights, weights, first_bias, second_bias)


def ffn_backward_kernel(held, g_ref, w1_ref, w2_ref, slope_ref, start_ref, out_ref):
    rows, width = g_ref.shape
    part = 256
    second = second_block(w2_ref, held, width)

    @pl.when(pl.program_id(0) == 0)
    def _():
        out_ref[...] = start_ref[...]

    def finish(at, grad_act):
        grad_pre = (slope_ref[at : at + part].astype(F32) * grad_act).astype(BF16)
        out_ref[at : at + part] += dot(grad_pre, w1_ref[...], 1, 1)

    waiting = None
    for at in range(0, rows, part):
        grad_act = dot(g_ref[at : at + part], second, 1, 1)
        if waiting is not None:
            finish(*waiting)
        waiting = (at, grad_act)
    finish(*waiting)


def ffn_backward(grads, weights, w2_at, w1_at, slope, start, held):
    rows, width = grads.shape
    wide = slope.shape[1]
    step = 512
    groups = wide // width
    return call(
        functools.partial(ffn_backward_kernel, held),
        "ffn_backward",
        (wide // step,),
        [
            whole((rows, width)),
            pl.BlockSpec((width, step), lambda i: (0, i + w1_at // step)),
            pl.BlockSpec((step // groups, wide), lambda i: (i, w2_at // wide)),
            pl.BlockSpec((rows, step), lambda i: (0, i)),
            whole((rows, width)),
        ],
        whole((rows, width)),
        jax.ShapeDtypeStruct((rows, width), F32),
        4 * rows * width * wide,
        10 * rows * width + 4 * width * wide + 2 * rows * wide,
    )(grads, weights, weights, slope, start)


def adapter_kernel(
    ramp_ref, n2_ref, ffn_ref, go_ref, down_ref, up_ref, gain2_ref, shift2_ref, gain3_ref, shift3_ref,
    gain_a_ref, shift_a_ref, down_b_ref, up_b_ref,
    out_ref, gffn_ref, rest_ref, grad_down_ref, grad_up_ref, small_ref,
):
    ramp = ramp_ref[0]

    @pl.when(pl.program_id(0) == 0)
    def _():
        grad_down_ref[...] = jnp.zeros_like(grad_down_ref)
        grad_up_ref[...] = jnp.zeros_like(grad_up_ref)
        small_ref[...] = jnp.zeros_like(small_ref)

    hidden = n2_ref[...] * gain2_ref[...] + shift2_ref[...]
    normal_a, scale_a = normalize(hidden)
    adapt_in = (normal_a * gain_a_ref[...] + shift_a_ref[...]).astype(BF16)
    lower = dot(adapt_in, down_ref[...], 1, 0) + down_b_ref[...]
    gate = 1.0 / (1.0 + jnp.exp(-lower))
    adapt_act = (lower * gate).astype(BF16)
    branch = dot(adapt_act, up_ref[...], 1, 0) + up_b_ref[...]
    normal, scale = normalize(hidden + ffn_ref[...] + ramp * branch)
    out_ref[...] = (normal * gain3_ref[...] + shift3_ref[...]).astype(BF16)
    grad_sum = normalize_back(normal, scale, gain3_ref[...] * go_ref[...].astype(F32))
    gffn_ref[...] = grad_sum.astype(BF16)
    grad_branch = (ramp * grad_sum).astype(BF16)
    grad_up_ref[...] += dot(adapt_act, grad_branch, 0, 0)
    grad_act = dot(grad_branch, up_ref[...], 1, 1).astype(BF16).astype(F32)
    grad_lower = (gate * (1.0 + lower * (1.0 - gate)) * grad_act).astype(BF16)
    grad_down_ref[...] += dot(adapt_in, grad_lower, 0, 0)
    grad_adapt = dot(grad_lower, down_ref[...], 1, 1)
    rest_ref[...] = grad_sum + normalize_back(normal_a, scale_a, gain_a_ref[...] * grad_adapt)
    hidden_units = lower.shape[1]
    small_ref[0:1, 0:hidden_units] += jnp.sum(grad_lower.astype(F32), 0, keepdims=True)
    small_ref[1:2] += jnp.sum(grad_branch.astype(F32), 0, keepdims=True)
    small_ref[2:3] += jnp.sum(grad_adapt * normal_a, 0, keepdims=True)
    small_ref[3:4] += jnp.sum(grad_adapt, 0, keepdims=True)


def adapter(ramp, normal2, ffn, grad_out, down, up, vectors, down_bias):
    rows, width = normal2.shape
    units = down.shape[1]
    step = 256
    vector = whole((1, width))
    gain2, shift2, gain3, shift3, gain_a, shift_a, up_bias = vectors
    return call(
        adapter_kernel,
        "adapter",
        (rows // step,),
        [pl.BlockSpec(memory_space=pltpu.SMEM)]
        + [rows_block(step, width)] * 3
        + [whole(down.shape), whole(up.shape)]
        + [vector] * 6
        + [whole((1, units)), vector],
        [rows_block(step, width)] * 3 + [whole(down.shape), whole(up.shape), whole((8, width))],
        [
            jax.ShapeDtypeStruct((rows, width), BF16),
            jax.ShapeDtypeStruct((rows, width), BF16),
            jax.ShapeDtypeStruct((rows, width), F32),
            jax.ShapeDtypeStruct(down.shape, F32),
            jax.ShapeDtypeStruct(up.shape, F32),
            jax.ShapeDtypeStruct((8, width), F32),
        ],
        12 * rows * width * units,
        18 * rows * width + 12 * width * units,
        rows * units,
    )(
        ramp, normal2, ffn, grad_out, down, up, gain2, shift2, gain3, shift3, gain_a, shift_a,
        down_bias, up_bias,
    )


def norm_back_kernel(g_ref, normal_ref, scale_ref, gain_ref, wo_ref, sum_ref, ctx_ref):
    part = 256
    for at in range(0, g_ref.shape[0], part):
        span = slice(at, at + part)
        grad = normalize_back(normal_ref[span], scale_ref[span, 0:1], gain_ref[...] * g_ref[span])
        sum_ref[span] = grad
        ctx_ref[span] = dot(grad.astype(BF16), wo_ref[...], 1, 1).astype(BF16)


def norm_back_query_kernel(
    g_ref, dq_ref, wq_ref, normal_ref, scale_ref, gain_ref, wo_ref, sum_ref, ctx_ref
):
    part = 256
    spans = [slice(at, at + part) for at in range(0, g_ref.shape[0], part)]
    totals = [g_ref[span] + dot(dq_ref[span], wq_ref[...], 1, 1) for span in spans]
    for span, total in zip(spans, totals):
        grad = normalize_back(normal_ref[span], scale_ref[span, 0:1], gain_ref[...] * total)
        sum_ref[span] = grad
        ctx_ref[span] = dot(grad.astype(BF16), wo_ref[...], 1, 1).astype(BF16)


def norm_back(grads, normal, scale, gain, weights, wo_at, query_grads=None, wq_at=None):
    rows, width = grads.shape
    step = 512
    block = rows_block(step, width)
    with_query = query_grads is not None
    extra_specs = [block, pl.BlockSpec((width, width), lambda i: (0, wq_at))] if with_query else []
    extra = [query_grads, weights] if with_query else []
    return call(
        norm_back_query_kernel if with_query else norm_back_kernel,
        "norm_one_back" if with_query else "norm_two_back",
        (rows // step,),
        [block]
        + extra_specs
        + [
            block,
            rows_block(step, 128),
            whole((1, width)),
            pl.BlockSpec((width, width), lambda i: (0, wo_at)),
        ],
        [block, block],
        [jax.ShapeDtypeStruct((rows, width), F32), jax.ShapeDtypeStruct((rows, width), BF16)],
        (4 if with_query else 2) * rows * width * width,
        16 * rows * width + 4 * width * width,
    )(grads, *extra, normal, scale, gain, weights)


def back_project_kernel(count, with_start, *refs):
    grads, rest = refs[:count], refs[count:]
    weights, rest = rest[:count], rest[count:]
    total = sum(dot(g[...], w[...], 1, 1) for g, w in zip(grads, weights))
    if with_start:
        total = total + rest[0][...]
    rest[-1][...] = total


def back_project(grads, weights, first, start, name):
    rows, width = grads[0].shape
    step = 256
    count = len(grads)
    column = pl.BlockSpec((rows, step), lambda i: (0, i))

    def row_of(at):
        return pl.BlockSpec((step, width), lambda i: (i, at))

    return call(
        functools.partial(back_project_kernel, count, start is not None),
        name,
        (width // step,),
        [whole((rows, width))] * count
        + [row_of(first + at) for at in range(count)]
        + ([column] if start is not None else []),
        column,
        jax.ShapeDtypeStruct((rows, width), F32),
        2 * rows * width * width * count,
        rows * width * (2 * count + 8) + 2 * count * width * width,
    )(*grads, *([weights] * count), *([start] if start is not None else []))


def local(
    inputs,
    encoder,
    grad_out,
    target_mask,
    source_lengths,
    step,
    attn_in,
    attn_out,
    ffn_in,
    ffn_in_bias,
    ffn_out,
    ffn_out_bias,
    attn_bias,
    norm_gain,
    norm_shift,
    adapter_down,
    adapter_down_bias,
    adapter_up,
    adapter_up_bias,
    adapter_gain,
    adapter_shift,
):
    sequences, row_count, width = inputs.shape
    source_count = encoder.shape[1]
    held = attn_in.shape[0]
    groups = ffn_out.shape[0] // held
    wide = ffn_in.shape[1]
    self_w = lax.all_gather(attn_in[:, 0 : 3 * width], "fsdp", axis=0, tiled=True)
    rest_w = jnp.concatenate(
        [ffn_out[at * held : (at + 1) * held] for at in range(groups)]
        + [ffn_in, attn_in[:, 3 * width :], attn_out],
        1,
    )
    rest_w = lax.all_gather(rest_w, "fsdp", axis=0, tiled=True)
    w1_at, w2_at = wide, 0
    cq_at = 2 * wide // width
    ck_at, so_at, co_at = cq_at + 1, cq_at + 3, cq_at + 4

    ramp = (4.0 * step.astype(F32) / RAMP).reshape(1)
    bias = [attn_bias[at : at + 1] for at in range(6)]
    gain = [norm_gain[at : at + 1] for at in range(3)]
    shift = [norm_shift[at : at + 1] for at in range(3)]
    none = jnp.zeros((1, width), F32)
    tokens, states = inputs.reshape(-1, width), encoder.reshape(-1, width)
    self_extra = key_extra(target_mask.reshape(-1) > 0)
    cross_extra = key_extra(jnp.arange(source_count, dtype=jnp.int32) < source_lengths[0])
    per = width // 128

    qkv = project(
        tokens, self_w, 0, 3 * width, jnp.concatenate([bias[0], none, bias[1]], 1), "self_project"
    )
    self_ctx, self_lse = attend_forward(
        qkv, 0, qkv, per, qkv, 2 * per, self_extra, width, True
    )
    normal1, scale1, cross_q = post_self(
        tokens, self_ctx, rest_w, so_at, cq_at, bias[2], gain[0], shift[0], bias[3]
    )
    cross_kv = project(
        states, rest_w, ck_at * width, 2 * width, jnp.concatenate([none, bias[4]], 1), "cross_project"
    )
    cross_ctx, cross_lse = attend_forward(
        cross_q, 0, cross_kv, 0, cross_kv, per, cross_extra, width, False
    )
    normal2, scale2, hidden2 = post_cross(
        normal1, cross_ctx, rest_w, co_at, bias[5], gain[0], shift[0], gain[1], shift[1]
    )
    ffn, slope = ffn_forward(
        hidden2, rest_w, w2_at, w1_at, ffn_in_bias[None], ffn_out_bias[None], held
    )
    layer_out, grad_ffn, grad_rest, grad_down, grad_up, small = adapter(
        ramp,
        normal2,
        ffn,
        grad_out.reshape(-1, width),
        adapter_down,
        adapter_up,
        (
            gain[1], shift[1], gain[2], shift[2], adapter_gain[None], adapter_shift[None],
            adapter_up_bias[None],
        ),
        adapter_down_bias[None],
    )
    grad_down, grad_up, small = lax.psum((grad_down, grad_up, small), ("fsdp", "dp"))
    grad_hidden2 = ffn_backward(grad_ffn, rest_w, w2_at, w1_at, slope, grad_rest, held)
    grad_sum2, grad_cross = norm_back(grad_hidden2, normal2, scale2, gain[1], rest_w, co_at)
    cross_dq, cross_dk, cross_dv = attend_backward(
        cross_q, 0, cross_kv, 0, cross_kv, per, cross_ctx, grad_cross, cross_lse, cross_extra,
        width, False,
    )
    grad_encoder = back_project((cross_dk, cross_dv), rest_w, ck_at, None, "encoder_back")
    grad_sum1, grad_self = norm_back(
        grad_sum2, normal1, scale1, gain[0], rest_w, so_at, cross_dq, cq_at
    )
    self_grads = attend_backward(
        qkv, 0, qkv, per, qkv, 2 * per, self_ctx, grad_self, self_lse, self_extra, width, True
    )
    grad_input = back_project(self_grads, self_w, 0, grad_sum1, "input_back")

    token_total = sequences * row_count * lax.axis_size("fsdp") * lax.axis_size("dp")
    factor = 1.0 / math.sqrt(token_total)
    units = adapter_down.shape[1]
    return (
        layer_out.reshape(inputs.shape),
        grad_input.reshape(inputs.shape),
        grad_encoder.reshape(encoder.shape),
        grad_down * factor,
        small[0, :units] * factor,
        grad_up * factor,
        small[1] * factor,
        small[2] * factor,
        small[3] * factor,
    )


def solution(mesh):
    batch = P(("fsdp", "dp"), None, None)
    split = P("fsdp", None)
    placed = (
        (batch,) * 3
        + (P(("fsdp", "dp"), None), P(("fsdp", "dp")), P())
        + (split, split, split, P(), split)
        + (P(),) * 10
    )
    return jax.shard_map(
        local,
        mesh=mesh,
        in_specs=placed,
        out_specs=(batch,) * 3 + (P(),) * 6,
        check_vma=False,
    )
```

```python
import functools
import math

import jax
import jax.numpy as jnp
from jax import lax
from jax.experimental import pallas as pl
from jax.experimental.pallas import tpu as pltpu
from jax.sharding import PartitionSpec as P

HEADS = 16
RAMP = 1000
EPS = 1e-05
F32 = jnp.float32
BF16 = jnp.bfloat16
VMEM_LIMIT = 58 * 2**20


def dot(left, right, left_dim, right_dim):
    return lax.dot_general(
        left, right, (((left_dim,), (right_dim,)), ((), ())), preferred_element_type=F32
    )


def call(kernel, name, grid, in_specs, out_specs, out_shape, flops, moved, exps=0, scratch=()):
    return pl.pallas_call(
        kernel,
        name=name,
        grid=grid,
        in_specs=in_specs,
        out_specs=out_specs,
        out_shape=out_shape,
        scratch_shapes=scratch,
        compiler_params=pltpu.CompilerParams(vmem_limit_bytes=VMEM_LIMIT),
        cost_estimate=pl.CostEstimate(
            flops=int(flops), bytes_accessed=int(moved), transcendentals=int(exps)
        ),
    )


def whole(shape):
    return pl.BlockSpec(shape, lambda *_: (0,) * len(shape))


def rows_block(rows, width):
    return pl.BlockSpec((rows, width), lambda i: (i, 0))


def normalize(values):
    center = values - jnp.mean(values, -1, keepdims=True)
    scale = lax.rsqrt(jnp.mean(center * center, -1, keepdims=True) + EPS)
    return center * scale, scale


def normalize_back(normal, scale, grad):
    return scale * (
        grad
        - jnp.mean(grad, -1, keepdims=True)
        - normal * jnp.mean(grad * normal, -1, keepdims=True)
    )


def split_three(values):
    high = values.astype(BF16).astype(F32)
    middle = (values - high).astype(BF16).astype(F32)
    return high, middle, values - high - middle


def key_extra(live):
    lane = jnp.arange(128) % 64
    bias = jnp.where(live, 0.0, -1e30)[:, None]
    ones = jnp.where((lane >= 1) & (lane <= 3), 1.0, 0.0)[None]
    return jnp.where(lane[None] == 0, bias, ones).astype(BF16)


def attend_forward_kernel(causal, chunk, ahead, q_ref, k_ref, v_ref, extra_ref, out_ref, lse_ref):
    rows, width = q_ref.shape
    keys, half = k_ref.shape[0], width // 2
    lane = lax.broadcasted_iota(jnp.int32, (rows, width), 1)
    key_lane = lax.broadcasted_iota(jnp.int32, (keys, width), 1)
    queries = q_ref[...] * jnp.asarray(half**-0.5, BF16)
    picks = jnp.where(lane % half == 0, 1.0, 0.0).astype(BF16)
    key_rows, extra, value_rows = k_ref[...], extra_ref[...], v_ref[...]
    one = jnp.asarray(1.0, BF16)
    head_q = [jnp.where(lane < half, queries, picks), jnp.where(lane < half, picks, queries)]
    head_k = [
        jnp.where(key_lane < half, key_rows, extra),
        jnp.where(key_lane < half, extra, key_rows),
    ]
    head_v = [
        jnp.where(key_lane < half, value_rows, one),
        jnp.where(key_lane < half, one, value_rows),
    ]

    def scores(at, head):
        low, high = at * chunk, (at + 1) * chunk
        live = high if causal else keys
        found = dot(head_q[head][low:high], head_k[head][:live], 1, 1)
        if not causal:
            return found
        query_at = lax.broadcasted_iota(jnp.int32, (chunk, chunk), 0)
        key_at = lax.broadcasted_iota(jnp.int32, (chunk, chunk), 1)
        edge = jnp.where(key_at <= query_at, found[:, low:high], -1e30)
        return jnp.concatenate([found[:, :low], edge], 1) if low else edge

    def mix(head, found):
        top = jnp.max(found, 1, keepdims=True)
        expo = jnp.exp(found - top).astype(BF16)
        mixed = dot(expo, head_v[head][: found.shape[1]], 1, 0)
        return mixed / pltpu.roll(mixed, half, 1), top + jnp.log(mixed)

    units = [(at, head) for at in range(rows // chunk) for head in range(2)]
    done, waiting = {}, []
    for unit in units:
        waiting.append((unit, scores(*unit)))
        if len(waiting) > ahead:
            first, found = waiting.pop(0)
            done[first] = mix(first[1], found)
    for first, found in waiting:
        done[first] = mix(first[1], found)
    left = lane[:chunk] < half
    place = lane[:chunk] % half
    for at in range(rows // chunk):
        low, high = at * chunk, (at + 1) * chunk
        out_ref[low:high, :] = jnp.where(left, done[at, 0][0], done[at, 1][0]).astype(BF16)
        parts = split_three(-jnp.where(left, done[at, 1][1], done[at, 0][1]))
        packed = jnp.where(place == 0, 1.0, 0.0)
        for index, part in enumerate(parts):
            packed = jnp.where(place == index + 1, part, packed)
        lse_ref[low:high, :] = packed.astype(BF16)


def attend_backward_kernel(
    causal, chunk, q_ref, k_ref, v_ref, out_ref, grad_ref, lse_ref, extra_ref,
    dq_ref, dk_ref, dv_ref, p_scr, s_scr,
):
    rows, width = q_ref.shape
    keys, half = k_ref.shape[0], width // 2
    scale = half**-0.5
    count = rows // chunk
    lane = lax.broadcasted_iota(jnp.int32, (rows, width), 1)
    key_lane = lax.broadcasted_iota(jnp.int32, (keys, width), 1)
    queries = q_ref[...] * jnp.asarray(scale, BF16)
    lse, extra = lse_ref[...], extra_ref[...]
    key_rows, value_rows, grads = k_ref[...], v_ref[...], grad_ref[...]
    place = key_lane % half
    ones = jnp.where((place >= 1) & (place <= 3), 1.0, 0.0).astype(BF16)
    products = grads.astype(F32) * out_ref[...].astype(F32)
    queries_t, grads_t = queries.T, grads.T
    grad_q = [[None] * count, [None] * count]
    grad_k_t, grad_v_t = [], []
    for head in range(2):
        mine = (lane < half) if head == 0 else (lane >= half)
        key_mine = (key_lane < half) if head == 0 else (key_lane >= half)
        base = half if head == 0 else 0
        head_q = jnp.where(mine, queries, lse)
        head_k = jnp.where(key_mine, key_rows, extra)
        head_v = jnp.where(key_mine, value_rows, ones)
        head_g = grads.astype(F32)
        dots = split_three(-jnp.sum(jnp.where(mine, products, 0.0), 1, keepdims=True))
        head_g = jnp.where(mine, head_g, 0.0)
        for index, part in enumerate(dots):
            head_g = jnp.where(lane == base + index + 1, part, head_g)
        head_g = head_g.astype(BF16)
        span = slice(head * half, (head + 1) * half)
        for at in range(count):
            low, high = at * chunk, (at + 1) * chunk
            live = high if causal else keys
            probs = jnp.exp(dot(head_q[low:high], head_k[:live], 1, 1))
            if causal:
                query_at = lax.broadcasted_iota(jnp.int32, (chunk, chunk), 0)
                key_at = lax.broadcasted_iota(jnp.int32, (chunk, chunk), 1)
                edge = jnp.where(key_at <= query_at, probs[:, low:high], 0.0)
                probs = jnp.concatenate([probs[:, :low], edge], 1) if low else edge
            grad_s = (probs * dot(head_g[low:high], head_v[:live], 1, 1)).astype(BF16)
            p_scr[head, low:high, :live] = probs.astype(BF16)
            s_scr[head, low:high, :live] = grad_s
            grad_q[head][at] = dot(grad_s, key_rows[:live], 1, 0)
        if causal:
            for total, source, saved in (
                (grad_v_t, grads_t, p_scr),
                (grad_k_t, queries_t, s_scr),
            ):
                total.append(
                    jnp.concatenate(
                        [
                            dot(
                                source[span, at * chunk :],
                                saved[head, at * chunk :, at * chunk : (at + 1) * chunk],
                                1,
                                0,
                            )
                            for at in range(count)
                        ],
                        1,
                    )
                )
        else:
            grad_v_t.append(dot(grads_t[span], p_scr[head], 1, 0))
            grad_k_t.append(dot(queries_t[span], s_scr[head], 1, 0))
    for at in range(count):
        low, high = at * chunk, (at + 1) * chunk
        both = jnp.where(lane[low:high] < half, grad_q[0][at], grad_q[1][at])
        dq_ref[low:high, :] = (both * scale).astype(BF16)
    dk_ref[...] = jnp.concatenate(grad_k_t, 0).T.astype(BF16)
    dv_ref[...] = jnp.concatenate(grad_v_t, 0).T.astype(BF16)


def attend_forward(queries, q_at, key_rows, k_at, value_rows, v_at, extra, width, causal):
    rows, keys = queries.shape[0], key_rows.shape[0]

    def pair(count, first):
        return pl.BlockSpec((count, 128), lambda i: (0, i + first))

    return call(
        functools.partial(attend_forward_kernel, causal, 256, 2),
        "self_forward" if causal else "cross_forward",
        (width // 128,),
        [pair(rows, q_at), pair(keys, k_at), pair(keys, v_at), whole((keys, 128))],
        [pair(rows, 0), pair(rows, 0)],
        [jax.ShapeDtypeStruct((rows, width), BF16)] * 2,
        4 * rows * keys * width,
        12 * rows * width,
        rows * keys * HEADS,
    )(queries, key_rows, value_rows, extra)


def attend_backward(
    queries, q_at, key_rows, k_at, value_rows, v_at, mixed, grads, lse, extra, width, causal
):
    rows, keys = queries.shape[0], key_rows.shape[0]

    def pair(count, first):
        return pl.BlockSpec((count, 128), lambda i: (0, i + first))

    return call(
        functools.partial(attend_backward_kernel, causal, 256),
        "self_backward" if causal else "cross_backward",
        (width // 128,),
        [pair(rows, q_at), pair(keys, k_at), pair(keys, v_at)]
        + [pair(rows, 0)] * 3
        + [whole((keys, 128))],
        [pair(rows, 0), pair(keys, 0), pair(keys, 0)],
        [
            jax.ShapeDtypeStruct((rows, width), BF16),
            jax.ShapeDtypeStruct((keys, width), BF16),
            jax.ShapeDtypeStruct((keys, width), BF16),
        ],
        10 * rows * keys * width,
        18 * rows * width,
        rows * keys * HEADS,
        [pltpu.VMEM((2, rows, keys), BF16)] * 2,
    )(queries, key_rows, value_rows, mixed, grads, lse, extra)


def project_kernel(x_ref, w_ref, bias_ref, out_ref):
    out_ref[...] = (dot(x_ref[...], w_ref[...], 1, 0) + bias_ref[...]).astype(BF16)


def project(values, weight, first, columns, bias, name):
    rows, depth = values.shape
    step = 512
    return call(
        project_kernel,
        name,
        (columns // step,),
        [
            whole((rows, depth)),
            pl.BlockSpec((depth, step), lambda i: (0, i + first // step)),
            pl.BlockSpec((1, step), lambda i: (0, i)),
        ],
        pl.BlockSpec((rows, step), lambda i: (0, i)),
        jax.ShapeDtypeStruct((rows, columns), BF16),
        2 * rows * depth * columns,
        2 * (rows * depth + depth * columns + rows * columns),
    )(values, weight, bias)


def post_self_kernel(
    x_ref, ctx_ref, wo_ref, wq_ref, bo_ref, gain_ref, shift_ref, bq_ref, normal_ref, scale_ref, q_ref
):
    part = 256
    spans = [slice(at, at + part) for at in range(0, x_ref.shape[0], part)]
    sums = [
        x_ref[span].astype(F32) + dot(ctx_ref[span], wo_ref[...], 1, 0) + bo_ref[...]
        for span in spans
    ]
    for span, total in zip(spans, sums):
        normal, scale = normalize(total)
        normal_ref[span] = normal
        scale_ref[span] = jnp.broadcast_to(scale, (part, 128))
        hidden = (normal * gain_ref[...] + shift_ref[...]).astype(BF16)
        q_ref[span] = (dot(hidden, wq_ref[...], 1, 0) + bq_ref[...]).astype(BF16)


def post_self(values, context, weights, wo_at, wq_at, out_bias, gain, shift, q_bias):
    rows, width = values.shape
    step = 512
    vector = whole((1, width))
    return call(
        post_self_kernel,
        "post_self",
        (rows // step,),
        [
            rows_block(step, width),
            rows_block(step, width),
            pl.BlockSpec((width, width), lambda i: (0, wo_at)),
            pl.BlockSpec((width, width), lambda i: (0, wq_at)),
        ]
        + [vector] * 4,
        [rows_block(step, width), rows_block(step, 128), rows_block(step, width)],
        [
            jax.ShapeDtypeStruct((rows, width), F32),
            jax.ShapeDtypeStruct((rows, 128), F32),
            jax.ShapeDtypeStruct((rows, width), BF16),
        ],
        4 * rows * width * width,
        rows * width * 10 + 4 * width * width,
    )(values, context, weights, weights, out_bias, gain, shift, q_bias)


def post_cross_kernel(
    n1_ref, ctx_ref, wo_ref, bo_ref, gain_ref, shift_ref, gain2_ref, shift2_ref,
    normal_ref, scale_ref, hidden_ref,
):
    part = 256
    spans = [slice(at, at + part) for at in range(0, n1_ref.shape[0], part)]
    sums = [
        n1_ref[span] * gain_ref[...]
        + shift_ref[...]
        + dot(ctx_ref[span], wo_ref[...], 1, 0)
        + bo_ref[...]
        for span in spans
    ]
    for span, total in zip(spans, sums):
        normal, scale = normalize(total)
        normal_ref[span] = normal
        scale_ref[span] = jnp.broadcast_to(scale, (part, 128))
        hidden_ref[span] = (normal * gain2_ref[...] + shift2_ref[...]).astype(BF16)


def post_cross(normal, context, weights, wo_at, out_bias, gain, shift, gain2, shift2):
    rows, width = normal.shape
    step = 512
    vector = whole((1, width))
    return call(
        post_cross_kernel,
        "post_cross",
        (rows // step,),
        [
            rows_block(step, width),
            rows_block(step, width),
            pl.BlockSpec((width, width), lambda i: (0, wo_at)),
        ]
        + [vector] * 5,
        [rows_block(step, width), rows_block(step, 128), rows_block(step, width)],
        [
            jax.ShapeDtypeStruct((rows, width), F32),
            jax.ShapeDtypeStruct((rows, 128), F32),
            jax.ShapeDtypeStruct((rows, width), BF16),
        ],
        2 * rows * width * width,
        rows * width * 12 + 2 * width * width,
    )(normal, context, weights, out_bias, gain, shift, gain2, shift2)


def second_block(w_ref, held, width):
    pieces = []
    for at in range(0, w_ref.shape[0], held):
        for group in range(w_ref.shape[1] // width):
            pieces.append(w_ref[at : at + held, group * width : (group + 1) * width])
    return jnp.concatenate(pieces, 0)


def ffn_forward_kernel(held, h_ref, w1_ref, w2_ref, b1_ref, b2_ref, out_ref, slope_ref):
    rows, width = h_ref.shape
    part = 256
    second = second_block(w2_ref, held, width)

    @pl.when(pl.program_id(0) == 0)
    def _():
        out_ref[...] = jnp.broadcast_to(b2_ref[...], out_ref.shape)

    def first(at):
        return dot(h_ref[at : at + part], w1_ref[...], 1, 0) + b1_ref[...]

    def finish(at, pre):
        phi = 0.5 + 0.5 * lax.erf(pre * (0.5**0.5))
        act = (pre * phi).astype(BF16)
        slope = phi + pre * (jnp.exp(pre * pre * -0.5) * (1.0 / math.sqrt(2.0 * math.pi)))
        slope_ref[at : at + part] = slope.astype(BF16)
        out_ref[at : at + part] += dot(act, second, 1, 0)

    waiting = None
    for at in range(0, rows, part):
        pre = first(at)
        if waiting is not None:
            finish(*waiting)
        waiting = (at, pre)
    finish(*waiting)


def ffn_forward(hidden, weights, w2_at, w1_at, first_bias, second_bias, held):
    rows, width = hidden.shape
    wide = first_bias.shape[1]
    step = 512
    groups = wide // width
    return call(
        functools.partial(ffn_forward_kernel, held),
        "ffn_forward",
        (wide // step,),
        [
            whole((rows, width)),
            pl.BlockSpec((width, step), lambda i: (0, i + w1_at // step)),
            pl.BlockSpec((step // groups, wide), lambda i: (i, w2_at // wide)),
            pl.BlockSpec((1, step), lambda i: (0, i)),
            whole((1, width)),
        ],
        [whole((rows, width)), pl.BlockSpec((rows, step), lambda i: (0, i))],
        [jax.ShapeDtypeStruct((rows, width), F32), jax.ShapeDtypeStruct((rows, wide), BF16)],
        4 * rows * width * wide,
        6 * rows * width + 4 * width * wide + 2 * rows * wide,
        2 * rows * wide,
    )(hidden, weights, weights, first_bias, second_bias)


def ffn_backward_kernel(held, g_ref, w1_ref, w2_ref, slope_ref, start_ref, out_ref):
    rows, width = g_ref.shape
    part = 256
    second = second_block(w2_ref, held, width)

    @pl.when(pl.program_id(0) == 0)
    def _():
        out_ref[...] = start_ref[...]

    def finish(at, grad_act):
        grad_pre = (slope_ref[at : at + part].astype(F32) * grad_act).astype(BF16)
        out_ref[at : at + part] += dot(grad_pre, w1_ref[...], 1, 1)

    waiting = None
    for at in range(0, rows, part):
        grad_act = dot(g_ref[at : at + part], second, 1, 1)
        if waiting is not None:
            finish(*waiting)
        waiting = (at, grad_act)
    finish(*waiting)


def ffn_backward(grads, weights, w2_at, w1_at, slope, start, held):
    rows, width = grads.shape
    wide = slope.shape[1]
    step = 512
    groups = wide // width
    return call(
        functools.partial(ffn_backward_kernel, held),
        "ffn_backward",
        (wide // step,),
        [
            whole((rows, width)),
            pl.BlockSpec((width, step), lambda i: (0, i + w1_at // step)),
            pl.BlockSpec((step // groups, wide), lambda i: (i, w2_at // wide)),
            pl.BlockSpec((rows, step), lambda i: (0, i)),
            whole((rows, width)),
        ],
        whole((rows, width)),
        jax.ShapeDtypeStruct((rows, width), F32),
        4 * rows * width * wide,
        10 * rows * width + 4 * width * wide + 2 * rows * wide,
    )(grads, weights, weights, slope, start)


def adapter_kernel(
    factor, ramp_ref, n2_ref, ffn_ref, go_ref, down_ref, up_ref, gain2_ref, shift2_ref, gain3_ref, shift3_ref,
    gain_a_ref, shift_a_ref, down_b_ref, up_b_ref,
    out_ref, gffn_ref, rest_ref, grads_ref,
):
    ramp = ramp_ref[0]
    width, units = down_ref.shape

    @pl.when(pl.program_id(0) == 0)
    def _():
        grads_ref[...] = jnp.zeros_like(grads_ref)

    hidden = n2_ref[...] * gain2_ref[...] + shift2_ref[...]
    normal_a, scale_a = normalize(hidden)
    adapt_in = (normal_a * gain_a_ref[...] + shift_a_ref[...]).astype(BF16)
    lower = dot(adapt_in, down_ref[...], 1, 0) + down_b_ref[...]
    gate = 1.0 / (1.0 + jnp.exp(-lower))
    adapt_act = (lower * gate).astype(BF16)
    branch = dot(adapt_act, up_ref[...], 1, 0) + up_b_ref[...]
    normal, scale = normalize(hidden + ffn_ref[...] + ramp * branch)
    out_ref[...] = (normal * gain3_ref[...] + shift3_ref[...]).astype(BF16)
    grad_sum = normalize_back(normal, scale, gain3_ref[...] * go_ref[...].astype(F32))
    gffn_ref[...] = grad_sum.astype(BF16)
    grad_branch = (ramp * grad_sum).astype(BF16)
    grads_ref[0:units] += dot(adapt_act, grad_branch, 0, 0)
    grad_act = dot(grad_branch, up_ref[...], 1, 1).astype(BF16).astype(F32)
    grad_lower = (gate * (1.0 + lower * (1.0 - gate)) * grad_act).astype(BF16)
    for at in range(0, width, units):
        grads_ref[units : 2 * units, at : at + units] += dot(
            adapt_in[:, at : at + units], grad_lower, 0, 0
        )
    grad_adapt = dot(grad_lower, down_ref[...], 1, 1)
    rest_ref[...] = grad_sum + normalize_back(normal_a, scale_a, gain_a_ref[...] * grad_adapt)
    for at, row in enumerate(
        (grad_branch.astype(F32), grad_adapt * normal_a, grad_adapt, grad_lower.astype(F32))
    ):
        grads_ref[2 * units + at : 2 * units + at + 1, 0 : row.shape[1]] += jnp.sum(
            row, 0, keepdims=True
        )

    @pl.when(pl.program_id(0) == pl.num_programs(0) - 1)
    def _():
        grads_ref[...] *= factor


def adapter(ramp, normal2, ffn, grad_out, down, up, vectors, down_bias, extra, factor):
    rows, width = normal2.shape
    units = down.shape[1]
    step = 256
    vector = whole((1, width))
    gain2, shift2, gain3, shift3, gain_a, shift_a, up_bias = vectors
    return call(
        functools.partial(adapter_kernel, factor),
        "adapter",
        (rows // step,),
        [pl.BlockSpec(memory_space=pltpu.SMEM)]
        + [rows_block(step, width)] * 3
        + [whole(down.shape), whole(up.shape)]
        + [vector] * 6
        + [whole((1, units)), vector],
        [rows_block(step, width)] * 3 + [whole((2 * units + extra, width))],
        [
            jax.ShapeDtypeStruct((rows, width), BF16),
            jax.ShapeDtypeStruct((rows, width), BF16),
            jax.ShapeDtypeStruct((rows, width), F32),
            jax.ShapeDtypeStruct((2 * units + extra, width), F32),
        ],
        12 * rows * width * units,
        18 * rows * width + 12 * width * units,
        rows * units,
    )(
        ramp, normal2, ffn, grad_out, down, up, gain2, shift2, gain3, shift3, gain_a, shift_a,
        down_bias, up_bias,
    )


def norm_back_kernel(g_ref, normal_ref, scale_ref, gain_ref, wo_ref, sum_ref, ctx_ref):
    part = 256
    for at in range(0, g_ref.shape[0], part):
        span = slice(at, at + part)
        grad = normalize_back(normal_ref[span], scale_ref[span, 0:1], gain_ref[...] * g_ref[span])
        sum_ref[span] = grad
        ctx_ref[span] = dot(grad.astype(BF16), wo_ref[...], 1, 1).astype(BF16)


def norm_back_query_kernel(
    g_ref, dq_ref, wq_ref, normal_ref, scale_ref, gain_ref, wo_ref, sum_ref, ctx_ref
):
    part = 256
    spans = [slice(at, at + part) for at in range(0, g_ref.shape[0], part)]
    totals = [g_ref[span] + dot(dq_ref[span], wq_ref[...], 1, 1) for span in spans]
    for span, total in zip(spans, totals):
        grad = normalize_back(normal_ref[span], scale_ref[span, 0:1], gain_ref[...] * total)
        sum_ref[span] = grad
        ctx_ref[span] = dot(grad.astype(BF16), wo_ref[...], 1, 1).astype(BF16)


def norm_back(grads, normal, scale, gain, weights, wo_at, query_grads=None, wq_at=None):
    rows, width = grads.shape
    step = 512
    block = rows_block(step, width)
    with_query = query_grads is not None
    extra_specs = [block, pl.BlockSpec((width, width), lambda i: (0, wq_at))] if with_query else []
    extra = [query_grads, weights] if with_query else []
    return call(
        norm_back_query_kernel if with_query else norm_back_kernel,
        "norm_one_back" if with_query else "norm_two_back",
        (rows // step,),
        [block]
        + extra_specs
        + [
            block,
            rows_block(step, 128),
            whole((1, width)),
            pl.BlockSpec((width, width), lambda i: (0, wo_at)),
        ],
        [block, block],
        [jax.ShapeDtypeStruct((rows, width), F32), jax.ShapeDtypeStruct((rows, width), BF16)],
        (4 if with_query else 2) * rows * width * width,
        16 * rows * width + 4 * width * width,
    )(grads, *extra, normal, scale, gain, weights)


def back_project_kernel(count, with_start, *refs):
    grads, rest = refs[:count], refs[count:]
    weights, rest = rest[:count], rest[count:]
    total = sum(dot(g[...], w[...], 1, 1) for g, w in zip(grads, weights))
    if with_start:
        total = total + rest[0][...]
    rest[-1][...] = total


def back_project(grads, weights, first, start, name):
    rows, width = grads[0].shape
    step = 256
    count = len(grads)
    column = pl.BlockSpec((rows, step), lambda i: (0, i))

    def row_of(at):
        return pl.BlockSpec((step, width), lambda i: (i, at))

    return call(
        functools.partial(back_project_kernel, count, start is not None),
        name,
        (width // step,),
        [whole((rows, width))] * count
        + [row_of(first + at) for at in range(count)]
        + ([column] if start is not None else []),
        column,
        jax.ShapeDtypeStruct((rows, width), F32),
        2 * rows * width * width * count,
        rows * width * (2 * count + 8) + 2 * count * width * width,
    )(*grads, *([weights] * count), *([start] if start is not None else []))


def gather(shard):
    return lax.all_gather(shard, "fsdp", axis=0, tiled=True)


def total_sum(part):
    count = lax.axis_size("dp")
    mine = lax.psum_scatter(part, "fsdp", scatter_dimension=0, tiled=True)
    total, travel = mine, mine
    for _ in range(count - 1):
        travel = lax.ppermute(travel, "dp", [(at, (at + 1) % count) for at in range(count)])
        total = total + travel
    return gather(total)


def local(
    inputs,
    encoder,
    grad_out,
    target_mask,
    source_lengths,
    step,
    attn_in,
    attn_out,
    ffn_in,
    ffn_in_bias,
    ffn_out,
    ffn_out_bias,
    attn_bias,
    norm_gain,
    norm_shift,
    adapter_down,
    adapter_down_bias,
    adapter_up,
    adapter_up_bias,
    adapter_gain,
    adapter_shift,
):
    sequences, row_count, width = inputs.shape
    source_count = encoder.shape[1]
    held = attn_in.shape[0]
    groups = ffn_out.shape[0] // held
    wide = ffn_in.shape[1]
    pad = jnp.zeros((held, 128), BF16)
    attn_w = gather(jnp.concatenate([attn_in, attn_out, pad], 1))
    ffn_w = jnp.concatenate(
        [ffn_out[at * held : (at + 1) * held] for at in range(groups)] + [ffn_in, pad], 1
    )
    ffn_w = gather(ffn_w)
    w1_at, w2_at = wide, 0
    cq_at, ck_at, so_at, co_at = 3, 4, 6, 7

    ramp = (4.0 * step.astype(F32) / RAMP).reshape(1)
    bias = [attn_bias[at : at + 1] for at in range(6)]
    gain = [norm_gain[at : at + 1] for at in range(3)]
    shift = [norm_shift[at : at + 1] for at in range(3)]
    none = jnp.zeros((1, width), F32)
    tokens, states = inputs.reshape(-1, width), encoder.reshape(-1, width)
    self_extra = key_extra(target_mask.reshape(-1) > 0)
    cross_extra = key_extra(jnp.arange(source_count, dtype=jnp.int32) < source_lengths[0])
    per = width // 128

    qkv = project(
        tokens, attn_w, 0, 3 * width, jnp.concatenate([bias[0], none, bias[1]], 1), "self_project"
    )
    self_ctx, self_lse = attend_forward(
        qkv, 0, qkv, per, qkv, 2 * per, self_extra, width, True
    )
    normal1, scale1, cross_q = post_self(
        tokens, self_ctx, attn_w, so_at, cq_at, bias[2], gain[0], shift[0], bias[3]
    )
    cross_kv = project(
        states, attn_w, ck_at * width, 2 * width, jnp.concatenate([none, bias[4]], 1), "cross_project"
    )
    cross_ctx, cross_lse = attend_forward(
        cross_q, 0, cross_kv, 0, cross_kv, per, cross_extra, width, False
    )
    normal2, scale2, hidden2 = post_cross(
        normal1, cross_ctx, attn_w, co_at, bias[5], gain[0], shift[0], gain[1], shift[1]
    )
    ffn, slope = ffn_forward(
        hidden2, ffn_w, w2_at, w1_at, ffn_in_bias[None], ffn_out_bias[None], held
    )
    token_total = sequences * row_count * lax.axis_size("fsdp") * lax.axis_size("dp")
    layer_out, grad_ffn, grad_rest, adapter_grads = adapter(
        ramp,
        normal2,
        ffn,
        grad_out.reshape(-1, width),
        adapter_down,
        adapter_up,
        (
            gain[1], shift[1], gain[2], shift[2], adapter_gain[None], adapter_shift[None],
            adapter_up_bias[None],
        ),
        adapter_down_bias[None],
        8 * lax.axis_size("fsdp"),
        1.0 / math.sqrt(token_total),
    )
    adapter_grads = total_sum(adapter_grads)
    grad_hidden2 = ffn_backward(grad_ffn, ffn_w, w2_at, w1_at, slope, grad_rest, held)
    grad_sum2, grad_cross = norm_back(grad_hidden2, normal2, scale2, gain[1], attn_w, co_at)
    cross_dq, cross_dk, cross_dv = attend_backward(
        cross_q, 0, cross_kv, 0, cross_kv, per, cross_ctx, grad_cross, cross_lse, cross_extra,
        width, False,
    )
    grad_encoder = back_project((cross_dk, cross_dv), attn_w, ck_at, None, "encoder_back")
    grad_sum1, grad_self = norm_back(
        grad_sum2, normal1, scale1, gain[0], attn_w, so_at, cross_dq, cq_at
    )
    self_grads = attend_backward(
        qkv, 0, qkv, per, qkv, 2 * per, self_ctx, grad_self, self_lse, self_extra, width, True
    )
    grad_input = back_project(self_grads, attn_w, 0, grad_sum1, "input_back")

    units = adapter_down.shape[1]
    grad_down = [adapter_grads[units : 2 * units, at : at + units] for at in range(0, width, units)]
    small = adapter_grads[2 * units :]
    return (
        layer_out.reshape(inputs.shape),
        grad_input.reshape(inputs.shape),
        grad_encoder.reshape(encoder.shape),
        jnp.concatenate(grad_down, 0),
        small[3, :units],
        adapter_grads[:units],
        small[0],
        small[1],
        small[2],
    )


def solution(mesh):
    batch = P(("fsdp", "dp"), None, None)
    split = P("fsdp", None)
    placed = (
        (batch,) * 3
        + (P(("fsdp", "dp"), None), P(("fsdp", "dp")), P())
        + (split, split, split, P(), split)
        + (P(),) * 10
    )
    return jax.shard_map(
        local,
        mesh=mesh,
        in_specs=placed,
        out_specs=(batch,) * 3 + (P(),) * 6,
        check_vma=False,
    )
```

```python
import functools
import math

import jax
import jax.numpy as jnp
from jax import lax
from jax.experimental import pallas as pl
from jax.experimental.pallas import tpu as pltpu
from jax.sharding import PartitionSpec as P

HEADS = 16
RAMP = 1000
EPS = 1e-05
F32 = jnp.float32
BF16 = jnp.bfloat16
VMEM_LIMIT = 58 * 2**20


def dot(left, right, left_dim, right_dim):
    return lax.dot_general(
        left, right, (((left_dim,), (right_dim,)), ((), ())), preferred_element_type=F32
    )


def call(kernel, name, grid, in_specs, out_specs, out_shape, flops, moved, exps=0, scratch=()):
    return pl.pallas_call(
        kernel,
        name=name,
        grid=grid,
        in_specs=in_specs,
        out_specs=out_specs,
        out_shape=out_shape,
        scratch_shapes=scratch,
        compiler_params=pltpu.CompilerParams(vmem_limit_bytes=VMEM_LIMIT),
        cost_estimate=pl.CostEstimate(
            flops=int(flops), bytes_accessed=int(moved), transcendentals=int(exps)
        ),
    )


def whole(shape):
    return pl.BlockSpec(shape, lambda *_: (0,) * len(shape), pipeline_mode=pl.Buffered(1))


def columns(rows, width, first=0):
    return pl.BlockSpec((rows, width), lambda i: (0, i + first))


def square(width, at):
    return pl.BlockSpec((width, width), lambda i: (0, at), pipeline_mode=pl.Buffered(1))


def normalize(values):
    center = values - jnp.mean(values, -1, keepdims=True)
    scale = lax.rsqrt(jnp.mean(center * center, -1, keepdims=True) + EPS)
    return center * scale, scale


def normalize_back(normal, scale, grad):
    return scale * (
        grad
        - jnp.mean(grad, -1, keepdims=True)
        - normal * jnp.mean(grad * normal, -1, keepdims=True)
    )


def split_three(values):
    high = values.astype(BF16).astype(F32)
    middle = (values - high).astype(BF16).astype(F32)
    return high, middle, values - high - middle


GROUP = 4
CHUNK = 256
SIZE = 64


def attend_forward(causal, ahead, q_ref, k_ref, v_ref, length, ctx_ref, expo_ref, inverse_ref):
    rows, keys = q_ref.shape[0], k_ref.shape[0]
    width = 2 * SIZE
    lane = lax.broadcasted_iota(jnp.int32, (rows, width), 1)
    key_lane = lax.broadcasted_iota(jnp.int32, (keys, width), 1)
    key_row = lax.broadcasted_iota(jnp.int32, (keys, width), 0)
    picks = jnp.where(lane % SIZE == 0, 1.0, 0.0).astype(BF16)
    extra = jnp.where(key_row < length, 0.0, -1e30).astype(BF16)
    one = jnp.asarray(1.0, BF16)
    left = lane[:CHUNK] < SIZE
    head_q, head_k, head_v = [], [], []
    for at in range(0, q_ref.shape[1], width):
        queries = q_ref[:, at : at + width]
        key_rows, value_rows = k_ref[:, at : at + width], v_ref[:, at : at + width]
        head_q += [jnp.where(lane < SIZE, queries, picks), jnp.where(lane < SIZE, picks, queries)]
        head_k += [
            jnp.where(key_lane < SIZE, key_rows, extra),
            jnp.where(key_lane < SIZE, extra, key_rows),
        ]
        head_v += [
            jnp.where(key_lane < SIZE, value_rows, one),
            jnp.where(key_lane < SIZE, one, value_rows),
        ]

    def scores(at, head):
        low, high = at * CHUNK, (at + 1) * CHUNK
        live = high if causal else keys
        found = dot(head_q[head][low:high], head_k[head][:live], 1, 1)
        if not causal:
            return found
        query_at = lax.broadcasted_iota(jnp.int32, (CHUNK, CHUNK), 0)
        key_at = lax.broadcasted_iota(jnp.int32, (CHUNK, CHUNK), 1)
        edge = jnp.where(key_at <= query_at, found[:, low:high], -1e30)
        return jnp.concatenate([found[:, :low], edge], 1) if low else edge

    done, waiting = {}, []

    def finish(at, head, found):
        low, high = at * CHUNK, (at + 1) * CHUNK
        live = found.shape[1]
        top = jnp.max(found, 1, keepdims=True)
        expo = jnp.exp(found - top).astype(BF16)
        expo_ref[head, low:high, :live] = expo
        done[head] = dot(expo, head_v[head][:live], 1, 0)
        if head % 2:
            first, second = done[head - 1], done[head]
            inverse = 1.0 / jnp.where(left, pltpu.roll(first, SIZE, 1), pltpu.roll(second, SIZE, 1))
            span = slice(head // 2 * width, (head // 2 + 1) * width)
            inverse_ref[low:high, span] = inverse
            ctx_ref[low:high, span] = (jnp.where(left, first, second) * inverse).astype(BF16)

    for pair in range(len(head_q) // 2):
        for at in range(rows // CHUNK):
            for head in (2 * pair, 2 * pair + 1):
                waiting.append((at, head, scores(at, head)))
                if len(waiting) > ahead:
                    finish(*waiting.pop(0))
    for unit in waiting:
        finish(*unit)


def attend_backward(
    causal, q_ref, k_ref, v_ref, ctx_ref, grad_ref, expo_ref, inverse_ref, dq_ref, dk_ref, dv_ref, s_scr,
    before, after,
):
    rows, keys = q_ref.shape[0], k_ref.shape[0]
    width = 2 * SIZE
    count = rows // CHUNK
    lane = lax.broadcasted_iota(jnp.int32, (rows, width), 1)
    key_lane = lax.broadcasted_iota(jnp.int32, (keys, width), 1)
    place = key_lane % SIZE
    ones = jnp.where((place >= 1) & (place <= 3), 1.0, 0.0).astype(BF16)
    for pair in range(q_ref.shape[1] // width):
        span = slice(pair * width, (pair + 1) * width)
        key_rows, value_rows = k_ref[:, span], v_ref[:, span]
        grads = (grad_ref[:, span].astype(F32) * inverse_ref[:, span]).astype(BF16)
        wide = grads.astype(F32)
        products = wide * ctx_ref[:, span].astype(F32)
        queries_t, grads_t = q_ref[:, span].T, grads.T
        head_g, head_v = [], []
        for head in range(2):
            mine = (lane < SIZE) if head == 0 else (lane >= SIZE)
            key_mine = (key_lane < SIZE) if head == 0 else (key_lane >= SIZE)
            base = SIZE if head == 0 else 0
            head_v.append(jnp.where(key_mine, value_rows, ones))
            dots = split_three(-jnp.sum(jnp.where(mine, products, 0.0), 1, keepdims=True))
            grad = jnp.where(mine, wide, 0.0)
            for index, part in enumerate(dots):
                grad = jnp.where(lane == base + index + 1, part, grad)
            head_g.append(grad.astype(BF16))

        grad_q, waiting = {}, []
        before(pair)

        def finish(at, head, grad_p, pair=pair, span=span, key_rows=key_rows, grad_q=grad_q):
            low, high = at * CHUNK, (at + 1) * CHUNK
            live = grad_p.shape[1]
            expo = expo_ref[2 * pair + head, low:high, :live]
            grad_s = (expo.astype(F32) * grad_p).astype(BF16)
            s_scr[head, low:high, :live] = grad_s
            grad_q[head] = dot(grad_s, key_rows[:live], 1, 0)
            if head:
                both = jnp.where(lane[low:high] < SIZE, grad_q[0], grad_q[1])
                dq_ref[low:high, span] = (both * SIZE**-0.5).astype(BF16)

        for at in range(count):
            for head in range(2):
                low, high = at * CHUNK, (at + 1) * CHUNK
                live = high if causal else keys
                waiting.append((at, head, dot(head_g[head][low:high], head_v[head][:live], 1, 1)))
                if len(waiting) > 1:
                    finish(*waiting.pop(0))
        for unit in waiting:
            finish(*unit)
        step = CHUNK if causal else keys
        for source, saved, first, to in (
            (grads_t, expo_ref, 2 * pair, dv_ref),
            (queries_t, s_scr, 0, dk_ref),
        ):
            for low in range(0, keys, step):
                start = low if causal else 0
                parts = [
                    dot(
                        source[head * SIZE : (head + 1) * SIZE, start:],
                        saved[first + head, start:, low : low + step],
                        1,
                        0,
                    )
                    for head in range(2)
                ]
                to[low : low + step, span] = jnp.concatenate(parts, 0).T.astype(BF16)
        after(pair)


def parts_of(rows):
    return [slice(at, at + CHUNK) for at in range(0, rows, CHUNK)]


def wide_scale(scale):
    return jnp.broadcast_to(scale, (scale.shape[0], 128))


def self_forward_kernel(
    length_ref, x_ref, wq_ref, wk_ref, wv_ref, bq_ref, bv_ref,
    q_ref, k_ref, v_ref, ctx_ref, expo_ref, inverse_ref,
):
    scale = jnp.asarray(SIZE**-0.5, BF16)
    for span in parts_of(x_ref.shape[0]):
        rows = x_ref[span]
        q_ref[span] = (dot(rows, wq_ref[...], 1, 0) + bq_ref[...]).astype(BF16) * scale
        k_ref[span] = dot(rows, wk_ref[...], 1, 0).astype(BF16)
        v_ref[span] = (dot(rows, wv_ref[...], 1, 0) + bv_ref[...]).astype(BF16)
    attend_forward(
        True, 2, q_ref, k_ref, v_ref, length_ref[0], ctx_ref, expo_ref, inverse_ref
    )


def anywhere():
    return pl.BlockSpec(memory_space=pl.ANY)


def scalar():
    return pl.BlockSpec(memory_space=pltpu.SMEM)


def attend_out(rows, keys, width):
    group = GROUP * SIZE
    heads = width // SIZE
    specs = (
        [columns(rows, group)]
        + [columns(keys, group)] * 2
        + [columns(rows, group)]
        + [pl.BlockSpec((GROUP, rows, keys), lambda i: (i, 0, 0)), columns(rows, group)]
    )
    shapes = (
        [jax.ShapeDtypeStruct((rows, width), BF16)]
        + [jax.ShapeDtypeStruct((keys, width), BF16)] * 2
        + [jax.ShapeDtypeStruct((rows, width), BF16)]
        + [
            jax.ShapeDtypeStruct((heads, rows, keys), BF16),
            jax.ShapeDtypeStruct((rows, width), F32),
        ]
    )
    return specs, shapes


def self_forward(length, values, weights, q_bias, v_bias):
    rows, width = values.shape
    group = GROUP * SIZE
    per = width // group
    specs, shapes = attend_out(rows, rows, width)
    return call(
        self_forward_kernel,
        "self_forward",
        (per,),
        [scalar(), whole((rows, width))]
        + [columns(width, group, at * per) for at in range(3)]
        + [columns(1, group)] * 2,
        specs,
        shapes,
        6 * rows * width * width + 4 * rows * rows * width,
        18 * rows * width + 6 * width * width + 32 * rows * rows,
        rows * rows * HEADS,
    )(length, values, weights, weights, weights, q_bias, v_bias)


def cross_forward_kernel(
    length_ref, x_ref, sctx_ref, states_ref, wo_ref, wq_ref, wk_ref, wv_ref,
    bo_ref, gain_ref, shift_ref, bq_ref, bv_ref,
    normal_ref, scale_ref, q_ref, k_ref, v_ref, ctx_ref, expo_ref, inverse_ref, hidden_scr,
):
    spans = parts_of(x_ref.shape[0])

    @pl.when(pl.program_id(0) == 0)
    def _():
        sums = [
            x_ref[span].astype(F32) + dot(sctx_ref[span], wo_ref[...], 1, 0) + bo_ref[...]
            for span in spans
        ]
        for span, total in zip(spans, sums):
            normal, scale = normalize(total)
            normal_ref[span] = normal
            scale_ref[span] = wide_scale(scale)
            hidden_scr[span] = (normal * gain_ref[...] + shift_ref[...]).astype(BF16)

    size = jnp.asarray(SIZE**-0.5, BF16)
    for span in parts_of(states_ref.shape[0]):
        rows = states_ref[span]
        k_ref[span] = dot(rows, wk_ref[...], 1, 0).astype(BF16)
        v_ref[span] = (dot(rows, wv_ref[...], 1, 0) + bv_ref[...]).astype(BF16)
    for span in spans:
        q_ref[span] = (dot(hidden_scr[span], wq_ref[...], 1, 0) + bq_ref[...]).astype(BF16) * size
    attend_forward(
        False, 2, q_ref, k_ref, v_ref, length_ref[0], ctx_ref, expo_ref, inverse_ref
    )


def cross_forward(length, values, context, states, weights, at, vectors):
    rows, width = values.shape
    keys = states.shape[0]
    group = GROUP * SIZE
    per = width // group
    specs, shapes = attend_out(rows, keys, width)
    return call(
        cross_forward_kernel,
        "cross_forward",
        (per,),
        [scalar(), whole((rows, width)), whole((rows, width)), whole((keys, width))]
        + [square(width, at[0])]
        + [columns(width, group, first * per) for first in at[1:]]
        + [whole((1, width))] * 3
        + [columns(1, group)] * 2,
        [whole((rows, width)), whole((rows, 128))] + specs,
        [jax.ShapeDtypeStruct((rows, width), F32), jax.ShapeDtypeStruct((rows, 128), F32)] + shapes,
        8 * rows * width * width + 4 * rows * keys * width,
        26 * rows * width + 8 * width * width + 32 * rows * keys,
        rows * keys * HEADS,
        [pltpu.VMEM((rows, width), BF16)],
    )(length, values, context, states, weights, weights, weights, weights, *vectors)


def second_block(w_ref, held, width):
    pieces = []
    for at in range(0, w_ref.shape[0], held):
        for group in range(w_ref.shape[1] // width):
            pieces.append(w_ref[at : at + held, group * width : (group + 1) * width])
    return jnp.concatenate(pieces, 0)


def middle_kernel(
    held, factor, ramp_ref, n1_ref, ctx_ref, wo_ref, w1_ref, w2_ref, b1_ref, go_ref, down_ref, up_ref,
    bo_ref, gain1_ref, shift1_ref, gain2_ref, shift2_ref, gain3_ref, shift3_ref, b2_ref,
    gain_a_ref, shift_a_ref, up_b_ref, down_b_ref,
    normal_out, scale_ref, slope_ref, out_out, gffn_out, rest_out, grads_out,
    hidden_scr, act_scr, branch_scr, lower_scr,
    normal_ref, out_ref, gffn_ref, rest_ref, grads_ref, go_scr, down_scr, up_scr, in_sems, out_sems,
):
    rows, width = ctx_ref.shape
    units = down_ref.shape[1]
    spans = parts_of(rows)
    step = pl.program_id(0)
    first_load, *loads = moved(
        [(n1_ref, normal_ref), (go_ref, go_scr), (down_ref, down_scr), (up_ref, up_scr)], in_sems
    )
    keep = pltpu.make_async_copy(normal_ref, normal_out, out_sems.at[0])

    @pl.when(step == 0)
    def _():
        first_load.start()
        start_all(loads)
        sums = [dot(ctx_ref[span], wo_ref[...], 1, 0) + bo_ref[...] for span in spans]
        first_load.wait()
        for span, total in zip(spans, sums):
            normal, scale = normalize(
                total + (normal_ref[span] * gain1_ref[...] + shift1_ref[...])
            )
            normal_ref[span] = normal
            scale_ref[span] = wide_scale(scale)
            hidden = normal * gain2_ref[...] + shift2_ref[...]
            hidden_scr[span] = hidden.astype(BF16)
            rest_ref[span] = hidden + b2_ref[...]
        keep.start()

    second = second_block(w2_ref, held, width)

    def first(span):
        return dot(hidden_scr[span], w1_ref[...], 1, 0) + b1_ref[...]

    def finish(span, pre):
        phi = 0.5 + 0.5 * lax.erf(pre * (0.5**0.5))
        act = (pre * phi).astype(BF16)
        slope = phi + pre * (jnp.exp(pre * pre * -0.5) * (1.0 / math.sqrt(2.0 * math.pi)))
        slope_ref[span] = slope.astype(BF16)
        rest_ref[span] += dot(act, second, 1, 0)

    waiting = None
    for span in spans:
        pre = first(span)
        if waiting is not None:
            finish(*waiting)
        waiting = (span, pre)
    finish(*waiting)

    @pl.when(step == pl.num_programs(0) - 1)
    def _():
        ramp = ramp_ref[0]
        wait_all(loads)
        outs = moved(
            [(normal_ref, normal_out), (out_ref, out_out), (gffn_ref, gffn_out), (grads_ref, grads_out)],
            out_sems,
        )
        sums = [jnp.zeros((1, width), F32)] * 3 + [jnp.zeros((1, units), F32)]
        kept = []
        for span in spans:
            hidden = normal_ref[span] * gain2_ref[...] + shift2_ref[...]
            mean_a = jnp.mean(hidden, -1, keepdims=True)
            normal_a, scale_a = normalize(hidden)
            hidden_scr[span] = (normal_a * gain_a_ref[...] + shift_a_ref[...]).astype(BF16)
            kept.append([scale_a, mean_a])
        for span, keep in zip(spans, kept):
            lower = dot(hidden_scr[span], down_scr[...], 1, 0) + down_b_ref[...]
            gate = 1.0 / (1.0 + jnp.exp(-lower))
            act_scr[span] = (lower * gate).astype(BF16)
            keep.append(gate * (1.0 + lower * (1.0 - gate)))
        for span, keep in zip(spans, kept):
            branch = dot(act_scr[span], up_scr[...], 1, 0) + up_b_ref[...]
            normal, scale = normalize(rest_ref[span] + ramp * branch)
            out_ref[span] = (normal * gain3_ref[...] + shift3_ref[...]).astype(BF16)
            grad = normalize_back(normal, scale, gain3_ref[...] * go_scr[span].astype(F32))
            gffn_ref[span] = grad.astype(BF16)
            rest_ref[span] = grad
            grad_branch = (ramp * grad).astype(BF16)
            branch_scr[span] = grad_branch
            sums[0] = sums[0] + jnp.sum(grad_branch.astype(F32), 0, keepdims=True)
        start_all(outs[1:3])
        for span, keep in zip(spans, kept):
            grad_act = dot(branch_scr[span], up_scr[...], 1, 1).astype(BF16).astype(F32)
            grad_lower = (keep[2] * grad_act).astype(BF16)
            lower_scr[span] = grad_lower
            sums[3] = sums[3] + jnp.sum(grad_lower.astype(F32), 0, keepdims=True)
        for at, (span, keep) in enumerate(zip(spans, kept)):
            grad_adapt = dot(lower_scr[span], down_scr[...], 1, 1)
            hidden = normal_ref[span] * gain2_ref[...] + shift2_ref[...]
            normal_a = (hidden - keep[1]) * keep[0]
            rest_ref[span] += normalize_back(normal_a, keep[0], gain_a_ref[...] * grad_adapt)
            outs.append(
                pltpu.make_async_copy(rest_ref.at[span], rest_out.at[span], out_sems.at[4 + at])
            )
            outs[-1].start()
            sums[1] = sums[1] + jnp.sum(grad_adapt * normal_a, 0, keepdims=True)
            sums[2] = sums[2] + jnp.sum(grad_adapt, 0, keepdims=True)
        kind = grads_ref.dtype
        grads_ref[0:units] = (dot(act_scr[...], branch_scr[...], 0, 0) * factor).astype(kind)
        for at in range(0, width, units):
            grads_ref[units : 2 * units, at : at + units] = (
                dot(hidden_scr[:, at : at + units], lower_scr[...], 0, 0) * factor
            ).astype(kind)
        sums[3] = jnp.concatenate([sums[3], jnp.zeros((1, width - units), F32)], 1)
        small = jnp.concatenate([*sums, jnp.zeros((grads_ref.shape[0] - 2 * units - 4, width), F32)], 0)
        grads_ref[2 * units :] = (small * factor).astype(kind)
        outs[3].start()
        wait_all(outs)


def middle(
    ramp, normal1, context, attn_w, wo_at, ffn_w, w2_at, w1_at, first_bias, grad_out, down, up, vectors,
    down_bias, held, extra, factor,
):
    rows, width = normal1.shape
    wide = first_bias.shape[1]
    units = down.shape[1]
    step = 512
    groups = wide // width
    block = whole((rows, width))
    return call(
        functools.partial(middle_kernel, held, factor),
        "middle",
        (wide // step,),
        [
            scalar(),
            anywhere(),
            block,
            square(width, wo_at),
            columns(width, step, w1_at // step),
            pl.BlockSpec((step // groups, wide), lambda i: (i, w2_at // wide)),
            columns(1, step),
            anywhere(),
            anywhere(),
            anywhere(),
        ]
        + [whole((1, width))] * 11
        + [whole((1, units))],
        [anywhere(), whole((rows, 128)), columns(rows, step)] + [anywhere()] * 4,
        [
            jax.ShapeDtypeStruct((rows, width), F32),
            jax.ShapeDtypeStruct((rows, 128), F32),
            jax.ShapeDtypeStruct((rows, wide), BF16),
            jax.ShapeDtypeStruct((rows, width), BF16),
            jax.ShapeDtypeStruct((rows, width), BF16),
            jax.ShapeDtypeStruct((rows, width), F32),
            jax.ShapeDtypeStruct((2 * units + extra, width), BF16),
        ],
        4 * rows * width * wide + 2 * rows * width * width + 12 * rows * width * units,
        22 * rows * width + 4 * width * wide + 2 * rows * wide + 12 * width * units,
        2 * rows * wide + rows * units,
        [
            pltpu.VMEM((rows, width), BF16),
            pltpu.VMEM((rows, units), BF16),
            pltpu.VMEM((rows, width), BF16),
            pltpu.VMEM((rows, units), BF16),
            pltpu.VMEM((rows, width), F32),
            pltpu.VMEM((rows, width), BF16),
            pltpu.VMEM((rows, width), BF16),
            pltpu.VMEM((rows, width), F32),
            pltpu.VMEM((2 * units + extra, width), BF16),
            pltpu.VMEM((rows, width), BF16),
            pltpu.VMEM(down.shape, BF16),
            pltpu.VMEM(up.shape, BF16),
            pltpu.SemaphoreType.DMA((4,)),
            pltpu.SemaphoreType.DMA((4 + rows // CHUNK,)),
        ],
    )(
        ramp, normal1, context, attn_w, ffn_w, ffn_w, first_bias, grad_out, down, up, *vectors, down_bias
    )


def moved(pairs, sems):
    return [
        pltpu.make_async_copy(source, target, sems.at[at])
        for at, (source, target) in enumerate(pairs)
    ]


def start_all(copies):
    for copy in copies:
        copy.start()


def wait_all(copies):
    for copy in copies:
        copy.wait()


def norm_back_out(
    spans, grads, start_scr, normal_scr, scale_ref, gain_ref, low_scr, out_ref, low_ref, sems
):
    outs = []
    for at, span in enumerate(spans):
        grad = normalize_back(
            normal_scr[span], scale_ref[span, 0:1], gain_ref[...] * (grads[span] + start_scr[span])
        )
        start_scr[span] = grad
        low_scr[span] = grad.astype(BF16)
        outs += moved(
            [(start_scr.at[span], out_ref.at[span]), (low_scr.at[span], low_ref.at[span])],
            sems.at[pl.ds(2 * at, 2)],
        )
        start_all(outs[-2:])
    return outs


def ffn_backward_kernel(
    held, g_ref, w1_ref, w2_ref, slope_ref, start_ref, normal_ref, scale_ref, gain_ref,
    out_ref, low_ref, sum_scr, start_scr, normal_scr, low_scr, in_sems, out_sems,
):
    rows, width = g_ref.shape
    second = second_block(w2_ref, held, width)
    spans = parts_of(rows)
    step = pl.program_id(0)
    loads = moved([(start_ref, start_scr), (normal_ref, normal_scr)], in_sems)

    @pl.when(step == 0)
    def _():
        start_all(loads)
        sum_scr[...] = jnp.zeros_like(sum_scr)

    def finish(span, grad_act):
        grad_pre = (slope_ref[span].astype(F32) * grad_act).astype(BF16)
        sum_scr[span] += dot(grad_pre, w1_ref[...], 1, 1)

    waiting = None
    for span in spans:
        grad_act = dot(g_ref[span], second, 1, 1)
        if waiting is not None:
            finish(*waiting)
        waiting = (span, grad_act)
    finish(*waiting)

    @pl.when(step == pl.num_programs(0) - 1)
    def _():
        wait_all(loads)
        outs = norm_back_out(
            spans, sum_scr, start_scr, normal_scr, scale_ref, gain_ref, low_scr, out_ref, low_ref, out_sems
        )
        wait_all(outs)


def ffn_backward(grads, weights, w2_at, w1_at, slope, start, normal, scale, gain, held):
    rows, width = grads.shape
    wide = slope.shape[1]
    step = 512
    groups = wide // width
    return call(
        functools.partial(ffn_backward_kernel, held),
        "ffn_backward",
        (wide // step,),
        [
            whole((rows, width)),
            columns(width, step, w1_at // step),
            pl.BlockSpec((step // groups, wide), lambda i: (i, w2_at // wide)),
            columns(rows, step),
            anywhere(),
            anywhere(),
            whole((rows, 128)),
            whole((1, width)),
        ],
        [anywhere()] * 2,
        [jax.ShapeDtypeStruct((rows, width), F32), jax.ShapeDtypeStruct((rows, width), BF16)],
        4 * rows * width * wide,
        16 * rows * width + 4 * width * wide + 2 * rows * wide,
        0,
        [pltpu.VMEM((rows, width), F32)] * 3
        + [
            pltpu.VMEM((rows, width), BF16),
            pltpu.SemaphoreType.DMA((2,)),
            pltpu.SemaphoreType.DMA((2 * rows // CHUNK,)),
        ],
    )(grads, weights, weights, slope, start, normal, scale, gain)


def expo_loads(expo_ref, expo_scr, sems):
    step, count = pl.program_id(0), pl.num_programs(0)

    def load(group, pair):
        heads = pl.ds(group * GROUP + 2 * pair, 2)
        return pltpu.make_async_copy(
            expo_ref.at[heads], expo_scr.at[pl.ds(2 * pair, 2)], sems.at[pair]
        )

    def begin():
        for pair in range(GROUP // 2):
            load(0, pair).start()

    def before(pair):
        load(step, pair).wait()

    def after(pair):
        @pl.when(step < count - 1)
        def _():
            load(step + 1, pair).start()

    return begin, before, after


def cross_backward_kernel(
    g_ref, low_ref, normal_ref, scale_ref, gain_ref, wo_ref, wq_ref, wk_ref, wv_ref,
    q_ref, k_ref, v_ref, ctx_ref, expo_ref, inverse_ref,
    states_ref, sum_ref, sum_low_ref,
    total_scr, states_scr, start_scr, normal_scr, low_scr, grad_scr, dq_scr, dk_scr, dv_scr, s_scr, expo_scr,
    in_sems, out_sems, expo_sems,
):
    spans = parts_of(low_ref.shape[0])
    step = pl.program_id(0)
    loads = moved([(g_ref, start_scr), (normal_ref, normal_scr)], in_sems)
    begin, before, after = expo_loads(expo_ref, expo_scr, expo_sems)

    @pl.when(step == 0)
    def _():
        begin()
        start_all(loads)
        total_scr[...] = jnp.zeros_like(total_scr)
        states_scr[...] = jnp.zeros_like(states_scr)

    for span in spans:
        grad_scr[span] = dot(low_ref[span], wo_ref[...], 1, 1).astype(BF16)
    attend_backward(
        False, q_ref, k_ref, v_ref, ctx_ref, grad_scr, expo_scr, inverse_ref, dq_scr, dk_scr, dv_scr, s_scr,
        before, after,
    )
    for span in parts_of(states_ref.shape[0]):
        states_scr[span] += dot(dk_scr[span], wk_ref[...], 1, 1) + dot(dv_scr[span], wv_ref[...], 1, 1)
    for span in spans:
        total_scr[span] += dot(dq_scr[span], wq_ref[...], 1, 1)

    @pl.when(step == pl.num_programs(0) - 1)
    def _():
        states = pltpu.make_async_copy(states_scr, states_ref, out_sems.at[2 * len(spans)])
        states.start()
        wait_all(loads)
        outs = norm_back_out(
            spans, total_scr, start_scr, normal_scr, scale_ref, gain_ref, low_scr, sum_ref, sum_low_ref,
            out_sems,
        )
        wait_all([states, *outs])


def self_backward_kernel(
    g_ref, low_ref, wo_ref, wq_ref, wk_ref, wv_ref, q_ref, k_ref, v_ref, ctx_ref, expo_ref, inverse_ref,
    out_ref, total_scr, start_scr, grad_scr, dq_scr, dk_scr, dv_scr, s_scr, expo_scr,
    in_sems, out_sems, expo_sems,
):
    spans = parts_of(low_ref.shape[0])
    step = pl.program_id(0)
    load = pltpu.make_async_copy(g_ref, start_scr, in_sems.at[0])
    begin, before, after = expo_loads(expo_ref, expo_scr, expo_sems)

    @pl.when(step == 0)
    def _():
        begin()
        load.start()
        total_scr[...] = jnp.zeros_like(total_scr)

    for span in spans:
        grad_scr[span] = dot(low_ref[span], wo_ref[...], 1, 1).astype(BF16)
    attend_backward(
        True, q_ref, k_ref, v_ref, ctx_ref, grad_scr, expo_scr, inverse_ref, dq_scr, dk_scr, dv_scr, s_scr,
        before, after,
    )

    def back(span):
        return (
            dot(dq_scr[span], wq_ref[...], 1, 1)
            + dot(dk_scr[span], wk_ref[...], 1, 1)
            + dot(dv_scr[span], wv_ref[...], 1, 1)
        )

    last = step == pl.num_programs(0) - 1

    @pl.when(jnp.logical_not(last))
    def _():
        for span in spans:
            total_scr[span] += back(span)

    @pl.when(last)
    def _():
        load.wait()
        outs = []
        for at, span in enumerate(spans):
            total_scr[span] += start_scr[span] + back(span)
            outs.append(
                pltpu.make_async_copy(total_scr.at[span], out_ref.at[span], out_sems.at[at])
            )
            outs[-1].start()
        wait_all(outs)


def attend_in(rows, keys, width, at):
    group = GROUP * SIZE
    per = width // group
    weights = [pl.BlockSpec((group, width), lambda i: (i, at[0]))] + [
        columns(width, group, first * per) for first in at[1:]
    ]
    return weights + [
        columns(rows, group),
        columns(keys, group),
        columns(keys, group),
        columns(rows, group),
        anywhere(),
        columns(rows, group),
    ]


def attend_scratch(rows, keys):
    group = GROUP * SIZE
    return [
        pltpu.VMEM((rows, group), BF16),
        pltpu.VMEM((rows, group), BF16),
        pltpu.VMEM((keys, group), BF16),
        pltpu.VMEM((keys, group), BF16),
        pltpu.VMEM((2, rows, keys), BF16),
        pltpu.VMEM((GROUP, rows, keys), BF16),
        pltpu.SemaphoreType.DMA((2,)),
        pltpu.SemaphoreType.DMA((2 * rows // CHUNK + 1,)),
        pltpu.SemaphoreType.DMA((GROUP // 2,)),
    ]


def cross_backward(grads, low, normal, scale, gain, weights, at, saved):
    rows, width = grads.shape
    keys = saved[1].shape[0]
    return call(
        cross_backward_kernel,
        "cross_backward",
        (width // (GROUP * SIZE),),
        [anywhere(), whole((rows, width)), anywhere(), whole((rows, 128)), whole((1, width))]
        + attend_in(rows, keys, width, at),
        [anywhere()] * 3,
        [
            jax.ShapeDtypeStruct((keys, width), F32),
            jax.ShapeDtypeStruct((rows, width), F32),
            jax.ShapeDtypeStruct((rows, width), BF16),
        ],
        8 * rows * width * width + 8 * rows * keys * width,
        32 * rows * width + 8 * width * width + 32 * rows * keys,
        0,
        [
            pltpu.VMEM((rows, width), F32),
            pltpu.VMEM((keys, width), F32),
            pltpu.VMEM((rows, width), F32),
            pltpu.VMEM((rows, width), F32),
            pltpu.VMEM((rows, width), BF16),
        ]
        + attend_scratch(rows, keys),
    )(grads, low, normal, scale, gain, weights, weights, weights, weights, *saved)


def self_backward(grads, low, weights, at, saved):
    rows, width = grads.shape
    return call(
        self_backward_kernel,
        "self_backward",
        (width // (GROUP * SIZE),),
        [anywhere(), whole((rows, width))] + attend_in(rows, rows, width, at),
        anywhere(),
        jax.ShapeDtypeStruct((rows, width), F32),
        8 * rows * width * width + 4 * rows * rows * width,
        20 * rows * width + 8 * width * width + 32 * rows * rows,
        0,
        [pltpu.VMEM((rows, width), F32)] * 2 + attend_scratch(rows, rows),
    )(grads, low, weights, weights, weights, weights, *saved)


def unpack_kernel(all_ref, down_ref, down_b_ref, up_ref, up_b_ref, gain_ref, shift_ref):
    width, units = down_ref.shape
    up_ref[...] = all_ref[0:units].astype(F32)
    for at in range(0, width, units):
        down_ref[at : at + units] = all_ref[units : 2 * units, at : at + units].astype(F32)
    last = 2 * units
    small = all_ref[last : last + 16].astype(F32)
    up_b_ref[...] = small[0:1]
    gain_ref[...] = small[1:2]
    shift_ref[...] = small[2:3]
    down_b_ref[...] = small[3:4, 0:units]


def unpack(grads, down_shape):
    width, units = down_shape
    shapes = [(width, units), (1, units), (units, width)] + [(1, width)] * 3
    return call(
        unpack_kernel,
        "unpack",
        (),
        [whole(grads.shape)],
        [whole(shape) for shape in shapes],
        [jax.ShapeDtypeStruct(shape, F32) for shape in shapes],
        0,
        16 * width * units,
    )(grads)


def gather(shard):
    return lax.all_gather(shard, "fsdp", axis=0, tiled=True)


def sum_over(part, axis):
    count = lax.axis_size(axis)
    total, travel = part.astype(F32), part
    for _ in range(count - 1):
        travel = lax.ppermute(travel, axis, [(at, (at + 1) % count) for at in range(count)])
        total = total + travel.astype(F32)
    return total.astype(part.dtype)


def local(
    inputs,
    encoder,
    grad_out,
    target_mask,
    source_lengths,
    step,
    attn_in,
    attn_out,
    ffn_in,
    ffn_in_bias,
    ffn_out,
    ffn_out_bias,
    attn_bias,
    norm_gain,
    norm_shift,
    adapter_down,
    adapter_down_bias,
    adapter_up,
    adapter_up_bias,
    adapter_gain,
    adapter_shift,
):
    sequences, row_count, width = inputs.shape
    held = attn_in.shape[0]
    groups = ffn_out.shape[0] // held
    wide = ffn_in.shape[1]
    pad = jnp.zeros((held, 128), BF16)
    attn_w = gather(jnp.concatenate([attn_in, attn_out, pad], 1))
    ffn_w = jnp.concatenate(
        [ffn_out[at * held : (at + 1) * held] for at in range(groups)] + [ffn_in, pad], 1
    )
    ffn_w = gather(ffn_w)
    w1_at, w2_at = wide, 0
    self_at, cross_at = (6, 0, 1, 2), (7, 3, 4, 5)

    ramp = (4.0 * step.astype(F32) / RAMP).reshape(1)
    bias = [attn_bias[at : at + 1] for at in range(6)]
    gain = [norm_gain[at : at + 1] for at in range(3)]
    shift = [norm_shift[at : at + 1] for at in range(3)]
    tokens, states = inputs.reshape(-1, width), encoder.reshape(-1, width)
    target_length = jnp.sum((target_mask > 0).astype(jnp.int32)).reshape(1)

    *self_saved, self_ctx, self_expo, self_inverse = self_forward(
        target_length, tokens, attn_w, bias[0], bias[1]
    )
    normal1, scale1, *cross_saved, cross_ctx, cross_expo, cross_inverse = cross_forward(
        source_lengths,
        tokens,
        self_ctx,
        states,
        attn_w,
        self_at[:1] + cross_at[1:],
        (bias[2], gain[0], shift[0], bias[3], bias[4]),
    )
    token_total = sequences * row_count * lax.axis_size("fsdp") * lax.axis_size("dp")
    normal2, scale2, slope, layer_out, grad_ffn, grad_rest, adapter_grads = middle(
        ramp,
        normal1,
        cross_ctx,
        attn_w,
        cross_at[0],
        ffn_w,
        w2_at,
        w1_at,
        ffn_in_bias[None],
        grad_out.reshape(-1, width),
        adapter_down,
        adapter_up,
        (bias[5], gain[0], shift[0], gain[1], shift[1], gain[2], shift[2], ffn_out_bias[None])
        + (adapter_gain[None], adapter_shift[None], adapter_up_bias[None]),
        adapter_down_bias[None],
        held,
        16 * lax.axis_size("fsdp"),
        1.0 / math.sqrt(token_total),
    )
    scattered = lax.psum_scatter(adapter_grads, "fsdp", scatter_dimension=0, tiled=True)
    grad_sum2, low_sum2 = ffn_backward(
        grad_ffn, ffn_w, w2_at, w1_at, slope, grad_rest, normal2, scale2, gain[1], held
    )
    grad_encoder, grad_sum1, low_sum1 = cross_backward(
        grad_sum2,
        low_sum2,
        normal1,
        scale1,
        gain[0],
        attn_w,
        cross_at,
        (*cross_saved, cross_ctx, cross_expo, cross_inverse),
    )
    scattered, low_sum1 = lax.optimization_barrier((scattered, low_sum1))
    adapter_grads = gather(sum_over(scattered, "dp"))
    grad_input = self_backward(
        grad_sum1, low_sum1, attn_w, self_at, (*self_saved, self_ctx, self_expo, self_inverse)
    )
    grad_down, down_bias, grad_up, up_bias, grad_gain, grad_shift = unpack(
        adapter_grads, adapter_down.shape
    )
    return (
        layer_out.reshape(inputs.shape),
        grad_input.reshape(inputs.shape),
        grad_encoder.reshape(encoder.shape),
        grad_down,
        down_bias.reshape(-1),
        grad_up,
        up_bias.reshape(-1),
        grad_gain.reshape(-1),
        grad_shift.reshape(-1),
    )


def solution(mesh):
    batch = P(("fsdp", "dp"), None, None)
    split = P("fsdp", None)
    placed = (
        (batch,) * 3
        + (P(("fsdp", "dp"), None), P(("fsdp", "dp")), P())
        + (split, split, split, P(), split)
        + (P(),) * 10
    )
    return jax.shard_map(
        local,
        mesh=mesh,
        in_specs=placed,
        out_specs=(batch,) * 3 + (P(),) * 6,
        check_vma=False,
    )
```

```python
import functools
import math

import jax
import jax.numpy as jnp
from jax import lax
from jax.experimental import pallas as pl
from jax.experimental.pallas import tpu as pltpu
from jax.sharding import PartitionSpec as P

HEADS = 16
RAMP = 1000
EPS = 1e-05
F32 = jnp.float32
BF16 = jnp.bfloat16
VMEM_LIMIT = 58 * 2**20


def dot(left, right, left_dim, right_dim):
    return lax.dot_general(
        left, right, (((left_dim,), (right_dim,)), ((), ())), preferred_element_type=F32
    )


def call(kernel, name, grid, in_specs, out_specs, out_shape, flops, moved, exps=0, scratch=()):
    return pl.pallas_call(
        kernel,
        name=name,
        grid=grid,
        in_specs=in_specs,
        out_specs=out_specs,
        out_shape=out_shape,
        scratch_shapes=scratch,
        compiler_params=pltpu.CompilerParams(vmem_limit_bytes=VMEM_LIMIT),
        cost_estimate=pl.CostEstimate(
            flops=int(flops), bytes_accessed=int(moved), transcendentals=int(exps)
        ),
    )


def whole(shape):
    return pl.BlockSpec(shape, lambda *_: (0,) * len(shape), pipeline_mode=pl.Buffered(1))


def columns(rows, width, first=0):
    return pl.BlockSpec((rows, width), lambda i: (0, i + first))


def square(width, at):
    return pl.BlockSpec((width, width), lambda i: (0, at), pipeline_mode=pl.Buffered(1))


def normalize(values):
    center = values - jnp.mean(values, -1, keepdims=True)
    scale = lax.rsqrt(jnp.mean(center * center, -1, keepdims=True) + EPS)
    return center * scale, scale


def normalize_back(normal, scale, grad):
    return scale * (
        grad
        - jnp.mean(grad, -1, keepdims=True)
        - normal * jnp.mean(grad * normal, -1, keepdims=True)
    )


def split_three(values):
    high = values.astype(BF16).astype(F32)
    middle = (values - high).astype(BF16).astype(F32)
    return high, middle, values - high - middle


GROUP = 4
CHUNK = 256
SIZE = 64


def attend_forward(causal, ahead, q_ref, k_ref, v_ref, length, ctx_ref, expo_ref, inverse_ref):
    rows, keys = q_ref.shape[0], k_ref.shape[0]
    width = 2 * SIZE
    lane = lax.broadcasted_iota(jnp.int32, (rows, width), 1)
    key_lane = lax.broadcasted_iota(jnp.int32, (keys, width), 1)
    key_row = lax.broadcasted_iota(jnp.int32, (keys, width), 0)
    picks = jnp.where(lane % SIZE == 0, 1.0, 0.0).astype(BF16)
    extra = jnp.where(key_row < length, 0.0, -1e30).astype(BF16)
    one = jnp.asarray(1.0, BF16)
    left = lane[:CHUNK] < SIZE
    head_q, head_k, head_v = [], [], []
    for at in range(0, q_ref.shape[1], width):
        queries = q_ref[:, at : at + width]
        key_rows, value_rows = k_ref[:, at : at + width], v_ref[:, at : at + width]
        head_q += [jnp.where(lane < SIZE, queries, picks), jnp.where(lane < SIZE, picks, queries)]
        head_k += [
            jnp.where(key_lane < SIZE, key_rows, extra),
            jnp.where(key_lane < SIZE, extra, key_rows),
        ]
        head_v += [
            jnp.where(key_lane < SIZE, value_rows, one),
            jnp.where(key_lane < SIZE, one, value_rows),
        ]

    def scores(at, head):
        low, high = at * CHUNK, (at + 1) * CHUNK
        live = high if causal else keys
        found = dot(head_q[head][low:high], head_k[head][:live], 1, 1)
        if not causal:
            return found
        query_at = lax.broadcasted_iota(jnp.int32, (CHUNK, CHUNK), 0)
        key_at = lax.broadcasted_iota(jnp.int32, (CHUNK, CHUNK), 1)
        edge = jnp.where(key_at <= query_at, found[:, low:high], -1e30)
        return jnp.concatenate([found[:, :low], edge], 1) if low else edge

    done, waiting = {}, []

    def finish(at, head, found):
        low, high = at * CHUNK, (at + 1) * CHUNK
        live = found.shape[1]
        top = jnp.max(found, 1, keepdims=True)
        expo = jnp.exp(found - top).astype(BF16)
        expo_ref[head, low:high, :live] = expo
        done[head] = dot(expo, head_v[head][:live], 1, 0)
        if head % 2:
            first, second = done[head - 1], done[head]
            inverse = 1.0 / jnp.where(left, pltpu.roll(first, SIZE, 1), pltpu.roll(second, SIZE, 1))
            span = slice(head // 2 * width, (head // 2 + 1) * width)
            inverse_ref[low:high, span] = inverse
            ctx_ref[low:high, span] = (jnp.where(left, first, second) * inverse).astype(BF16)

    for pair in range(len(head_q) // 2):
        for at in range(rows // CHUNK):
            for head in (2 * pair, 2 * pair + 1):
                waiting.append((at, head, scores(at, head)))
                if len(waiting) > ahead:
                    finish(*waiting.pop(0))
    for unit in waiting:
        finish(*unit)


def attend_backward(
    causal, q_ref, k_ref, v_ref, ctx_ref, grad_ref, expo_ref, inverse_ref, dq_ref, dk_ref, dv_ref, s_scr,
    before, after,
):
    rows, keys = q_ref.shape[0], k_ref.shape[0]
    width = 2 * SIZE
    count = rows // CHUNK
    lane = lax.broadcasted_iota(jnp.int32, (rows, width), 1)
    key_lane = lax.broadcasted_iota(jnp.int32, (keys, width), 1)
    place = key_lane % SIZE
    ones = jnp.where((place >= 1) & (place <= 3), 1.0, 0.0).astype(BF16)
    for pair in range(q_ref.shape[1] // width):
        span = slice(pair * width, (pair + 1) * width)
        key_rows, value_rows = k_ref[:, span], v_ref[:, span]
        grads = (grad_ref[:, span].astype(F32) * inverse_ref[:, span]).astype(BF16)
        wide = grads.astype(F32)
        products = wide * ctx_ref[:, span].astype(F32)
        queries_t, grads_t = q_ref[:, span].T, grads.T
        head_g, head_v = [], []
        for head in range(2):
            mine = (lane < SIZE) if head == 0 else (lane >= SIZE)
            key_mine = (key_lane < SIZE) if head == 0 else (key_lane >= SIZE)
            base = SIZE if head == 0 else 0
            head_v.append(jnp.where(key_mine, value_rows, ones))
            dots = split_three(-jnp.sum(jnp.where(mine, products, 0.0), 1, keepdims=True))
            grad = jnp.where(mine, wide, 0.0)
            for index, part in enumerate(dots):
                grad = jnp.where(lane == base + index + 1, part, grad)
            head_g.append(grad.astype(BF16))

        grad_q, waiting = {}, []
        before(pair)

        def finish(at, head, grad_p, pair=pair, span=span, key_rows=key_rows, grad_q=grad_q):
            low, high = at * CHUNK, (at + 1) * CHUNK
            live = grad_p.shape[1]
            expo = expo_ref[2 * pair + head, low:high, :live]
            grad_s = (expo.astype(F32) * grad_p).astype(BF16)
            s_scr[head, low:high, :live] = grad_s
            grad_q[head] = dot(grad_s, key_rows[:live], 1, 0)
            if head:
                both = jnp.where(lane[low:high] < SIZE, grad_q[0], grad_q[1])
                dq_ref[low:high, span] = (both * SIZE**-0.5).astype(BF16)

        for at in range(count):
            for head in range(2):
                low, high = at * CHUNK, (at + 1) * CHUNK
                live = high if causal else keys
                waiting.append((at, head, dot(head_g[head][low:high], head_v[head][:live], 1, 1)))
                if len(waiting) > 1:
                    finish(*waiting.pop(0))
        for unit in waiting:
            finish(*unit)
        step = CHUNK if causal else keys
        for source, saved, first, to in (
            (grads_t, expo_ref, 2 * pair, dv_ref),
            (queries_t, s_scr, 0, dk_ref),
        ):
            for low in range(0, keys, step):
                start = low if causal else 0
                parts = [
                    dot(
                        source[head * SIZE : (head + 1) * SIZE, start:],
                        saved[first + head, start:, low : low + step],
                        1,
                        0,
                    )
                    for head in range(2)
                ]
                to[low : low + step, span] = jnp.concatenate(parts, 0).T.astype(BF16)
        after(pair)


def parts_of(rows):
    return [slice(at, at + CHUNK) for at in range(0, rows, CHUNK)]


def wide_scale(scale):
    return jnp.broadcast_to(scale, (scale.shape[0], 128))


def self_forward_kernel(
    length_ref, x_ref, wq_ref, wk_ref, wv_ref, bq_ref, bv_ref,
    q_ref, k_ref, v_ref, ctx_ref, expo_ref, inverse_ref,
):
    scale = jnp.asarray(SIZE**-0.5, BF16)
    for span in parts_of(x_ref.shape[0]):
        rows = x_ref[span]
        q_ref[span] = (dot(rows, wq_ref[...], 1, 0) + bq_ref[...]).astype(BF16) * scale
        k_ref[span] = dot(rows, wk_ref[...], 1, 0).astype(BF16)
        v_ref[span] = (dot(rows, wv_ref[...], 1, 0) + bv_ref[...]).astype(BF16)
    attend_forward(
        True, 2, q_ref, k_ref, v_ref, length_ref[0], ctx_ref, expo_ref, inverse_ref
    )


def anywhere():
    return pl.BlockSpec(memory_space=pl.ANY)


def scalar():
    return pl.BlockSpec(memory_space=pltpu.SMEM)


def attend_out(rows, keys, width):
    group = GROUP * SIZE
    heads = width // SIZE
    specs = (
        [columns(rows, group)]
        + [columns(keys, group)] * 2
        + [columns(rows, group)]
        + [pl.BlockSpec((GROUP, rows, keys), lambda i: (i, 0, 0)), columns(rows, group)]
    )
    shapes = (
        [jax.ShapeDtypeStruct((rows, width), BF16)]
        + [jax.ShapeDtypeStruct((keys, width), BF16)] * 2
        + [jax.ShapeDtypeStruct((rows, width), BF16)]
        + [
            jax.ShapeDtypeStruct((heads, rows, keys), BF16),
            jax.ShapeDtypeStruct((rows, width), F32),
        ]
    )
    return specs, shapes


def self_forward(length, values, weights, q_bias, v_bias):
    rows, width = values.shape
    group = GROUP * SIZE
    per = width // group
    specs, shapes = attend_out(rows, rows, width)
    return call(
        self_forward_kernel,
        "self_forward",
        (per,),
        [scalar(), whole((rows, width))]
        + [columns(width, group, at * per) for at in range(3)]
        + [columns(1, group)] * 2,
        specs,
        shapes,
        6 * rows * width * width + 4 * rows * rows * width,
        18 * rows * width + 6 * width * width + 32 * rows * rows,
        rows * rows * HEADS,
    )(length, values, weights, weights, weights, q_bias, v_bias)


def cross_forward_kernel(
    length_ref, x_ref, sctx_ref, states_ref, wo_ref, wq_ref, wk_ref, wv_ref,
    bo_ref, gain_ref, shift_ref, bq_ref, bv_ref,
    normal_ref, scale_ref, q_ref, k_ref, v_ref, ctx_ref, expo_ref, inverse_ref, hidden_scr,
):
    spans = parts_of(x_ref.shape[0])

    @pl.when(pl.program_id(0) == 0)
    def _():
        sums = [
            x_ref[span].astype(F32) + dot(sctx_ref[span], wo_ref[...], 1, 0) + bo_ref[...]
            for span in spans
        ]
        for span, total in zip(spans, sums):
            normal, scale = normalize(total)
            normal_ref[span] = normal
            scale_ref[span] = wide_scale(scale)
            hidden_scr[span] = (normal * gain_ref[...] + shift_ref[...]).astype(BF16)

    size = jnp.asarray(SIZE**-0.5, BF16)
    for span in parts_of(states_ref.shape[0]):
        rows = states_ref[span]
        k_ref[span] = dot(rows, wk_ref[...], 1, 0).astype(BF16)
        v_ref[span] = (dot(rows, wv_ref[...], 1, 0) + bv_ref[...]).astype(BF16)
    for span in spans:
        q_ref[span] = (dot(hidden_scr[span], wq_ref[...], 1, 0) + bq_ref[...]).astype(BF16) * size
    attend_forward(
        False, 2, q_ref, k_ref, v_ref, length_ref[0], ctx_ref, expo_ref, inverse_ref
    )


def cross_forward(length, values, context, states, weights, at, vectors):
    rows, width = values.shape
    keys = states.shape[0]
    group = GROUP * SIZE
    per = width // group
    specs, shapes = attend_out(rows, keys, width)
    return call(
        cross_forward_kernel,
        "cross_forward",
        (per,),
        [scalar(), whole((rows, width)), whole((rows, width)), whole((keys, width))]
        + [square(width, at[0])]
        + [columns(width, group, first * per) for first in at[1:]]
        + [whole((1, width))] * 3
        + [columns(1, group)] * 2,
        [whole((rows, width)), whole((rows, 128))] + specs,
        [jax.ShapeDtypeStruct((rows, width), F32), jax.ShapeDtypeStruct((rows, 128), F32)] + shapes,
        8 * rows * width * width + 4 * rows * keys * width,
        26 * rows * width + 8 * width * width + 32 * rows * keys,
        rows * keys * HEADS,
        [pltpu.VMEM((rows, width), BF16)],
    )(length, values, context, states, weights, weights, weights, weights, *vectors)


FFN_STEP = 1024


def second_block(w_ref, held, width):
    pieces = []
    for at in range(0, w_ref.shape[0], held):
        for group in range(w_ref.shape[1] // width):
            pieces.append(w_ref[at : at + held, group * width : (group + 1) * width])
    return jnp.concatenate(pieces, 0)


def in_turn(units, finish):
    waiting = None
    for first, span in units:
        value = first(span)
        if waiting is not None:
            finish(*waiting)
        waiting = (span, value)
    finish(*waiting)


def post_cross_kernel(
    ramp_ref, n1_ref, ctx_ref, wo_ref, down_ref, up_ref,
    bo_ref, gain1_ref, shift1_ref, gain2_ref, shift2_ref, b2_ref, gain_a_ref, shift_a_ref, up_b_ref,
    down_b_ref,
    normal_ref, hidden_ref, in_ref, act_ref, slope_ref, base_ref, stats_ref,
):
    spans = parts_of(n1_ref.shape[0])
    sums = [dot(ctx_ref[span], wo_ref[...], 1, 0) + bo_ref[...] for span in spans]
    for span, total in zip(spans, sums):
        normal, scale = normalize(total + (n1_ref[span] * gain1_ref[...] + shift1_ref[...]))
        normal_ref[span] = normal
        hidden = normal * gain2_ref[...] + shift2_ref[...]
        hidden_ref[span] = hidden.astype(BF16)
        base_ref[span] = hidden + b2_ref[...] + ramp_ref[0] * up_b_ref[...]
        mean_a = jnp.mean(hidden, -1, keepdims=True)
        normal_a, scale_a = normalize(hidden)
        in_ref[span] = (normal_a * gain_a_ref[...] + shift_a_ref[...]).astype(BF16)
        for at, value in enumerate((scale, mean_a, scale_a)):
            stats_ref[span, at * 128 : (at + 1) * 128] = wide_scale(value)
    for span in spans:
        lower = dot(in_ref[span], down_ref[...], 1, 0) + down_b_ref[...]
        gate = 1.0 / (1.0 + jnp.exp(-lower))
        act_ref[span] = (lower * gate).astype(BF16)
        slope_ref[span] = gate * (1.0 + lower * (1.0 - gate))
    for span in spans:
        base_ref[span] += ramp_ref[0] * dot(act_ref[span], up_ref[...], 1, 0)


def post_cross(ramp, normal1, context, weights, wo_at, down, up, vectors, down_bias):
    rows, width = normal1.shape
    units = down.shape[1]
    step = 512

    def block(wide):
        return pl.BlockSpec((step, wide), lambda i: (i, 0))

    return call(
        post_cross_kernel,
        "post_cross",
        (rows // step,),
        [scalar(), block(width), block(width), square(width, wo_at), whole(down.shape), whole(up.shape)]
        + [whole((1, width))] * 9
        + [whole((1, units))],
        [block(width)] * 3 + [block(units)] * 2 + [block(width), block(384)],
        [
            jax.ShapeDtypeStruct((rows, width), F32),
            jax.ShapeDtypeStruct((rows, width), BF16),
            jax.ShapeDtypeStruct((rows, width), BF16),
            jax.ShapeDtypeStruct((rows, units), BF16),
            jax.ShapeDtypeStruct((rows, units), F32),
            jax.ShapeDtypeStruct((rows, width), F32),
            jax.ShapeDtypeStruct((rows, 384), F32),
        ],
        2 * rows * width * width + 4 * rows * width * units,
        22 * rows * width,
        rows * units,
    )(ramp, normal1, context, weights, down, up, *vectors, down_bias)


def middle_kernel(
    held, factor, ramp_ref, hidden_ref, w1_ref, w2_ref, b1_ref, stats_ref,
    gain2_ref, shift2_ref, gain3_ref, shift3_ref, gain_a_ref,
    base_in, normal_in, in_in, act_in, slope_in, go_in, down_in, up_in,
    slope_ref, out_out, gffn_out, rest_out, grads_out,
    base_scr, normal_scr, in_scr, act_scr, slope_scr, go_scr, down_scr, up_scr,
    total_scr, out_scr, gffn_scr, branch_scr, lower_scr, grads_scr, in_sems, out_sems,
):
    rows, width = hidden_ref.shape
    units = down_in.shape[1]
    spans = parts_of(rows)
    step = pl.program_id(0)
    loads = moved(
        [
            (base_in, base_scr), (normal_in, normal_scr), (in_in, in_scr), (act_in, act_scr),
            (slope_in, slope_scr), (go_in, go_scr), (down_in, down_scr), (up_in, up_scr),
        ],
        in_sems,
    )

    @pl.when(step == 0)
    def _():
        total_scr[...] = jnp.zeros_like(total_scr)

    @pl.when(step == 1)
    def _():
        start_all(loads)

    def first(span):
        return dot(hidden_ref[span], w1_ref[...], 1, 0) + b1_ref[...]

    def finish(span, pre):
        phi = 0.5 + 0.5 * lax.erf(pre * (0.5**0.5))
        act = (pre * phi).astype(BF16)
        slope = phi + pre * (jnp.exp(pre * pre * -0.5) * (1.0 / math.sqrt(2.0 * math.pi)))
        slope_ref[span] = slope.astype(BF16)
        total_scr[span] += dot(act, second_block(w2_ref, held, width), 1, 0)

    in_turn([(first, span) for span in spans], finish)

    @pl.when(step == pl.num_programs(0) - 1)
    def _():
        ramp = ramp_ref[0]
        wait_all(loads)
        outs = moved([(out_scr, out_out), (gffn_scr, gffn_out), (grads_scr, grads_out)], out_sems)
        kind = grads_scr.dtype
        sums = [jnp.zeros((1, width), F32)] * 3 + [jnp.zeros((1, units), F32)]

        def norm_three(span):
            normal, scale = normalize(total_scr[span] + base_scr[span])
            out_scr[span] = (normal * gain3_ref[...] + shift3_ref[...]).astype(BF16)
            grad = normalize_back(normal, scale, gain3_ref[...] * go_scr[span].astype(F32))
            gffn_scr[span] = grad.astype(BF16)
            total_scr[span] = grad
            grad_branch = (ramp * grad).astype(BF16)
            branch_scr[span] = grad_branch
            sums[0] = sums[0] + jnp.sum(grad_branch.astype(F32), 0, keepdims=True)

        def adapter_back(span):
            grad_act = dot(branch_scr[span], up_scr[...], 1, 1).astype(BF16).astype(F32)
            grad_lower = (slope_scr[span] * grad_act).astype(BF16)
            lower_scr[span] = grad_lower
            sums[3] = sums[3] + jnp.sum(grad_lower.astype(F32), 0, keepdims=True)

        for span in spans:
            norm_three(span)
            adapter_back(span)
        start_all(outs[:2])
        grads_scr[0:units, 0:width] = (dot(act_scr[...], branch_scr[...], 0, 0) * factor).astype(kind)
        for at, span in enumerate(spans):
            grad_adapt = dot(lower_scr[span], down_scr[...], 1, 1)
            hidden = normal_scr[span] * gain2_ref[...] + shift2_ref[...]
            scale_a = stats_ref[span, 256:257]
            normal_a = (hidden - stats_ref[span, 128:129]) * scale_a
            total_scr[span] += normalize_back(normal_a, scale_a, gain_a_ref[...] * grad_adapt)
            outs.append(
                pltpu.make_async_copy(total_scr.at[span], rest_out.at[span], out_sems.at[3 + at])
            )
            outs[-1].start()
            sums[1] = sums[1] + jnp.sum(grad_adapt * normal_a, 0, keepdims=True)
            sums[2] = sums[2] + jnp.sum(grad_adapt, 0, keepdims=True)
        for at in range(0, width, units):
            grads_scr[units : 2 * units, at : at + units] = (
                dot(in_scr[:, at : at + units], lower_scr[...], 0, 0) * factor
            ).astype(kind)
        vectors = []
        for row in sums:
            row = row * factor
            vectors += [row[:, low : low + 128] for low in range(0, row.shape[1], 128)]
        vectors += [jnp.zeros((1, 128), F32)] * (4 * width // 128 - len(vectors))
        small = jnp.concatenate(vectors, 0).astype(kind)
        lines = small.shape[0]
        grads_scr[0:lines, width:] = small
        grads_scr[lines:, width:] = jnp.zeros((2 * units - lines, 128), kind)
        outs[2].start()
        wait_all(outs)


def middle(
    ramp, hidden, ffn_w, w2_at, w1_at, first_bias, stats, vectors, late, held, factor
):
    rows, width = hidden.shape
    wide = first_bias.shape[1]
    down, up = late[-2:]
    units = down.shape[1]
    step = FFN_STEP
    groups = wide // width
    return call(
        functools.partial(middle_kernel, held, factor),
        "middle",
        (wide // step,),
        [
            scalar(),
            whole((rows, width)),
            columns(width, step, w1_at // step),
            pl.BlockSpec((step // groups, wide), lambda i: (i, w2_at // wide)),
            columns(1, step),
            whole((rows, 384)),
        ]
        + [whole((1, width))] * 5
        + [anywhere()] * len(late),
        [columns(rows, step)] + [anywhere()] * 4,
        [
            jax.ShapeDtypeStruct((rows, wide), BF16),
            jax.ShapeDtypeStruct((rows, width), BF16),
            jax.ShapeDtypeStruct((rows, width), BF16),
            jax.ShapeDtypeStruct((rows, width), F32),
            jax.ShapeDtypeStruct((2 * units, width + 128), BF16),
        ],
        4 * rows * width * wide + 8 * rows * width * units,
        22 * rows * width + 4 * width * wide + 2 * rows * wide + 12 * width * units,
        2 * rows * wide,
        [pltpu.VMEM(value.shape, value.dtype) for value in late]
        + [
            pltpu.VMEM((rows, width), F32),
            pltpu.VMEM((rows, width), BF16),
            pltpu.VMEM((rows, width), BF16),
            pltpu.VMEM((rows, width), BF16),
            pltpu.VMEM((rows, units), BF16),
            pltpu.VMEM((2 * units, width + 128), BF16),
            pltpu.SemaphoreType.DMA((len(late),)),
            pltpu.SemaphoreType.DMA((3 + rows // CHUNK,)),
        ],
    )(ramp, hidden, ffn_w, ffn_w, first_bias, stats, *vectors, *late)


def moved(pairs, sems):
    return [
        pltpu.make_async_copy(source, target, sems.at[at])
        for at, (source, target) in enumerate(pairs)
    ]


def start_all(copies):
    for copy in copies:
        copy.start()


def wait_all(copies):
    for copy in copies:
        copy.wait()


def norm_back_out(
    grads, start_scr, normal_scr, scale_ref, gain_ref, low_scr, out_ref, low_ref, sems
):
    outs = []

    def back(span):
        grad = normalize_back(
            normal_scr[span], scale_ref[span, 0:1], gain_ref[...] * (grads[span] + start_scr[span])
        )
        start_scr[span] = grad
        low_scr[span] = grad.astype(BF16)
        copies = moved(
            [(start_scr.at[span], out_ref.at[span]), (low_scr.at[span], low_ref.at[span])],
            sems.at[pl.ds(len(outs), 2)],
        )
        start_all(copies)
        outs.extend(copies)

    return outs, back


def ffn_backward_kernel(
    held, g_ref, w1_ref, w2_ref, slope_ref, start_ref, normal_ref, scale_ref, gain_ref,
    out_ref, low_ref, sum_scr, start_scr, normal_scr, low_scr, in_sems, out_sems,
):
    rows, width = g_ref.shape
    spans = parts_of(rows)
    step = pl.program_id(0)
    loads = moved([(start_ref, start_scr), (normal_ref, normal_scr)], in_sems)

    @pl.when(step == 0)
    def _():
        sum_scr[...] = jnp.zeros_like(sum_scr)

    @pl.when(step == 1)
    def _():
        start_all(loads)

    def finish(span, grad_act):
        grad_pre = (slope_ref[span].astype(F32) * grad_act).astype(BF16)
        sum_scr[span] += dot(grad_pre, w1_ref[...], 1, 1)

    def first(span):
        return dot(g_ref[span], second_block(w2_ref, held, width), 1, 1)

    last = step == pl.num_programs(0) - 1

    @pl.when(jnp.logical_not(last))
    def _():
        in_turn([(first, span) for span in spans], finish)

    @pl.when(last)
    def _():
        wait_all(loads)
        outs, back = norm_back_out(
            sum_scr, start_scr, normal_scr, scale_ref, gain_ref, low_scr, out_ref, low_ref, out_sems
        )
        held_act, done = None, []
        for span in [*spans, None]:
            grad_act = first(span) if span is not None else None
            if held_act is not None:
                finish(*held_act)
                done.append(held_act[0])
            held_act = (span, grad_act)
            if len(done) > 1:
                back(done.pop(0))
        back(done.pop(0))
        wait_all(outs)


def ffn_backward(grads, weights, w2_at, w1_at, slope, start, normal, scale, gain, held):
    rows, width = grads.shape
    wide = slope.shape[1]
    step = FFN_STEP
    groups = wide // width
    return call(
        functools.partial(ffn_backward_kernel, held),
        "ffn_backward",
        (wide // step,),
        [
            whole((rows, width)),
            columns(width, step, w1_at // step),
            pl.BlockSpec((step // groups, wide), lambda i: (i, w2_at // wide)),
            columns(rows, step),
            anywhere(),
            anywhere(),
            pl.BlockSpec((rows, 128), lambda i: (0, 0), pipeline_mode=pl.Buffered(1)),
            whole((1, width)),
        ],
        [anywhere()] * 2,
        [jax.ShapeDtypeStruct((rows, width), F32), jax.ShapeDtypeStruct((rows, width), BF16)],
        4 * rows * width * wide,
        16 * rows * width + 4 * width * wide + 2 * rows * wide,
        0,
        [pltpu.VMEM((rows, width), F32)] * 3
        + [
            pltpu.VMEM((rows, width), BF16),
            pltpu.SemaphoreType.DMA((2,)),
            pltpu.SemaphoreType.DMA((2 * rows // CHUNK,)),
        ],
    )(grads, weights, weights, slope, start, normal, scale, gain)


def expo_loads(expo_ref, expo_scr, sems):
    step, count = pl.program_id(0), pl.num_programs(0)

    def load(group, pair):
        heads = pl.ds(group * GROUP + 2 * pair, 2)
        return pltpu.make_async_copy(
            expo_ref.at[heads], expo_scr.at[pl.ds(2 * pair, 2)], sems.at[pair]
        )

    def begin():
        load(0, 0).start()

    def before(pair):
        load(step, pair).wait()

        @pl.when(step == 0)
        def _():
            for later in range(pair + 1, min(pair + 2, GROUP // 2)):
                load(0, later).start()

    def after(pair):
        @pl.when(step < count - 1)
        def _():
            load(step + 1, pair).start()

    return begin, before, after


def cross_backward_kernel(
    g_ref, low_ref, normal_ref, scale_ref, gain_ref, wo_ref, wq_ref, wk_ref, wv_ref,
    q_ref, k_ref, v_ref, ctx_ref, expo_ref, inverse_ref,
    states_ref, sum_ref, sum_low_ref,
    total_scr, states_scr, start_scr, normal_scr, low_scr, grad_scr, dq_scr, dk_scr, dv_scr, s_scr, expo_scr,
    in_sems, out_sems, expo_sems,
):
    spans = parts_of(low_ref.shape[0])
    step = pl.program_id(0)
    loads = moved([(g_ref, start_scr), (normal_ref, normal_scr)], in_sems)
    begin, before, after = expo_loads(expo_ref, expo_scr, expo_sems)

    @pl.when(step == 0)
    def _():
        begin()
        total_scr[...] = jnp.zeros_like(total_scr)
        states_scr[...] = jnp.zeros_like(states_scr)

    @pl.when(step == 1)
    def _():
        start_all(loads)

    for span in spans:
        grad_scr[span] = dot(low_ref[span], wo_ref[...], 1, 1).astype(BF16)
    attend_backward(
        False, q_ref, k_ref, v_ref, ctx_ref, grad_scr, expo_scr, inverse_ref, dq_scr, dk_scr, dv_scr, s_scr,
        before, after,
    )
    for span in parts_of(states_ref.shape[0]):
        states_scr[span] += dot(dk_scr[span], wk_ref[...], 1, 1) + dot(dv_scr[span], wv_ref[...], 1, 1)

    def add(span):
        total_scr[span] += dot(dq_scr[span], wq_ref[...], 1, 1)

    last = step == pl.num_programs(0) - 1

    @pl.when(jnp.logical_not(last))
    def _():
        for span in spans:
            add(span)

    @pl.when(last)
    def _():
        states = pltpu.make_async_copy(states_scr, states_ref, out_sems.at[2 * len(spans)])
        states.start()
        wait_all(loads)
        outs, back = norm_back_out(
            total_scr, start_scr, normal_scr, scale_ref, gain_ref, low_scr, sum_ref, sum_low_ref, out_sems
        )
        add(spans[0])
        for before_span, span in zip(spans, spans[1:]):
            add(span)
            back(before_span)
        back(spans[-1])
        wait_all([states, *outs])


def self_backward_kernel(
    g_ref, low_ref, wo_ref, wq_ref, wk_ref, wv_ref, q_ref, k_ref, v_ref, ctx_ref, expo_ref, inverse_ref,
    out_ref, total_scr, start_scr, grad_scr, dq_scr, dk_scr, dv_scr, s_scr, expo_scr,
    in_sems, out_sems, expo_sems,
):
    spans = parts_of(low_ref.shape[0])
    step = pl.program_id(0)
    load = pltpu.make_async_copy(g_ref, start_scr, in_sems.at[0])
    begin, before, after = expo_loads(expo_ref, expo_scr, expo_sems)

    @pl.when(step == 0)
    def _():
        begin()
        total_scr[...] = jnp.zeros_like(total_scr)

    @pl.when(step == 1)
    def _():
        load.start()

    for span in spans:
        grad_scr[span] = dot(low_ref[span], wo_ref[...], 1, 1).astype(BF16)
    attend_backward(
        True, q_ref, k_ref, v_ref, ctx_ref, grad_scr, expo_scr, inverse_ref, dq_scr, dk_scr, dv_scr, s_scr,
        before, after,
    )

    def back(span):
        return (
            dot(dq_scr[span], wq_ref[...], 1, 1)
            + dot(dk_scr[span], wk_ref[...], 1, 1)
            + dot(dv_scr[span], wv_ref[...], 1, 1)
        )

    last = step == pl.num_programs(0) - 1

    @pl.when(jnp.logical_not(last))
    def _():
        for span in spans:
            total_scr[span] += back(span)

    @pl.when(last)
    def _():
        load.wait()
        outs = []
        for at, span in enumerate(spans):
            total_scr[span] += start_scr[span] + back(span)
            outs.append(
                pltpu.make_async_copy(total_scr.at[span], out_ref.at[span], out_sems.at[at])
            )
            outs[-1].start()
        wait_all(outs)


def attend_in(rows, keys, width, at):
    group = GROUP * SIZE
    per = width // group
    weights = [pl.BlockSpec((group, width), lambda i: (i, at[0]))] + [
        columns(width, group, first * per) for first in at[1:]
    ]
    return weights + [
        columns(rows, group),
        columns(keys, group),
        columns(keys, group),
        columns(rows, group),
        anywhere(),
        columns(rows, group),
    ]


def attend_scratch(rows, keys):
    group = GROUP * SIZE
    return [
        pltpu.VMEM((rows, group), BF16),
        pltpu.VMEM((rows, group), BF16),
        pltpu.VMEM((keys, group), BF16),
        pltpu.VMEM((keys, group), BF16),
        pltpu.VMEM((2, rows, keys), BF16),
        pltpu.VMEM((GROUP, rows, keys), BF16),
        pltpu.SemaphoreType.DMA((2,)),
        pltpu.SemaphoreType.DMA((2 * rows // CHUNK + 1,)),
        pltpu.SemaphoreType.DMA((GROUP // 2,)),
    ]


def cross_backward(grads, low, normal, scale, gain, weights, at, saved):
    rows, width = grads.shape
    keys = saved[1].shape[0]
    return call(
        cross_backward_kernel,
        "cross_backward",
        (width // (GROUP * SIZE),),
        [anywhere(), whole((rows, width)), anywhere(), whole((rows, 128)), whole((1, width))]
        + attend_in(rows, keys, width, at),
        [anywhere()] * 3,
        [
            jax.ShapeDtypeStruct((keys, width), F32),
            jax.ShapeDtypeStruct((rows, width), F32),
            jax.ShapeDtypeStruct((rows, width), BF16),
        ],
        8 * rows * width * width + 8 * rows * keys * width,
        32 * rows * width + 8 * width * width + 32 * rows * keys,
        0,
        [
            pltpu.VMEM((rows, width), F32),
            pltpu.VMEM((keys, width), F32),
            pltpu.VMEM((rows, width), F32),
            pltpu.VMEM((rows, width), F32),
            pltpu.VMEM((rows, width), BF16),
        ]
        + attend_scratch(rows, keys),
    )(grads, low, normal, scale, gain, weights, weights, weights, weights, *saved)


def self_backward(grads, low, weights, at, saved):
    rows, width = grads.shape
    return call(
        self_backward_kernel,
        "self_backward",
        (width // (GROUP * SIZE),),
        [anywhere(), whole((rows, width))] + attend_in(rows, rows, width, at),
        anywhere(),
        jax.ShapeDtypeStruct((rows, width), F32),
        8 * rows * width * width + 4 * rows * rows * width,
        20 * rows * width + 8 * width * width + 32 * rows * rows,
        0,
        [pltpu.VMEM((rows, width), F32)] * 2 + attend_scratch(rows, rows),
    )(grads, low, weights, weights, weights, weights, *saved)


def unpack_kernel(up_in, down_in, small_in, down_ref, up_ref, up_b_ref, gain_ref, shift_ref, down_b_ref):
    units = down_ref.shape[2]
    up_ref[...] = up_in[...].astype(F32)
    for at in range(down_ref.shape[0]):
        down_ref[at] = down_in[:, at * units : (at + 1) * units].astype(F32)

    @pl.when(pl.program_id(0) == 0)
    def _():
        small = small_in[...].astype(F32)
        per = up_b_ref.shape[1] // 128
        for at, ref in enumerate((up_b_ref, gain_ref, shift_ref, down_b_ref)):
            for part in range(ref.shape[1] // 128):
                row = at * per + part
                ref[:, part * 128 : (part + 1) * 128] = small[row : row + 1]


def unpack(grads, down_shape):
    width, units = down_shape
    halves = width // units
    steps = 4
    step = units // steps
    small = 4 * width // 128

    def fixed(shape):
        return pl.BlockSpec(shape, lambda i: (0, 0))

    down, *rest = call(
        unpack_kernel,
        "unpack",
        (steps,),
        [
            pl.BlockSpec((step, width), lambda i: (i, 0)),
            pl.BlockSpec((step, width), lambda i: (i + steps, 0)),
            pl.BlockSpec((small, 128), lambda i: (0, width // 128)),
        ],
        [
            pl.BlockSpec((halves, step, units), lambda i: (0, i, 0)),
            pl.BlockSpec((step, width), lambda i: (i, 0)),
        ]
        + [fixed((1, width))] * 3
        + [fixed((1, units))],
        [
            jax.ShapeDtypeStruct((halves, units, units), F32),
            jax.ShapeDtypeStruct((units, width), F32),
        ]
        + [jax.ShapeDtypeStruct((1, width), F32)] * 3
        + [jax.ShapeDtypeStruct((1, units), F32)],
        0,
        16 * width * units,
    )(grads, grads, grads)
    return down.reshape(down_shape), *rest


def gather(shard):
    return lax.all_gather(shard, "fsdp", axis=0, tiled=True)


def sum_over(part, axis):
    count = lax.axis_size(axis)
    total, travel = part.astype(F32), part
    for _ in range(count - 1):
        travel = lax.ppermute(travel, axis, [(at, (at + 1) % count) for at in range(count)])
        total = total + travel.astype(F32)
    return total.astype(part.dtype)


def local(
    inputs,
    encoder,
    grad_out,
    target_mask,
    source_lengths,
    step,
    attn_in,
    attn_out,
    ffn_in,
    ffn_in_bias,
    ffn_out,
    ffn_out_bias,
    attn_bias,
    norm_gain,
    norm_shift,
    adapter_down,
    adapter_down_bias,
    adapter_up,
    adapter_up_bias,
    adapter_gain,
    adapter_shift,
):
    sequences, row_count, width = inputs.shape
    held = attn_in.shape[0]
    groups = ffn_out.shape[0] // held
    wide = ffn_in.shape[1]
    pad = jnp.zeros((held, 128), BF16)
    attn_w = gather(jnp.concatenate([attn_in, attn_out, pad], 1))
    ffn_w = jnp.concatenate(
        [ffn_out[at * held : (at + 1) * held] for at in range(groups)] + [ffn_in, pad], 1
    )
    ffn_w = gather(ffn_w)
    w1_at, w2_at = wide, 0
    self_at, cross_at = (6, 0, 1, 2), (7, 3, 4, 5)

    ramp = (4.0 * step.astype(F32) / RAMP).reshape(1)
    bias = [attn_bias[at : at + 1] for at in range(6)]
    gain = [norm_gain[at : at + 1] for at in range(3)]
    shift = [norm_shift[at : at + 1] for at in range(3)]
    tokens, states = inputs.reshape(-1, width), encoder.reshape(-1, width)
    target_length = jnp.sum((target_mask > 0).astype(jnp.int32)).reshape(1)

    *self_saved, self_ctx, self_expo, self_inverse = self_forward(
        target_length, tokens, attn_w, bias[0], bias[1]
    )
    normal1, scale1, *cross_saved, cross_ctx, cross_expo, cross_inverse = cross_forward(
        source_lengths,
        tokens,
        self_ctx,
        states,
        attn_w,
        self_at[:1] + cross_at[1:],
        (bias[2], gain[0], shift[0], bias[3], bias[4]),
    )
    token_total = sequences * row_count * lax.axis_size("fsdp") * lax.axis_size("dp")
    normal2, hidden2, adapt_in, adapt_act, adapt_slope, base, stats = post_cross(
        ramp,
        normal1,
        cross_ctx,
        attn_w,
        cross_at[0],
        adapter_down,
        adapter_up,
        (bias[5], gain[0], shift[0], gain[1], shift[1], ffn_out_bias[None])
        + (adapter_gain[None], adapter_shift[None], adapter_up_bias[None]),
        adapter_down_bias[None],
    )
    slope, layer_out, grad_ffn, grad_rest, adapter_grads = middle(
        ramp,
        hidden2,
        ffn_w,
        w2_at,
        w1_at,
        ffn_in_bias[None],
        stats,
        (gain[1], shift[1], gain[2], shift[2], adapter_gain[None]),
        (base, normal2, adapt_in, adapt_act, adapt_slope)
        + (grad_out.reshape(-1, width), adapter_down, adapter_up),
        held,
        1.0 / math.sqrt(token_total),
    )
    scattered = lax.psum_scatter(adapter_grads, "fsdp", scatter_dimension=0, tiled=True)
    grad_sum2, low_sum2 = ffn_backward(
        grad_ffn, ffn_w, w2_at, w1_at, slope, grad_rest, normal2, stats, gain[1], held
    )
    grad_encoder, grad_sum1, low_sum1 = cross_backward(
        grad_sum2,
        low_sum2,
        normal1,
        scale1,
        gain[0],
        attn_w,
        cross_at,
        (*cross_saved, cross_ctx, cross_expo, cross_inverse),
    )
    scattered, low_sum1 = lax.optimization_barrier((scattered, low_sum1))
    adapter_grads = gather(sum_over(scattered, "dp"))
    grad_input = self_backward(
        grad_sum1, low_sum1, attn_w, self_at, (*self_saved, self_ctx, self_expo, self_inverse)
    )
    grad_down, grad_up, up_bias, grad_gain, grad_shift, down_bias = unpack(
        adapter_grads, adapter_down.shape
    )
    return (
        layer_out.reshape(inputs.shape),
        grad_input.reshape(inputs.shape),
        grad_encoder.reshape(encoder.shape),
        grad_down,
        down_bias.reshape(-1),
        grad_up,
        up_bias.reshape(-1),
        grad_gain.reshape(-1),
        grad_shift.reshape(-1),
    )


def solution(mesh):
    batch = P(("fsdp", "dp"), None, None)
    split = P("fsdp", None)
    placed = (
        (batch,) * 3
        + (P(("fsdp", "dp"), None), P(("fsdp", "dp")), P())
        + (split, split, split, P(), split)
        + (P(),) * 10
    )
    return jax.shard_map(
        local,
        mesh=mesh,
        in_specs=placed,
        out_specs=(batch,) * 3 + (P(),) * 6,
        check_vma=False,
    )
```

```python
import functools
import math

import jax
import jax.numpy as jnp
from jax import lax
from jax.experimental import pallas as pl
from jax.experimental.pallas import tpu as pltpu
from jax.sharding import PartitionSpec as P

HEADS = 16
RAMP = 1000
EPS = 1e-05
F32 = jnp.float32
BF16 = jnp.bfloat16
VMEM_LIMIT = 58 * 2**20


def dot(left, right, left_dim, right_dim):
    return lax.dot_general(
        left, right, (((left_dim,), (right_dim,)), ((), ())), preferred_element_type=F32
    )


def call(kernel, name, grid, in_specs, out_specs, out_shape, flops, moved, exps=0, scratch=()):
    return pl.pallas_call(
        kernel,
        name=name,
        grid=grid,
        in_specs=in_specs,
        out_specs=out_specs,
        out_shape=out_shape,
        scratch_shapes=scratch,
        compiler_params=pltpu.CompilerParams(vmem_limit_bytes=VMEM_LIMIT),
        cost_estimate=pl.CostEstimate(
            flops=int(flops), bytes_accessed=int(moved), transcendentals=int(exps)
        ),
    )


def whole(shape):
    return pl.BlockSpec(shape, lambda *_: (0,) * len(shape), pipeline_mode=pl.Buffered(1))


def columns(rows, width, first=0):
    return pl.BlockSpec((rows, width), lambda i: (0, i + first))


def square(width, at):
    return pl.BlockSpec((width, width), lambda i: (0, at), pipeline_mode=pl.Buffered(1))


def normalize(values):
    center = values - jnp.mean(values, -1, keepdims=True)
    scale = lax.rsqrt(jnp.mean(center * center, -1, keepdims=True) + EPS)
    return center * scale, scale


def normalize_back(normal, scale, grad):
    return scale * (
        grad
        - jnp.mean(grad, -1, keepdims=True)
        - normal * jnp.mean(grad * normal, -1, keepdims=True)
    )


def split_three(values):
    high = values.astype(BF16).astype(F32)
    middle = (values - high).astype(BF16).astype(F32)
    return high, middle, values - high - middle


GROUP = 4
CHUNK = 256
SIZE = 64


def attend_forward(causal, ahead, q_ref, k_ref, v_ref, length, ctx_ref, expo_ref, inverse_ref):
    rows, keys = q_ref.shape[0], k_ref.shape[0]
    width = 2 * SIZE
    lane = lax.broadcasted_iota(jnp.int32, (rows, width), 1)
    key_lane = lax.broadcasted_iota(jnp.int32, (keys, width), 1)
    key_row = lax.broadcasted_iota(jnp.int32, (keys, width), 0)
    picks = jnp.where(lane % SIZE == 0, 1.0, 0.0).astype(BF16)
    extra = jnp.where(key_row < length, 0.0, -1e30).astype(BF16)
    one = jnp.asarray(1.0, BF16)
    left = lane[:CHUNK] < SIZE
    head_q, head_k, head_v = [], [], []
    for at in range(0, q_ref.shape[1], width):
        queries = q_ref[:, at : at + width]
        key_rows, value_rows = k_ref[:, at : at + width], v_ref[:, at : at + width]
        head_q += [jnp.where(lane < SIZE, queries, picks), jnp.where(lane < SIZE, picks, queries)]
        head_k += [
            jnp.where(key_lane < SIZE, key_rows, extra),
            jnp.where(key_lane < SIZE, extra, key_rows),
        ]
        head_v += [
            jnp.where(key_lane < SIZE, value_rows, one),
            jnp.where(key_lane < SIZE, one, value_rows),
        ]

    def scores(at, head):
        low, high = at * CHUNK, (at + 1) * CHUNK
        live = high if causal else keys
        found = dot(head_q[head][low:high], head_k[head][:live], 1, 1)
        if not causal:
            return found
        query_at = lax.broadcasted_iota(jnp.int32, (CHUNK, CHUNK), 0)
        key_at = lax.broadcasted_iota(jnp.int32, (CHUNK, CHUNK), 1)
        edge = jnp.where(key_at <= query_at, found[:, low:high], -1e30)
        return jnp.concatenate([found[:, :low], edge], 1) if low else edge

    done, waiting = {}, []

    def finish(at, head, found):
        low, high = at * CHUNK, (at + 1) * CHUNK
        live = found.shape[1]
        top = jnp.max(found, 1, keepdims=True)
        expo = jnp.exp(found - top).astype(BF16)
        expo_ref[head, low:high, :live] = expo
        done[head] = dot(expo, head_v[head][:live], 1, 0)
        if head % 2:
            first, second = done[head - 1], done[head]
            inverse = 1.0 / jnp.where(left, pltpu.roll(first, SIZE, 1), pltpu.roll(second, SIZE, 1))
            span = slice(head // 2 * width, (head // 2 + 1) * width)
            inverse_ref[low:high, span] = inverse
            ctx_ref[low:high, span] = (jnp.where(left, first, second) * inverse).astype(BF16)

    for pair in range(len(head_q) // 2):
        for at in range(rows // CHUNK):
            for head in (2 * pair, 2 * pair + 1):
                waiting.append((at, head, scores(at, head)))
                if len(waiting) > ahead:
                    finish(*waiting.pop(0))
    for unit in waiting:
        finish(*unit)


def attend_backward(
    causal, q_ref, k_ref, v_ref, ctx_ref, grad_ref, expo_ref, inverse_ref, dq_ref, dk_ref, dv_ref, s_scr,
    before, after,
):
    rows, keys = q_ref.shape[0], k_ref.shape[0]
    width = 2 * SIZE
    count = rows // CHUNK
    pairs = q_ref.shape[1] // width
    lane = lax.broadcasted_iota(jnp.int32, (rows, width), 1)
    key_lane = lax.broadcasted_iota(jnp.int32, (keys, width), 1)
    place, key_place = lane % SIZE, key_lane % SIZE
    ones = jnp.where((key_place >= 1) & (key_place <= 3), 1.0, 0.0).astype(BF16)
    from_lane = lax.broadcasted_iota(jnp.int32, (2 * width, width), 0) % width
    to_lane = lax.broadcasted_iota(jnp.int32, (2 * width, width), 1)
    swap = jnp.where((from_lane < SIZE) != (to_lane < SIZE), 1.0, 0.0).astype(BF16)

    def prepare(pair):
        span = slice(pair * width, (pair + 1) * width)
        value_rows = v_ref[:, span]
        grads = (grad_ref[:, span].astype(F32) * inverse_ref[:, span]).astype(BF16)
        products = grads.astype(F32) * ctx_ref[:, span].astype(F32)
        high = products.astype(BF16)
        low = (products - high.astype(F32)).astype(BF16)
        parts = split_three(-dot(jnp.concatenate([high, low], 1), swap, 1, 0))
        packed = jnp.zeros((rows, width), F32)
        for index, part in enumerate(parts):
            packed = jnp.where(place == index + 1, part, packed)
        packed = packed.astype(BF16)
        head_g = [jnp.where(lane < SIZE, grads, packed), jnp.where(lane < SIZE, packed, grads)]
        head_v = [
            jnp.where(key_lane < SIZE, value_rows, ones),
            jnp.where(key_lane < SIZE, ones, value_rows),
        ]
        return head_g, head_v, q_ref[:, span].T, grads.T

    def multiply(pair, head_g, head_v):
        span = slice(pair * width, (pair + 1) * width)
        key_rows = k_ref[:, span]
        grad_q, waiting = {}, []

        def finish(at, head, grad_p):
            low, high = at * CHUNK, (at + 1) * CHUNK
            live = grad_p.shape[1]
            expo = expo_ref[2 * pair + head, low:high, :live]
            grad_s = (expo.astype(F32) * grad_p).astype(BF16)
            s_scr[head, low:high, :live] = grad_s
            grad_q[head] = dot(grad_s, key_rows[:live], 1, 0)
            if head:
                both = jnp.where(lane[low:high] < SIZE, grad_q[0], grad_q[1])
                dq_ref[low:high, span] = (both * SIZE**-0.5).astype(BF16)

        for at in range(count):
            for head in range(2):
                low, high = at * CHUNK, (at + 1) * CHUNK
                live = high if causal else keys
                waiting.append((at, head, dot(head_g[head][low:high], head_v[head][:live], 1, 1)))
                if len(waiting) > 1:
                    finish(*waiting.pop(0))
        for unit in waiting:
            finish(*unit)

    def collect(pair, queries_t, grads_t):
        span = slice(pair * width, (pair + 1) * width)
        step = CHUNK if causal else keys
        for source, saved, first, to in (
            (grads_t, expo_ref, 2 * pair, dv_ref),
            (queries_t, s_scr, 0, dk_ref),
        ):
            for low in range(0, keys, step):
                start = low if causal else 0
                parts = [
                    dot(
                        source[head * SIZE : (head + 1) * SIZE, start:],
                        saved[first + head, start:, low : low + step],
                        1,
                        0,
                    )
                    for head in range(2)
                ]
                to[low : low + step, span] = jnp.concatenate(parts, 0).T.astype(BF16)

    ready = prepare(0)
    for pair in range(pairs):
        head_g, head_v, queries_t, grads_t = ready
        before(pair)
        multiply(pair, head_g, head_v)
        ready = prepare(pair + 1) if pair + 1 < pairs else None
        collect(pair, queries_t, grads_t)
        after(pair)


def parts_of(rows):
    return [slice(at, at + CHUNK) for at in range(0, rows, CHUNK)]


def wide_scale(scale):
    return jnp.broadcast_to(scale, (scale.shape[0], 128))


def self_forward_kernel(
    length_ref, x_ref, wq_ref, wk_ref, wv_ref, bq_ref, bv_ref,
    q_ref, k_ref, v_ref, ctx_ref, expo_ref, inverse_ref,
):
    scale = jnp.asarray(SIZE**-0.5, BF16)
    for span in parts_of(x_ref.shape[0]):
        rows = x_ref[span]
        q_ref[span] = (dot(rows, wq_ref[...], 1, 0) + bq_ref[...]).astype(BF16) * scale
        k_ref[span] = dot(rows, wk_ref[...], 1, 0).astype(BF16)
        v_ref[span] = (dot(rows, wv_ref[...], 1, 0) + bv_ref[...]).astype(BF16)
    attend_forward(
        True, 2, q_ref, k_ref, v_ref, length_ref[0], ctx_ref, expo_ref, inverse_ref
    )


def anywhere():
    return pl.BlockSpec(memory_space=pl.ANY)


def scalar():
    return pl.BlockSpec(memory_space=pltpu.SMEM)


def attend_out(rows, keys, width):
    group = GROUP * SIZE
    heads = width // SIZE
    specs = (
        [columns(rows, group)]
        + [columns(keys, group)] * 2
        + [columns(rows, group)]
        + [pl.BlockSpec((GROUP, rows, keys), lambda i: (i, 0, 0)), columns(rows, group)]
    )
    shapes = (
        [jax.ShapeDtypeStruct((rows, width), BF16)]
        + [jax.ShapeDtypeStruct((keys, width), BF16)] * 2
        + [jax.ShapeDtypeStruct((rows, width), BF16)]
        + [
            jax.ShapeDtypeStruct((heads, rows, keys), BF16),
            jax.ShapeDtypeStruct((rows, width), F32),
        ]
    )
    return specs, shapes


def self_forward(length, values, weights, q_bias, v_bias):
    rows, width = values.shape
    group = GROUP * SIZE
    per = width // group
    specs, shapes = attend_out(rows, rows, width)
    return call(
        self_forward_kernel,
        "self_forward",
        (per,),
        [scalar(), whole((rows, width))]
        + [columns(width, group, at * per) for at in range(3)]
        + [columns(1, group)] * 2,
        specs,
        shapes,
        6 * rows * width * width + 4 * rows * rows * width,
        18 * rows * width + 6 * width * width + 32 * rows * rows,
        rows * rows * HEADS,
    )(length, values, weights, weights, weights, q_bias, v_bias)


def cross_forward_kernel(
    length_ref, x_ref, sctx_ref, states_ref, wo_ref, wq_ref, wk_ref, wv_ref,
    bo_ref, gain_ref, shift_ref, bq_ref, bv_ref,
    normal_ref, scale_ref, q_ref, k_ref, v_ref, ctx_ref, expo_ref, inverse_ref, hidden_scr,
):
    spans = parts_of(x_ref.shape[0])

    @pl.when(pl.program_id(0) == 0)
    def _():
        sums = [
            x_ref[span].astype(F32) + dot(sctx_ref[span], wo_ref[...], 1, 0) + bo_ref[...]
            for span in spans
        ]
        for span, total in zip(spans, sums):
            normal, scale = normalize(total)
            normal_ref[span] = normal
            scale_ref[span] = wide_scale(scale)
            hidden_scr[span] = (normal * gain_ref[...] + shift_ref[...]).astype(BF16)

    size = jnp.asarray(SIZE**-0.5, BF16)
    for span in parts_of(states_ref.shape[0]):
        rows = states_ref[span]
        k_ref[span] = dot(rows, wk_ref[...], 1, 0).astype(BF16)
        v_ref[span] = (dot(rows, wv_ref[...], 1, 0) + bv_ref[...]).astype(BF16)
    for span in spans:
        q_ref[span] = (dot(hidden_scr[span], wq_ref[...], 1, 0) + bq_ref[...]).astype(BF16) * size
    attend_forward(
        False, 2, q_ref, k_ref, v_ref, length_ref[0], ctx_ref, expo_ref, inverse_ref
    )


def cross_forward(length, values, context, states, weights, at, vectors):
    rows, width = values.shape
    keys = states.shape[0]
    group = GROUP * SIZE
    per = width // group
    specs, shapes = attend_out(rows, keys, width)
    return call(
        cross_forward_kernel,
        "cross_forward",
        (per,),
        [scalar(), whole((rows, width)), whole((rows, width)), whole((keys, width))]
        + [square(width, at[0])]
        + [columns(width, group, first * per) for first in at[1:]]
        + [whole((1, width))] * 3
        + [columns(1, group)] * 2,
        [whole((rows, width)), whole((rows, 128))] + specs,
        [jax.ShapeDtypeStruct((rows, width), F32), jax.ShapeDtypeStruct((rows, 128), F32)] + shapes,
        8 * rows * width * width + 4 * rows * keys * width,
        26 * rows * width + 8 * width * width + 32 * rows * keys,
        rows * keys * HEADS,
        [pltpu.VMEM((rows, width), BF16)],
    )(length, values, context, states, weights, weights, weights, weights, *vectors)


FFN_STEP = 1024
FFN_BACK_STEP = 512


def second_block(w_ref, held, width):
    pieces = []
    for at in range(0, w_ref.shape[0], held):
        for group in range(w_ref.shape[1] // width):
            pieces.append(w_ref[at : at + held, group * width : (group + 1) * width])
    return jnp.concatenate(pieces, 0)


def in_turn(units, finish):
    waiting = None
    for first, span in units:
        value = first(span)
        if waiting is not None:
            finish(*waiting)
        waiting = (span, value)
    finish(*waiting)


def post_cross_kernel(
    ramp_ref, n1_ref, ctx_ref, wo_ref, down_ref, up_ref,
    bo_ref, gain1_ref, shift1_ref, gain2_ref, shift2_ref, b2_ref, gain_a_ref, shift_a_ref, up_b_ref,
    down_b_ref,
    normal_ref, hidden_ref, in_ref, act_ref, slope_ref, base_ref, scale_ref, scale_a_ref,
):
    spans = parts_of(n1_ref.shape[0])
    sums = [dot(ctx_ref[span], wo_ref[...], 1, 0) + bo_ref[...] for span in spans]
    for span, total in zip(spans, sums):
        normal, scale = normalize(total + (n1_ref[span] * gain1_ref[...] + shift1_ref[...]))
        normal_ref[span] = normal
        hidden = normal * gain2_ref[...] + shift2_ref[...]
        hidden_ref[span] = hidden.astype(BF16)
        base_ref[span] = hidden + b2_ref[...] + ramp_ref[0] * up_b_ref[...]
        normal_a, scale_a = normalize(hidden)
        in_ref[span] = (normal_a * gain_a_ref[...] + shift_a_ref[...]).astype(BF16)
        scale_ref[span] = wide_scale(scale)
        scale_a_ref[span] = wide_scale(scale_a)
    for span in spans:
        lower = dot(in_ref[span], down_ref[...], 1, 0) + down_b_ref[...]
        gate = 1.0 / (1.0 + jnp.exp(-lower))
        act_ref[span] = (lower * gate).astype(BF16)
        slope_ref[span] = (gate * (1.0 + lower * (1.0 - gate))).astype(BF16)
    for span in spans:
        base_ref[span] += ramp_ref[0] * dot(act_ref[span], up_ref[...], 1, 0)


def post_cross(ramp, normal1, context, weights, wo_at, down, up, vectors, down_bias):
    rows, width = normal1.shape
    units = down.shape[1]
    step = 512

    def block(wide):
        return pl.BlockSpec((step, wide), lambda i: (i, 0))

    return call(
        post_cross_kernel,
        "post_cross",
        (rows // step,),
        [scalar(), block(width), block(width), square(width, wo_at), whole(down.shape), whole(up.shape)]
        + [whole((1, width))] * 9
        + [whole((1, units))],
        [block(width)] * 3 + [block(units)] * 2 + [block(width)] + [block(128)] * 2,
        [
            jax.ShapeDtypeStruct((rows, width), F32),
            jax.ShapeDtypeStruct((rows, width), BF16),
            jax.ShapeDtypeStruct((rows, width), BF16),
            jax.ShapeDtypeStruct((rows, units), BF16),
            jax.ShapeDtypeStruct((rows, units), BF16),
            jax.ShapeDtypeStruct((rows, width), F32),
            jax.ShapeDtypeStruct((rows, 128), F32),
            jax.ShapeDtypeStruct((rows, 128), F32),
        ],
        2 * rows * width * width + 4 * rows * width * units,
        22 * rows * width,
        rows * units,
    )(ramp, normal1, context, weights, down, up, *vectors, down_bias)


def middle_kernel(
    held, factor, ramp_ref, hidden_ref, w1_ref, w2_ref, b1_ref, scale_a_ref,
    gain3_ref, shift3_ref, gain_a_ref, shift_a_ref,
    base_in, go_in, slope_in, up_in, act_in, down_in, in_in,
    slope_ref, out_out, gffn_out, rest_out, grads_out,
    base_scr, go_scr, slope_scr, up_scr, act_scr, down_scr, in_scr,
    total_scr, out_scr, gffn_scr, branch_scr, lower_scr, grads_scr, in_sems, out_sems,
):
    rows, width = hidden_ref.shape
    units = down_in.shape[1]
    spans = parts_of(rows)
    step = pl.program_id(0)
    loads = moved(
        [
            (base_in, base_scr), (go_in, go_scr), (slope_in, slope_scr), (up_in, up_scr),
            (act_in, act_scr), (down_in, down_scr), (in_in, in_scr),
        ],
        in_sems,
    )

    @pl.when(step == 0)
    def _():
        total_scr[...] = jnp.zeros_like(total_scr)

    for at, part in enumerate((loads[:1], loads[1:4], loads[4:])):
        pl.when(step == at + 1)(functools.partial(start_all, part))

    def first(span):
        return dot(hidden_ref[span], w1_ref[...], 1, 0) + b1_ref[...]

    def finish(span, pre):
        phi = 0.5 + 0.5 * lax.erf(pre * (0.5**0.5))
        act = (pre * phi).astype(BF16)
        slope = phi + pre * (jnp.exp(pre * pre * -0.5) * (1.0 / math.sqrt(2.0 * math.pi)))
        slope_ref[span] = slope.astype(BF16)
        total_scr[span] += dot(act, second_block(w2_ref, held, width), 1, 0)

    in_turn([(first, span) for span in spans], finish)

    @pl.when(step == pl.num_programs(0) - 1)
    def _():
        ramp = ramp_ref[0]
        wait_all(loads[:4])
        outs = moved([(out_scr, out_out), (gffn_scr, gffn_out), (grads_scr, grads_out)], out_sems)
        kind = grads_scr.dtype
        sums = [jnp.zeros((1, width), F32)] * 3 + [jnp.zeros((1, units), F32)]

        def norm_three(span):
            normal, scale = normalize(total_scr[span] + base_scr[span])
            out_scr[span] = (normal * gain3_ref[...] + shift3_ref[...]).astype(BF16)
            grad = normalize_back(normal, scale, gain3_ref[...] * go_scr[span].astype(F32))
            gffn_scr[span] = grad.astype(BF16)
            total_scr[span] = grad
            grad_branch = (ramp * grad).astype(BF16)
            branch_scr[span] = grad_branch
            sums[0] = sums[0] + jnp.sum(grad_branch.astype(F32), 0, keepdims=True)

        def adapter_back(span):
            grad_act = dot(branch_scr[span], up_scr[...], 1, 1).astype(BF16).astype(F32)
            grad_lower = (slope_scr[span].astype(F32) * grad_act).astype(BF16)
            lower_scr[span] = grad_lower
            sums[3] = sums[3] + jnp.sum(grad_lower.astype(F32), 0, keepdims=True)

        for span in spans:
            norm_three(span)
            adapter_back(span)
        start_all(outs[:2])
        wait_all(loads[4:])
        grads_scr[0:units, 0:width] = (dot(act_scr[...], branch_scr[...], 0, 0) * factor).astype(kind)
        for at, span in enumerate(spans):
            grad_adapt = dot(lower_scr[span], down_scr[...], 1, 1)
            normal_a = (in_scr[span].astype(F32) - shift_a_ref[...]) * (1.0 / gain_a_ref[...])
            scale_a = scale_a_ref[span, 0:1]
            total_scr[span] += normalize_back(normal_a, scale_a, gain_a_ref[...] * grad_adapt)
            outs.append(
                pltpu.make_async_copy(total_scr.at[span], rest_out.at[span], out_sems.at[3 + at])
            )
            outs[-1].start()
            sums[1] = sums[1] + jnp.sum(grad_adapt * normal_a, 0, keepdims=True)
            sums[2] = sums[2] + jnp.sum(grad_adapt, 0, keepdims=True)
        for at in range(0, width, units):
            grads_scr[units : 2 * units, at : at + units] = (
                dot(in_scr[:, at : at + units], lower_scr[...], 0, 0) * factor
            ).astype(kind)
        vectors = []
        for row in sums:
            row = row * factor
            vectors += [row[:, low : low + 128] for low in range(0, row.shape[1], 128)]
        vectors += [jnp.zeros((1, 128), F32)] * (4 * width // 128 - len(vectors))
        small = jnp.concatenate(vectors, 0).astype(kind)
        lines = small.shape[0]
        grads_scr[0:lines, width:] = small
        grads_scr[lines:, width:] = jnp.zeros((2 * units - lines, 128), kind)
        outs[2].start()
        wait_all(outs)


def middle(
    ramp, hidden, ffn_w, w2_at, w1_at, first_bias, scale_a, vectors, late, held, factor
):
    rows, width = hidden.shape
    wide = first_bias.shape[1]
    units = late[2].shape[1]
    step = FFN_STEP
    groups = wide // width
    return call(
        functools.partial(middle_kernel, held, factor),
        "middle",
        (wide // step,),
        [
            scalar(),
            whole((rows, width)),
            columns(width, step, w1_at // step),
            pl.BlockSpec((step // groups, wide), lambda i: (i, w2_at // wide)),
            columns(1, step),
            whole((rows, 128)),
        ]
        + [whole((1, width))] * 4
        + [anywhere()] * len(late),
        [columns(rows, step)] + [anywhere()] * 4,
        [
            jax.ShapeDtypeStruct((rows, wide), BF16),
            jax.ShapeDtypeStruct((rows, width), BF16),
            jax.ShapeDtypeStruct((rows, width), BF16),
            jax.ShapeDtypeStruct((rows, width), F32),
            jax.ShapeDtypeStruct((2 * units, width + 128), BF16),
        ],
        4 * rows * width * wide + 8 * rows * width * units,
        22 * rows * width + 4 * width * wide + 2 * rows * wide + 12 * width * units,
        2 * rows * wide,
        [pltpu.VMEM(value.shape, value.dtype) for value in late]
        + [
            pltpu.VMEM((rows, width), F32),
            pltpu.VMEM((rows, width), BF16),
            pltpu.VMEM((rows, width), BF16),
            pltpu.VMEM((rows, width), BF16),
            pltpu.VMEM((rows, units), BF16),
            pltpu.VMEM((2 * units, width + 128), BF16),
            pltpu.SemaphoreType.DMA((len(late),)),
            pltpu.SemaphoreType.DMA((3 + rows // CHUNK,)),
        ],
    )(ramp, hidden, ffn_w, ffn_w, first_bias, scale_a, *vectors, *late)


def moved(pairs, sems):
    return [
        pltpu.make_async_copy(source, target, sems.at[at])
        for at, (source, target) in enumerate(pairs)
    ]


def start_all(copies):
    for copy in copies:
        copy.start()


def wait_all(copies):
    for copy in copies:
        copy.wait()


def expo_loads(expo_ref, expo_scr, sems, group, count):
    def load(which, pair):
        heads = pl.ds(which * GROUP + 2 * pair, 2)
        return pltpu.make_async_copy(
            expo_ref.at[heads], expo_scr.at[pl.ds(2 * pair, 2)], sems.at[pair]
        )

    def begin():
        for pair in range(GROUP // 2):
            load(0, pair).start()

    def before(pair):
        load(group, pair).wait()

    def after(pair):
        @pl.when(group < count - 1)
        def _():
            load(group + 1, pair).start()

    return begin, before, after


def group_loads(pairs, sems):
    def copies(group, part):
        slot = lax.rem(group, 2)
        return [
            pltpu.make_async_copy(source(group), target.at[slot], sems.at[at, slot])
            for at, (source, target) in list(enumerate(pairs))[part]
        ]

    def start(group):
        start_all(copies(group, slice(None)))

    def wait(group, part):
        wait_all(copies(group, part))

    return start, wait


def column_group(ref, first=0):
    width = GROUP * SIZE
    return lambda group: ref.at[:, pl.ds(pl.multiple_of(group * width, width) + first, width)]


def row_group(ref, first, width):
    depth = GROUP * SIZE
    return lambda group: ref.at[
        pl.ds(pl.multiple_of(group * depth, depth), depth), pl.ds(first, width)
    ]


def ffn_cross_backward_kernel(
    held, ffn_steps, at,
    g_ref, w1_ref, w2_ref, slope_ref, start_ref, normal2_ref, scale2_ref, gain2_ref,
    normal1_ref, scale1_ref, gain1_ref, attn_ref, q_ref, k_ref, v_ref, ctx_ref, expo_ref, inverse_ref,
    sum_ref, sum_low_ref, dk_ref, dv_ref,
    total_scr, start_scr, normal_scr, low_scr, grad_scr, dq_scr, s_scr, expo_scr,
    in_sems, out_sems, expo_sems,
    wo_scr, wq_scr, q_scr, k_scr, v_scr, ctx_scr, inverse_scr, group_sems,
):
    rows, width = g_ref.shape
    spans = parts_of(rows)
    step, steps = pl.program_id(0), pl.num_programs(0)
    loads = moved([(start_ref, start_scr), (normal2_ref, normal_scr)], in_sems)
    late = pltpu.make_async_copy(normal1_ref, normal_scr, in_sems.at[2])
    group, groups = step - ffn_steps, steps - ffn_steps
    begin, before, after = expo_loads(expo_ref, expo_scr, expo_sems, group, groups)
    start_group, wait_group = group_loads(
        [
            (row_group(attn_ref, at[0] * width, width), wo_scr),
            (column_group(q_ref), q_scr),
            (column_group(k_ref), k_scr),
            (column_group(v_ref), v_scr),
            (column_group(ctx_ref), ctx_scr),
            (column_group(inverse_ref), inverse_scr),
            (column_group(attn_ref, at[1] * width), wq_scr),
        ],
        group_sems,
    )

    @pl.when(step == 0)
    def _():
        total_scr[...] = jnp.zeros_like(total_scr)

    pl.when(step == 1)(loads[0].start)
    pl.when(step == ffn_steps // 2)(loads[1].start)
    pl.when(step == ffn_steps - 2)(functools.partial(start_group, 0))

    def first(span):
        return dot(g_ref[span], second_block(w2_ref, held, width), 1, 1)

    def finish(span, grad_act):
        grad_pre = (slope_ref[span].astype(F32) * grad_act).astype(BF16)
        total_scr[span] += dot(grad_pre, w1_ref[...], 1, 1)

    @pl.when(step < ffn_steps - 1)
    def _():
        in_turn([(first, span) for span in spans], finish)

    @pl.when(step == ffn_steps - 1)
    def _():
        begin()
        wait_all(loads)

        def back(span):
            grad = normalize_back(
                normal_scr[span],
                scale2_ref[span, 0:1],
                gain2_ref[...] * (total_scr[span] + start_scr[span]),
            )
            total_scr[span] = grad
            low_scr[span] = grad.astype(BF16)

        held_act, done = None, []
        for span in [*spans, None]:
            grad_act = first(span) if span is not None else None
            if held_act is not None:
                finish(*held_act)
                done.append(held_act[0])
            held_act = (span, grad_act)
            if len(done) > 1:
                back(done.pop(0))
        back(done.pop(0))
        late.start()

    slot = lax.rem(step, 2) if ffn_steps % 2 == 0 else lax.rem(step + 1, 2)

    def add(span):
        total_scr[span] += dot(dq_scr[span], wq_scr[slot], 1, 1)

    @pl.when(step == ffn_steps)
    def _():
        dq_scr[...] = jnp.zeros_like(dq_scr)

    @pl.when(step >= ffn_steps)
    def _():
        wait_group(group, slice(None))
        for span in spans:
            grad_scr[span] = dot(low_scr[span], wo_scr[slot], 1, 1).astype(BF16)
        last_slot = jnp.where(group > 0, 1 - slot, slot)
        for span in spans:
            total_scr[span] += dot(dq_scr[span], wq_scr[last_slot], 1, 1)
        pl.when(group < groups - 1)(functools.partial(start_group, group + 1))
        attend_backward(
            False, q_scr.at[slot], k_scr.at[slot], v_scr.at[slot], ctx_scr.at[slot], grad_scr, expo_scr,
            inverse_scr.at[slot], dq_scr, dk_ref, dv_ref, s_scr, before, after,
        )

    last = step == steps - 1

    @pl.when(last)
    def _():
        late.wait()
        outs = []

        def back(span):
            grad = normalize_back(
                normal_scr[span], scale1_ref[span, 0:1], gain1_ref[...] * total_scr[span]
            )
            total_scr[span] = grad
            low_scr[span] = grad.astype(BF16)
            copies = moved(
                [(total_scr.at[span], sum_ref.at[span]), (low_scr.at[span], sum_low_ref.at[span])],
                out_sems.at[pl.ds(len(outs), 2)],
            )
            start_all(copies)
            outs.extend(copies)

        add(spans[0])
        for before_span, span in zip(spans, spans[1:]):
            add(span)
            back(before_span)
        back(spans[-1])
        wait_all(outs)


def self_backward_kernel(
    at, cross_at,
    g_ref, low_ref, cdk_ref, cdv_ref, attn_ref, q_ref, k_ref, v_ref, ctx_ref, expo_ref, inverse_ref,
    out_ref, states_ref,
    total_scr, states_scr, start_scr, low_scr, grad_scr, dq_scr, dk_scr, dv_scr, s_scr, expo_scr,
    in_sems, out_sems, expo_sems,
    wo_scr, wq_scr, wk_scr, wv_scr, q_scr, k_scr, v_scr, ctx_scr, inverse_scr,
    cdk_scr, cdv_scr, cwk_scr, cwv_scr, group_sems,
):
    width = low_ref.shape[1]
    spans = parts_of(low_ref.shape[0])
    step, steps = pl.program_id(0), pl.num_programs(0)
    slot = lax.rem(step, 2)
    load, low_load = moved([(g_ref, start_scr), (low_ref, low_scr)], in_sems)
    begin, before, after = expo_loads(expo_ref, expo_scr, expo_sems, step, steps)
    start_group, wait_group = group_loads(
        [
            (row_group(attn_ref, at[0] * width, width), wo_scr),
            (column_group(cdk_ref), cdk_scr),
            (column_group(attn_ref, cross_at[2] * width), cwk_scr),
            (column_group(cdv_ref), cdv_scr),
            (column_group(attn_ref, cross_at[3] * width), cwv_scr),
            (column_group(q_ref), q_scr),
            (column_group(k_ref), k_scr),
            (column_group(v_ref), v_scr),
            (column_group(ctx_ref), ctx_scr),
            (column_group(inverse_ref), inverse_scr),
            (column_group(attn_ref, at[1] * width), wq_scr),
            (column_group(attn_ref, at[2] * width), wk_scr),
            (column_group(attn_ref, at[3] * width), wv_scr),
        ],
        group_sems,
    )

    @pl.when(step == 0)
    def _():
        low_load.start()
        start_group(0)
        begin()
        total_scr[...] = jnp.zeros_like(total_scr)
        states_scr[...] = jnp.zeros_like(states_scr)

    pl.when(step == 1)(load.start)

    pl.when(step == 0)(low_load.wait)
    wait_group(step, slice(None))
    pl.when(step < steps - 1)(functools.partial(start_group, step + 1))
    for span in spans:
        grad_scr[span] = dot(low_scr[span], wo_scr[slot], 1, 1).astype(BF16)
    for span in parts_of(states_scr.shape[0]):
        states_scr[span] += dot(cdk_scr[slot, span], cwk_scr[slot], 1, 1) + dot(
            cdv_scr[slot, span], cwv_scr[slot], 1, 1
        )
    attend_backward(
        True, q_scr.at[slot], k_scr.at[slot], v_scr.at[slot], ctx_scr.at[slot], grad_scr, expo_scr,
        inverse_scr.at[slot], dq_scr, dk_scr, dv_scr, s_scr, before, after,
    )

    def back(span):
        return (
            dot(dq_scr[span], wq_scr[slot], 1, 1)
            + dot(dk_scr[span], wk_scr[slot], 1, 1)
            + dot(dv_scr[span], wv_scr[slot], 1, 1)
        )

    last = step == steps - 1

    @pl.when(jnp.logical_not(last))
    def _():
        for span in spans:
            total_scr[span] += back(span)

    @pl.when(last)
    def _():
        load.wait()
        outs = [pltpu.make_async_copy(states_scr, states_ref, out_sems.at[len(spans)])]
        outs[0].start()
        for index, span in enumerate(spans):
            total_scr[span] += start_scr[span] + back(span)
            outs.append(
                pltpu.make_async_copy(total_scr.at[span], out_ref.at[span], out_sems.at[index])
            )
            outs[-1].start()
        wait_all(outs)


def attend_scratch(rows, keys):
    return [
        pltpu.VMEM((2, rows, keys), BF16),
        pltpu.VMEM((GROUP, rows, keys), BF16),
        pltpu.SemaphoreType.DMA((3,)),
        pltpu.SemaphoreType.DMA((2 * rows // CHUNK,)),
        pltpu.SemaphoreType.DMA((GROUP // 2,)),
    ]


def group_scratch(rows, keys, width, weights):
    group = GROUP * SIZE
    return (
        [pltpu.VMEM((2, group, width), BF16)]
        + [pltpu.VMEM((2, width, group), BF16)] * weights
        + [pltpu.VMEM((2, rows, group), BF16)]
        + [pltpu.VMEM((2, keys, group), BF16)] * 2
        + [pltpu.VMEM((2, rows, group), BF16), pltpu.VMEM((2, rows, group), F32)]
    )


def ffn_cross_backward(
    grads, ffn_w, w2_at, w1_at, slope, start, normal2, scale2, gain2, normal1, scale1, gain1, attn_w, at, saved,
    held,
):
    rows, width = grads.shape
    keys = saved[1].shape[0]
    wide = slope.shape[1]
    groups = wide // width
    block = FFN_BACK_STEP
    steps = wide // block
    group = GROUP * SIZE

    def unit(i):
        return jnp.minimum(i, steps - 1)

    def out(i):
        return (0, jnp.maximum(i - steps, 0))

    return call(
        functools.partial(ffn_cross_backward_kernel, held, steps, at),
        "ffn_cross_backward",
        (steps + width // group,),
        [
            whole((rows, width)),
            pl.BlockSpec((width, block), lambda i: (0, unit(i) + w1_at // block)),
            pl.BlockSpec((block // groups, wide), lambda i: (unit(i), w2_at // wide)),
            pl.BlockSpec((rows, block), lambda i: (0, unit(i))),
            anywhere(),
            anywhere(),
            whole((rows, 128)),
            whole((1, width)),
            anywhere(),
            whole((rows, 128)),
            whole((1, width)),
        ]
        + [anywhere()] * 7,
        [anywhere()] * 2 + [pl.BlockSpec((keys, group), out)] * 2,
        [
            jax.ShapeDtypeStruct((rows, width), F32),
            jax.ShapeDtypeStruct((rows, width), BF16),
            jax.ShapeDtypeStruct((keys, width), BF16),
            jax.ShapeDtypeStruct((keys, width), BF16),
        ],
        4 * rows * width * (width + wide) + 8 * rows * keys * width,
        48 * rows * width + 4 * width * (width + wide) + 2 * rows * wide + 32 * rows * keys,
        0,
        [pltpu.VMEM((rows, width), F32)] * 3
        + [pltpu.VMEM((rows, width), BF16)]
        + [pltpu.VMEM((rows, group), BF16)] * 2
        + attend_scratch(rows, keys)
        + group_scratch(rows, keys, width, 1)
        + [pltpu.SemaphoreType.DMA((7, 2))],
    )(
        grads, ffn_w, ffn_w, slope, start, normal2, scale2, gain2, normal1, scale1, gain1, attn_w, *saved
    )


def self_backward(grads, low, cross_grads, weights, at, cross_at, saved):
    rows, width = grads.shape
    keys = cross_grads[0].shape[0]
    group = GROUP * SIZE
    return call(
        functools.partial(self_backward_kernel, at, cross_at),
        "self_backward",
        (width // group,),
        [anywhere()] * 11,
        [anywhere()] * 2,
        [jax.ShapeDtypeStruct((rows, width), F32), jax.ShapeDtypeStruct((keys, width), F32)],
        8 * rows * width * width + 4 * keys * width * width + 4 * rows * rows * width,
        28 * rows * width + 12 * width * width + 32 * rows * rows,
        0,
        [pltpu.VMEM((rows, width), F32), pltpu.VMEM((keys, width), F32), pltpu.VMEM((rows, width), F32)]
        + [pltpu.VMEM((rows, width), BF16)]
        + [pltpu.VMEM((rows, group), BF16)] * 4
        + attend_scratch(rows, rows)
        + group_scratch(rows, rows, width, 3)
        + [pltpu.VMEM((2, keys, group), BF16)] * 2
        + [pltpu.VMEM((2, width, group), BF16)] * 2
        + [pltpu.SemaphoreType.DMA((13, 2))],
    )(grads, low, *cross_grads, weights, *saved)


def unpack_kernel(up_in, down_in, small_in, down_ref, up_ref, up_b_ref, gain_ref, shift_ref, down_b_ref):
    units = down_ref.shape[2]
    up_ref[...] = up_in[...].astype(F32)
    for at in range(down_ref.shape[0]):
        down_ref[at] = down_in[:, at * units : (at + 1) * units].astype(F32)

    @pl.when(pl.program_id(0) == 0)
    def _():
        small = small_in[...].astype(F32)
        per = up_b_ref.shape[1] // 128
        for at, ref in enumerate((up_b_ref, gain_ref, shift_ref, down_b_ref)):
            for part in range(ref.shape[1] // 128):
                row = at * per + part
                ref[:, part * 128 : (part + 1) * 128] = small[row : row + 1]


def unpack(grads, down_shape):
    width, units = down_shape
    halves = width // units
    steps = 4
    step = units // steps
    small = 4 * width // 128

    def fixed(shape):
        return pl.BlockSpec(shape, lambda i: (0, 0))

    down, *rest = call(
        unpack_kernel,
        "unpack",
        (steps,),
        [
            pl.BlockSpec((step, width), lambda i: (i, 0)),
            pl.BlockSpec((step, width), lambda i: (i + steps, 0)),
            pl.BlockSpec((small, 128), lambda i: (0, width // 128)),
        ],
        [
            pl.BlockSpec((halves, step, units), lambda i: (0, i, 0)),
            pl.BlockSpec((step, width), lambda i: (i, 0)),
        ]
        + [fixed((1, width))] * 3
        + [fixed((1, units))],
        [
            jax.ShapeDtypeStruct((halves, units, units), F32),
            jax.ShapeDtypeStruct((units, width), F32),
        ]
        + [jax.ShapeDtypeStruct((1, width), F32)] * 3
        + [jax.ShapeDtypeStruct((1, units), F32)],
        0,
        16 * width * units,
    )(grads, grads, grads)
    return down.reshape(down_shape), *rest


def gather(shard):
    return lax.all_gather(shard, "fsdp", axis=0, tiled=True)


def sum_over(part, axis):
    count = lax.axis_size(axis)
    total, travel = part.astype(F32), part
    for _ in range(count - 1):
        travel = lax.ppermute(travel, axis, [(at, (at + 1) % count) for at in range(count)])
        total = total + travel.astype(F32)
    return total.astype(part.dtype)


def local(
    inputs,
    encoder,
    grad_out,
    target_mask,
    source_lengths,
    step,
    attn_in,
    attn_out,
    ffn_in,
    ffn_in_bias,
    ffn_out,
    ffn_out_bias,
    attn_bias,
    norm_gain,
    norm_shift,
    adapter_down,
    adapter_down_bias,
    adapter_up,
    adapter_up_bias,
    adapter_gain,
    adapter_shift,
):
    sequences, row_count, width = inputs.shape
    held = attn_in.shape[0]
    groups = ffn_out.shape[0] // held
    wide = ffn_in.shape[1]
    pad = jnp.zeros((held, 128), BF16)
    attn_w = gather(jnp.concatenate([attn_in, attn_out, pad], 1))
    ffn_w = jnp.concatenate(
        [ffn_out[at * held : (at + 1) * held] for at in range(groups)] + [ffn_in, pad], 1
    )
    ffn_w = gather(ffn_w)
    w1_at, w2_at = wide, 0
    self_at, cross_at = (6, 0, 1, 2), (7, 3, 4, 5)

    ramp = (4.0 * step.astype(F32) / RAMP).reshape(1)
    bias = [attn_bias[at : at + 1] for at in range(6)]
    gain = [norm_gain[at : at + 1] for at in range(3)]
    shift = [norm_shift[at : at + 1] for at in range(3)]
    tokens, states = inputs.reshape(-1, width), encoder.reshape(-1, width)
    target_length = jnp.sum((target_mask > 0).astype(jnp.int32)).reshape(1)

    *self_saved, self_ctx, self_expo, self_inverse = self_forward(
        target_length, tokens, attn_w, bias[0], bias[1]
    )
    normal1, scale1, *cross_saved, cross_ctx, cross_expo, cross_inverse = cross_forward(
        source_lengths,
        tokens,
        self_ctx,
        states,
        attn_w,
        self_at[:1] + cross_at[1:],
        (bias[2], gain[0], shift[0], bias[3], bias[4]),
    )
    token_total = sequences * row_count * lax.axis_size("fsdp") * lax.axis_size("dp")
    normal2, hidden2, adapt_in, adapt_act, adapt_slope, base, scale2, scale_a = post_cross(
        ramp,
        normal1,
        cross_ctx,
        attn_w,
        cross_at[0],
        adapter_down,
        adapter_up,
        (bias[5], gain[0], shift[0], gain[1], shift[1], ffn_out_bias[None])
        + (adapter_gain[None], adapter_shift[None], adapter_up_bias[None]),
        adapter_down_bias[None],
    )
    slope, layer_out, grad_ffn, grad_rest, adapter_grads = middle(
        ramp,
        hidden2,
        ffn_w,
        w2_at,
        w1_at,
        ffn_in_bias[None],
        scale_a,
        (gain[2], shift[2], adapter_gain[None], adapter_shift[None]),
        (base, grad_out.reshape(-1, width), adapt_slope, adapter_up, adapt_act, adapter_down, adapt_in),
        held,
        1.0 / math.sqrt(token_total),
    )
    scattered = lax.psum_scatter(adapter_grads, "fsdp", scatter_dimension=0, tiled=True)
    grad_sum1, low_sum1, *cross_grads = ffn_cross_backward(
        grad_ffn,
        ffn_w,
        w2_at,
        w1_at,
        slope,
        grad_rest,
        normal2,
        scale2,
        gain[1],
        normal1,
        scale1,
        gain[0],
        attn_w,
        cross_at,
        (*cross_saved, cross_ctx, cross_expo, cross_inverse),
        held,
    )
    scattered, low_sum1 = lax.optimization_barrier((scattered, low_sum1))
    adapter_grads = gather(sum_over(scattered, "dp"))
    grad_input, grad_encoder = self_backward(
        grad_sum1,
        low_sum1,
        cross_grads,
        attn_w,
        self_at,
        cross_at,
        (*self_saved, self_ctx, self_expo, self_inverse),
    )
    grad_down, grad_up, up_bias, grad_gain, grad_shift, down_bias = unpack(
        adapter_grads, adapter_down.shape
    )
    return (
        layer_out.reshape(inputs.shape),
        grad_input.reshape(inputs.shape),
        grad_encoder.reshape(encoder.shape),
        grad_down,
        down_bias.reshape(-1),
        grad_up,
        up_bias.reshape(-1),
        grad_gain.reshape(-1),
        grad_shift.reshape(-1),
    )


def solution(mesh):
    batch = P(("fsdp", "dp"), None, None)
    split = P("fsdp", None)
    placed = (
        (batch,) * 3
        + (P(("fsdp", "dp"), None), P(("fsdp", "dp")), P())
        + (split, split, split, P(), split)
        + (P(),) * 10
    )
    return jax.shard_map(
        local,
        mesh=mesh,
        in_specs=placed,
        out_specs=(batch,) * 3 + (P(),) * 6,
        check_vma=False,
    )
```

```python
import functools
import math

import jax
import jax.numpy as jnp
from jax import lax
from jax.experimental import pallas as pl
from jax.experimental.pallas import tpu as pltpu
from jax.sharding import PartitionSpec as P

HEADS = 16
RAMP = 1000
EPS = 1e-05
F32 = jnp.float32
BF16 = jnp.bfloat16
VMEM_LIMIT = 58 * 2**20


def dot(left, right, left_dim, right_dim):
    return lax.dot_general(
        left, right, (((left_dim,), (right_dim,)), ((), ())), preferred_element_type=F32
    )


def call(kernel, name, grid, in_specs, out_specs, out_shape, flops, moved, exps=0, scratch=()):
    return pl.pallas_call(
        kernel,
        name=name,
        grid=grid,
        in_specs=in_specs,
        out_specs=out_specs,
        out_shape=out_shape,
        scratch_shapes=scratch,
        compiler_params=pltpu.CompilerParams(vmem_limit_bytes=VMEM_LIMIT),
        cost_estimate=pl.CostEstimate(
            flops=int(flops), bytes_accessed=int(moved), transcendentals=int(exps)
        ),
    )


def whole(shape):
    return pl.BlockSpec(shape, lambda *_: (0,) * len(shape), pipeline_mode=pl.Buffered(1))


def columns(rows, width, first=0):
    return pl.BlockSpec((rows, width), lambda i: (0, i + first))


def square(width, at):
    return pl.BlockSpec((width, width), lambda i: (0, at), pipeline_mode=pl.Buffered(1))


def normalize(values):
    center = values - jnp.mean(values, -1, keepdims=True)
    scale = lax.rsqrt(jnp.mean(center * center, -1, keepdims=True) + EPS)
    return center * scale, scale


def normalize_back(normal, scale, grad):
    return scale * (
        grad
        - jnp.mean(grad, -1, keepdims=True)
        - normal * jnp.mean(grad * normal, -1, keepdims=True)
    )


def split_three(values):
    high = values.astype(BF16).astype(F32)
    middle = (values - high).astype(BF16).astype(F32)
    return high, middle, values - high - middle


GROUP = 4
CHUNK = 256
SIZE = 64


def attend_forward(causal, ahead, q_ref, k_ref, v_ref, length, ctx_ref, expo_ref, inverse_ref):
    rows, keys = q_ref.shape[0], k_ref.shape[0]
    width = 2 * SIZE
    lane = lax.broadcasted_iota(jnp.int32, (rows, width), 1)
    key_lane = lax.broadcasted_iota(jnp.int32, (keys, width), 1)
    key_row = lax.broadcasted_iota(jnp.int32, (keys, width), 0)
    picks = jnp.where(lane % SIZE == 0, 1.0, 0.0).astype(BF16)
    extra = jnp.where(key_row < length, 0.0, -1e30).astype(BF16)
    one = jnp.asarray(1.0, BF16)
    left = lane[:CHUNK] < SIZE
    head_q, head_k, head_v = [], [], []
    for at in range(0, q_ref.shape[1], width):
        queries = q_ref[:, at : at + width]
        key_rows, value_rows = k_ref[:, at : at + width], v_ref[:, at : at + width]
        head_q += [jnp.where(lane < SIZE, queries, picks), jnp.where(lane < SIZE, picks, queries)]
        head_k += [
            jnp.where(key_lane < SIZE, key_rows, extra),
            jnp.where(key_lane < SIZE, extra, key_rows),
        ]
        head_v += [
            jnp.where(key_lane < SIZE, value_rows, one),
            jnp.where(key_lane < SIZE, one, value_rows),
        ]

    def scores(at, head):
        low, high = at * CHUNK, (at + 1) * CHUNK
        live = high if causal else keys
        found = dot(head_q[head][low:high], head_k[head][:live], 1, 1)
        if not causal:
            return found
        query_at = lax.broadcasted_iota(jnp.int32, (CHUNK, CHUNK), 0)
        key_at = lax.broadcasted_iota(jnp.int32, (CHUNK, CHUNK), 1)
        edge = jnp.where(key_at <= query_at, found[:, low:high], -1e30)
        return jnp.concatenate([found[:, :low], edge], 1) if low else edge

    done, waiting = {}, []

    def finish(at, head, found):
        low, high = at * CHUNK, (at + 1) * CHUNK
        live = found.shape[1]
        top = jnp.max(found, 1, keepdims=True)
        expo = jnp.exp(found - top).astype(BF16)
        expo_ref[head, low:high, :live] = expo
        done[head] = dot(expo, head_v[head][:live], 1, 0)
        if head % 2:
            first, second = done[head - 1], done[head]
            inverse = 1.0 / jnp.where(left, pltpu.roll(first, SIZE, 1), pltpu.roll(second, SIZE, 1))
            span = slice(head // 2 * width, (head // 2 + 1) * width)
            inverse_ref[low:high, span] = inverse
            ctx_ref[low:high, span] = (jnp.where(left, first, second) * inverse).astype(BF16)

    for pair in range(len(head_q) // 2):
        for at in range(rows // CHUNK):
            for head in (2 * pair, 2 * pair + 1):
                waiting.append((at, head, scores(at, head)))
                if len(waiting) > ahead:
                    finish(*waiting.pop(0))
    for unit in waiting:
        finish(*unit)


def attend_backward(
    causal, q_ref, k_ref, v_ref, ctx_ref, grad_ref, expo_ref, inverse_ref, dq_ref, dk_ref, dv_ref, s_scr,
    before, after,
):
    rows, keys = q_ref.shape[0], k_ref.shape[0]
    width = 2 * SIZE
    count = rows // CHUNK
    pairs = q_ref.shape[1] // width
    lane = lax.broadcasted_iota(jnp.int32, (rows, width), 1)
    key_lane = lax.broadcasted_iota(jnp.int32, (keys, width), 1)
    place, key_place = lane % SIZE, key_lane % SIZE
    ones = jnp.where((key_place >= 1) & (key_place <= 3), 1.0, 0.0).astype(BF16)
    from_lane = lax.broadcasted_iota(jnp.int32, (2 * width, width), 0) % width
    to_lane = lax.broadcasted_iota(jnp.int32, (2 * width, width), 1)
    swap = jnp.where((from_lane < SIZE) != (to_lane < SIZE), 1.0, 0.0).astype(BF16)

    def prepare(pair):
        span = slice(pair * width, (pair + 1) * width)
        value_rows = v_ref[:, span]
        grads = (grad_ref[:, span].astype(F32) * inverse_ref[:, span]).astype(BF16)
        products = grads.astype(F32) * ctx_ref[:, span].astype(F32)
        high = products.astype(BF16)
        low = (products - high.astype(F32)).astype(BF16)
        parts = split_three(-dot(jnp.concatenate([high, low], 1), swap, 1, 0))
        packed = jnp.zeros((rows, width), F32)
        for index, part in enumerate(parts):
            packed = jnp.where(place == index + 1, part, packed)
        packed = packed.astype(BF16)
        head_g = [jnp.where(lane < SIZE, grads, packed), jnp.where(lane < SIZE, packed, grads)]
        head_v = [
            jnp.where(key_lane < SIZE, value_rows, ones),
            jnp.where(key_lane < SIZE, ones, value_rows),
        ]
        return head_g, head_v, q_ref[:, span].T, grads.T

    def multiply(pair, head_g, head_v):
        span = slice(pair * width, (pair + 1) * width)
        key_rows = k_ref[:, span]
        grad_q, waiting = {}, []

        def finish(at, head, grad_p):
            low, high = at * CHUNK, (at + 1) * CHUNK
            live = grad_p.shape[1]
            expo = expo_ref[2 * pair + head, low:high, :live]
            grad_s = (expo.astype(F32) * grad_p).astype(BF16)
            s_scr[head, low:high, :live] = grad_s
            grad_q[head] = dot(grad_s, key_rows[:live], 1, 0)
            if head:
                both = jnp.where(lane[low:high] < SIZE, grad_q[0], grad_q[1])
                dq_ref[low:high, span] = (both * SIZE**-0.5).astype(BF16)

        for at in range(count):
            for head in range(2):
                low, high = at * CHUNK, (at + 1) * CHUNK
                live = high if causal else keys
                waiting.append((at, head, dot(head_g[head][low:high], head_v[head][:live], 1, 1)))
                if len(waiting) > 1:
                    finish(*waiting.pop(0))
        for unit in waiting:
            finish(*unit)

    def collect(pair, queries_t, grads_t):
        span = slice(pair * width, (pair + 1) * width)
        step = CHUNK if causal else keys
        for source, saved, first, to in (
            (grads_t, expo_ref, 2 * pair, dv_ref),
            (queries_t, s_scr, 0, dk_ref),
        ):
            for low in range(0, keys, step):
                start = low if causal else 0
                parts = [
                    dot(
                        source[head * SIZE : (head + 1) * SIZE, start:],
                        saved[first + head, start:, low : low + step],
                        1,
                        0,
                    )
                    for head in range(2)
                ]
                to[low : low + step, span] = jnp.concatenate(parts, 0).T.astype(BF16)

    ready = prepare(0)
    for pair in range(pairs):
        head_g, head_v, queries_t, grads_t = ready
        before(pair)
        multiply(pair, head_g, head_v)
        more = pair + 1 < pairs
        if causal and more:
            ready = prepare(pair + 1)
        collect(pair, queries_t, grads_t)
        if more and not causal:
            ready = prepare(pair + 1)
        after(pair)


def parts_of(rows):
    return [slice(at, at + CHUNK) for at in range(0, rows, CHUNK)]


def wide_scale(scale):
    return jnp.broadcast_to(scale, (scale.shape[0], 128))


def self_forward_kernel(
    length_ref, x_ref, wq_ref, wk_ref, wv_ref, bq_ref, bv_ref,
    q_ref, k_ref, v_ref, ctx_ref, expo_ref, inverse_ref,
):
    scale = jnp.asarray(SIZE**-0.5, BF16)
    for span in parts_of(x_ref.shape[0]):
        rows = x_ref[span]
        q_ref[span] = (dot(rows, wq_ref[...], 1, 0) + bq_ref[...]).astype(BF16) * scale
        k_ref[span] = dot(rows, wk_ref[...], 1, 0).astype(BF16)
        v_ref[span] = (dot(rows, wv_ref[...], 1, 0) + bv_ref[...]).astype(BF16)
    attend_forward(
        True, 2, q_ref, k_ref, v_ref, length_ref[0], ctx_ref, expo_ref, inverse_ref
    )


def anywhere():
    return pl.BlockSpec(memory_space=pl.ANY)


def scalar():
    return pl.BlockSpec(memory_space=pltpu.SMEM)


def attend_out(rows, keys, width):
    group = GROUP * SIZE
    heads = width // SIZE
    specs = (
        [columns(rows, group)]
        + [columns(keys, group)] * 2
        + [columns(rows, group)]
        + [pl.BlockSpec((GROUP, rows, keys), lambda i: (i, 0, 0)), columns(rows, group)]
    )
    shapes = (
        [jax.ShapeDtypeStruct((rows, width), BF16)]
        + [jax.ShapeDtypeStruct((keys, width), BF16)] * 2
        + [jax.ShapeDtypeStruct((rows, width), BF16)]
        + [
            jax.ShapeDtypeStruct((heads, rows, keys), BF16),
            jax.ShapeDtypeStruct((rows, width), F32),
        ]
    )
    return specs, shapes


def self_forward(length, values, weights, q_bias, v_bias):
    rows, width = values.shape
    group = GROUP * SIZE
    per = width // group
    specs, shapes = attend_out(rows, rows, width)
    return call(
        self_forward_kernel,
        "self_forward",
        (per,),
        [scalar(), whole((rows, width))]
        + [columns(width, group, at * per) for at in range(3)]
        + [columns(1, group)] * 2,
        specs,
        shapes,
        6 * rows * width * width + 4 * rows * rows * width,
        18 * rows * width + 6 * width * width + 32 * rows * rows,
        rows * rows * HEADS,
    )(length, values, weights, weights, weights, q_bias, v_bias)


def cross_forward_kernel(
    length_ref, x_ref, sctx_ref, states_ref, wo_ref, wq_ref, wk_ref, wv_ref,
    bo_ref, gain_ref, shift_ref, bq_ref, bv_ref,
    normal_ref, scale_ref, q_ref, k_ref, v_ref, ctx_ref, expo_ref, inverse_ref, hidden_scr,
):
    spans = parts_of(x_ref.shape[0])

    @pl.when(pl.program_id(0) == 0)
    def _():
        sums = [
            x_ref[span].astype(F32) + dot(sctx_ref[span], wo_ref[...], 1, 0) + bo_ref[...]
            for span in spans
        ]
        for span, total in zip(spans, sums):
            normal, scale = normalize(total)
            normal_ref[span] = normal
            scale_ref[span] = wide_scale(scale)
            hidden_scr[span] = (normal * gain_ref[...] + shift_ref[...]).astype(BF16)

    size = jnp.asarray(SIZE**-0.5, BF16)
    for span in parts_of(states_ref.shape[0]):
        rows = states_ref[span]
        k_ref[span] = dot(rows, wk_ref[...], 1, 0).astype(BF16)
        v_ref[span] = (dot(rows, wv_ref[...], 1, 0) + bv_ref[...]).astype(BF16)
    for span in spans:
        q_ref[span] = (dot(hidden_scr[span], wq_ref[...], 1, 0) + bq_ref[...]).astype(BF16) * size
    attend_forward(
        False, 2, q_ref, k_ref, v_ref, length_ref[0], ctx_ref, expo_ref, inverse_ref
    )


def cross_forward(length, values, context, states, weights, at, vectors):
    rows, width = values.shape
    keys = states.shape[0]
    group = GROUP * SIZE
    per = width // group
    specs, shapes = attend_out(rows, keys, width)
    return call(
        cross_forward_kernel,
        "cross_forward",
        (per,),
        [scalar(), whole((rows, width)), whole((rows, width)), whole((keys, width))]
        + [square(width, at[0])]
        + [columns(width, group, first * per) for first in at[1:]]
        + [whole((1, width))] * 3
        + [columns(1, group)] * 2,
        [whole((rows, width)), whole((rows, 128))] + specs,
        [jax.ShapeDtypeStruct((rows, width), F32), jax.ShapeDtypeStruct((rows, 128), F32)] + shapes,
        8 * rows * width * width + 4 * rows * keys * width,
        26 * rows * width + 8 * width * width + 32 * rows * keys,
        rows * keys * HEADS,
        [pltpu.VMEM((rows, width), BF16)],
    )(length, values, context, states, weights, weights, weights, weights, *vectors)


FFN_STEP = 1024
FFN_BACK_STEP = 512


def second_block(w_ref, held, width):
    pieces = []
    for at in range(0, w_ref.shape[0], held):
        for group in range(w_ref.shape[1] // width):
            pieces.append(w_ref[at : at + held, group * width : (group + 1) * width])
    return jnp.concatenate(pieces, 0)


def in_turn(units, finish):
    waiting = None
    for first, span in units:
        value = first(span)
        if waiting is not None:
            finish(*waiting)
        waiting = (span, value)
    finish(*waiting)


def post_cross_kernel(
    ramp_ref, n1_ref, ctx_ref, wo_ref, down_ref, up_ref,
    bo_ref, gain1_ref, shift1_ref, gain2_ref, shift2_ref, b2_ref, gain_a_ref, shift_a_ref, up_b_ref,
    down_b_ref,
    normal_ref, hidden_ref, in_ref, act_ref, slope_ref, base_ref, scale_ref, scale_a_ref,
):
    spans = parts_of(n1_ref.shape[0])
    sums = [dot(ctx_ref[span], wo_ref[...], 1, 0) + bo_ref[...] for span in spans]
    for span, total in zip(spans, sums):
        normal, scale = normalize(total + (n1_ref[span] * gain1_ref[...] + shift1_ref[...]))
        normal_ref[span] = normal
        hidden = normal * gain2_ref[...] + shift2_ref[...]
        hidden_ref[span] = hidden.astype(BF16)
        base_ref[span] = hidden + b2_ref[...] + ramp_ref[0] * up_b_ref[...]
        normal_a, scale_a = normalize(hidden)
        in_ref[span] = (normal_a * gain_a_ref[...] + shift_a_ref[...]).astype(BF16)
        scale_ref[span] = wide_scale(scale)
        scale_a_ref[span] = wide_scale(scale_a)
    for span in spans:
        lower = dot(in_ref[span], down_ref[...], 1, 0) + down_b_ref[...]
        gate = 1.0 / (1.0 + jnp.exp(-lower))
        act_ref[span] = (lower * gate).astype(BF16)
        slope_ref[span] = (gate * (1.0 + lower * (1.0 - gate))).astype(BF16)
    for span in spans:
        base_ref[span] += ramp_ref[0] * dot(act_ref[span], up_ref[...], 1, 0)


def post_cross(ramp, normal1, context, weights, wo_at, down, up, vectors, down_bias):
    rows, width = normal1.shape
    units = down.shape[1]
    step = 512

    def block(wide):
        return pl.BlockSpec((step, wide), lambda i: (i, 0))

    return call(
        post_cross_kernel,
        "post_cross",
        (rows // step,),
        [scalar(), block(width), block(width), square(width, wo_at), whole(down.shape), whole(up.shape)]
        + [whole((1, width))] * 9
        + [whole((1, units))],
        [block(width)] * 3 + [block(units)] * 2 + [block(width)] + [block(128)] * 2,
        [
            jax.ShapeDtypeStruct((rows, width), F32),
            jax.ShapeDtypeStruct((rows, width), BF16),
            jax.ShapeDtypeStruct((rows, width), BF16),
            jax.ShapeDtypeStruct((rows, units), BF16),
            jax.ShapeDtypeStruct((rows, units), BF16),
            jax.ShapeDtypeStruct((rows, width), F32),
            jax.ShapeDtypeStruct((rows, 128), F32),
            jax.ShapeDtypeStruct((rows, 128), F32),
        ],
        2 * rows * width * width + 4 * rows * width * units,
        22 * rows * width,
        rows * units,
    )(ramp, normal1, context, weights, down, up, *vectors, down_bias)


def middle_kernel(
    held, factor, ramp_ref, hidden_ref, w1_ref, w2_ref, b1_ref, scale_a_ref,
    gain3_ref, shift3_ref, gain_a_ref, shift_a_ref,
    base_in, go_in, slope_in, up_in, act_in, down_in, in_in,
    slope_ref, out_out, gffn_out, rest_out, grads_out,
    base_scr, go_scr, slope_scr, up_scr, act_scr, down_scr, in_scr,
    total_scr, out_scr, gffn_scr, branch_scr, lower_scr, grads_scr, in_sems, out_sems,
):
    rows, width = hidden_ref.shape
    units = down_in.shape[1]
    spans = parts_of(rows)
    step = pl.program_id(0)
    loads = moved(
        [
            (base_in, base_scr), (go_in, go_scr), (slope_in, slope_scr), (up_in, up_scr),
            (act_in, act_scr), (down_in, down_scr), (in_in, in_scr),
        ],
        in_sems,
    )

    @pl.when(step == 0)
    def _():
        total_scr[...] = jnp.zeros_like(total_scr)

    for at, part in enumerate((loads[:1], loads[1:4], loads[4:])):
        pl.when(step == at + 1)(functools.partial(start_all, part))

    def first(span):
        return dot(hidden_ref[span], w1_ref[...], 1, 0) + b1_ref[...]

    def finish(span, pre):
        phi = 0.5 + 0.5 * lax.erf(pre * (0.5**0.5))
        act = (pre * phi).astype(BF16)
        slope = phi + pre * (jnp.exp(pre * pre * -0.5) * (1.0 / math.sqrt(2.0 * math.pi)))
        slope_ref[span] = slope.astype(BF16)
        total_scr[span] += dot(act, second_block(w2_ref, held, width), 1, 0)

    in_turn([(first, span) for span in spans], finish)

    @pl.when(step == pl.num_programs(0) - 1)
    def _():
        ramp = ramp_ref[0]
        wait_all(loads[:4])
        main, beside = pl.ds(0, width), pl.ds(width, 128)
        outs = moved(
            [
                (out_scr, out_out),
                (gffn_scr, gffn_out),
                (grads_scr.at[:, main], grads_out.at[:, main]),
            ],
            out_sems,
        )
        kind = grads_scr.dtype
        sums = [jnp.zeros((1, width), F32)] * 3 + [jnp.zeros((1, units), F32)]

        def norm_three(span):
            normal, scale = normalize(total_scr[span] + base_scr[span])
            out_scr[span] = (normal * gain3_ref[...] + shift3_ref[...]).astype(BF16)
            grad = normalize_back(normal, scale, gain3_ref[...] * go_scr[span].astype(F32))
            gffn_scr[span] = grad.astype(BF16)
            total_scr[span] = grad
            grad_branch = (ramp * grad).astype(BF16)
            branch_scr[span] = grad_branch
            sums[0] = sums[0] + jnp.sum(grad_branch.astype(F32), 0, keepdims=True)

        def adapter_back(span):
            grad_act = dot(branch_scr[span], up_scr[...], 1, 1).astype(BF16).astype(F32)
            grad_lower = (slope_scr[span].astype(F32) * grad_act).astype(BF16)
            lower_scr[span] = grad_lower
            sums[3] = sums[3] + jnp.sum(grad_lower.astype(F32), 0, keepdims=True)

        for span in spans:
            norm_three(span)
            adapter_back(span)
        start_all(outs[:2])
        wait_all(loads[4:])
        grads_scr[0:units, 0:width] = (dot(act_scr[...], branch_scr[...], 0, 0) * factor).astype(kind)
        for at, span in enumerate(spans):
            grad_adapt = dot(lower_scr[span], down_scr[...], 1, 1)
            normal_a = (in_scr[span].astype(F32) - shift_a_ref[...]) * (1.0 / gain_a_ref[...])
            scale_a = scale_a_ref[span, 0:1]
            total_scr[span] += normalize_back(normal_a, scale_a, gain_a_ref[...] * grad_adapt)
            outs.append(
                pltpu.make_async_copy(total_scr.at[span], rest_out.at[span], out_sems.at[3 + at])
            )
            outs[-1].start()
            sums[1] = sums[1] + jnp.sum(grad_adapt * normal_a, 0, keepdims=True)
            sums[2] = sums[2] + jnp.sum(grad_adapt, 0, keepdims=True)
        for at in range(0, width, units):
            grads_scr[units : 2 * units, at : at + units] = (
                dot(in_scr[:, at : at + units], lower_scr[...], 0, 0) * factor
            ).astype(kind)
        outs[2].start()
        vectors = []
        for row in sums:
            row = row * factor
            vectors += [row[:, low : low + 128] for low in range(0, row.shape[1], 128)]
        vectors += [jnp.zeros((1, 128), F32)] * (4 * width // 128 - len(vectors))
        small = jnp.concatenate(vectors, 0).astype(kind)
        lines = small.shape[0]
        grads_scr[0:lines, width:] = small
        grads_scr[lines:, width:] = jnp.zeros((2 * units - lines, 128), kind)
        outs.append(
            pltpu.make_async_copy(
                grads_scr.at[:, beside], grads_out.at[:, beside], out_sems.at[3 + len(spans)]
            )
        )
        outs[-1].start()
        wait_all(outs)


def middle(
    ramp, hidden, ffn_w, w2_at, w1_at, first_bias, scale_a, vectors, late, held, factor
):
    rows, width = hidden.shape
    wide = first_bias.shape[1]
    units = late[2].shape[1]
    step = FFN_STEP
    groups = wide // width
    return call(
        functools.partial(middle_kernel, held, factor),
        "middle",
        (wide // step,),
        [
            scalar(),
            whole((rows, width)),
            columns(width, step, w1_at // step),
            pl.BlockSpec((step // groups, wide), lambda i: (i, w2_at // wide)),
            columns(1, step),
            whole((rows, 128)),
        ]
        + [whole((1, width))] * 4
        + [anywhere()] * len(late),
        [columns(rows, step)] + [anywhere()] * 4,
        [
            jax.ShapeDtypeStruct((rows, wide), BF16),
            jax.ShapeDtypeStruct((rows, width), BF16),
            jax.ShapeDtypeStruct((rows, width), BF16),
            jax.ShapeDtypeStruct((rows, width), F32),
            jax.ShapeDtypeStruct((2 * units, width + 128), BF16),
        ],
        4 * rows * width * wide + 8 * rows * width * units,
        22 * rows * width + 4 * width * wide + 2 * rows * wide + 12 * width * units,
        2 * rows * wide,
        [pltpu.VMEM(value.shape, value.dtype) for value in late]
        + [
            pltpu.VMEM((rows, width), F32),
            pltpu.VMEM((rows, width), BF16),
            pltpu.VMEM((rows, width), BF16),
            pltpu.VMEM((rows, width), BF16),
            pltpu.VMEM((rows, units), BF16),
            pltpu.VMEM((2 * units, width + 128), BF16),
            pltpu.SemaphoreType.DMA((len(late),)),
            pltpu.SemaphoreType.DMA((4 + rows // CHUNK,)),
        ],
    )(ramp, hidden, ffn_w, ffn_w, first_bias, scale_a, *vectors, *late)


def moved(pairs, sems):
    return [
        pltpu.make_async_copy(source, target, sems.at[at])
        for at, (source, target) in enumerate(pairs)
    ]


def start_all(copies):
    for copy in copies:
        copy.start()


def wait_all(copies):
    for copy in copies:
        copy.wait()


def expo_loads(expo_ref, expo_scr, sems, group, count):
    def load(which, pair):
        heads = pl.ds(which * GROUP + 2 * pair, 2)
        return pltpu.make_async_copy(
            expo_ref.at[heads], expo_scr.at[pl.ds(2 * pair, 2)], sems.at[pair]
        )

    def begin():
        for pair in range(GROUP // 2):
            load(0, pair).start()

    def before(pair):
        load(group, pair).wait()

    def after(pair):
        @pl.when(group < count - 1)
        def _():
            load(group + 1, pair).start()

    return begin, before, after


def group_loads(pairs, sems):
    def copies(group, part):
        slot = lax.rem(group, 2)
        return [
            pltpu.make_async_copy(source(group), target.at[slot], sems.at[at, slot])
            for at, (source, target) in list(enumerate(pairs))[part]
        ]

    def start(group):
        start_all(copies(group, slice(None)))

    def wait(group, part):
        wait_all(copies(group, part))

    return start, wait


def column_group(ref, first=0):
    width = GROUP * SIZE
    return lambda group: ref.at[:, pl.ds(pl.multiple_of(group * width, width) + first, width)]


def row_group(ref, first, width):
    depth = GROUP * SIZE
    return lambda group: ref.at[
        pl.ds(pl.multiple_of(group * depth, depth), depth), pl.ds(first, width)
    ]


def ffn_cross_backward_kernel(
    held, ffn_steps, at,
    g_ref, w1_ref, w2_ref, slope_ref, start_ref, normal2_ref, scale2_ref, gain2_ref,
    normal1_ref, scale1_ref, gain1_ref, attn_ref, q_ref, k_ref, v_ref, ctx_ref, expo_ref, inverse_ref,
    sum_ref, sum_low_ref, dk_ref, dv_ref,
    total_scr, start_scr, normal_scr, low_scr, grad_scr, dq_scr, s_scr, expo_scr,
    in_sems, out_sems, expo_sems,
    wo_scr, wq_scr, q_scr, k_scr, v_scr, ctx_scr, inverse_scr, group_sems,
):
    rows, width = g_ref.shape
    spans = parts_of(rows)
    step, steps = pl.program_id(0), pl.num_programs(0)
    loads = moved([(start_ref, start_scr), (normal2_ref, normal_scr)], in_sems)
    late = pltpu.make_async_copy(normal1_ref, normal_scr, in_sems.at[2])
    group, groups = step - ffn_steps, steps - ffn_steps
    begin, before, after = expo_loads(expo_ref, expo_scr, expo_sems, group, groups)
    start_group, wait_group = group_loads(
        [
            (row_group(attn_ref, at[0] * width, width), wo_scr),
            (column_group(q_ref), q_scr),
            (column_group(k_ref), k_scr),
            (column_group(v_ref), v_scr),
            (column_group(ctx_ref), ctx_scr),
            (column_group(inverse_ref), inverse_scr),
            (column_group(attn_ref, at[1] * width), wq_scr),
        ],
        group_sems,
    )

    @pl.when(step == 0)
    def _():
        total_scr[...] = jnp.zeros_like(total_scr)

    pl.when(step == 1)(loads[0].start)
    pl.when(step == ffn_steps // 2)(loads[1].start)
    pl.when(step == ffn_steps - 2)(functools.partial(start_group, 0))

    def first(span):
        return dot(g_ref[span], second_block(w2_ref, held, width), 1, 1)

    def finish(span, grad_act):
        grad_pre = (slope_ref[span].astype(F32) * grad_act).astype(BF16)
        total_scr[span] += dot(grad_pre, w1_ref[...], 1, 1)

    @pl.when(step < ffn_steps - 1)
    def _():
        in_turn([(first, span) for span in spans], finish)

    @pl.when(step == ffn_steps - 1)
    def _():
        begin()
        wait_all(loads)

        def back(span):
            grad = normalize_back(
                normal_scr[span],
                scale2_ref[span, 0:1],
                gain2_ref[...] * (total_scr[span] + start_scr[span]),
            )
            total_scr[span] = grad
            low_scr[span] = grad.astype(BF16)

        held_act, done = None, []
        for span in [*spans, None]:
            grad_act = first(span) if span is not None else None
            if held_act is not None:
                finish(*held_act)
                done.append(held_act[0])
            held_act = (span, grad_act)
            if len(done) > 1:
                back(done.pop(0))
        back(done.pop(0))
        late.start()

    slot = lax.rem(step, 2) if ffn_steps % 2 == 0 else lax.rem(step + 1, 2)

    def add(span):
        total_scr[span] += dot(dq_scr[span], wq_scr[slot], 1, 1)

    @pl.when(step == ffn_steps)
    def _():
        dq_scr[...] = jnp.zeros_like(dq_scr)

    @pl.when(step >= ffn_steps)
    def _():
        wait_group(group, slice(None))
        for span in spans:
            grad_scr[span] = dot(low_scr[span], wo_scr[slot], 1, 1).astype(BF16)
        last_slot = jnp.where(group > 0, 1 - slot, slot)
        for span in spans:
            total_scr[span] += dot(dq_scr[span], wq_scr[last_slot], 1, 1)
        pl.when(group < groups - 1)(functools.partial(start_group, group + 1))
        attend_backward(
            False, q_scr.at[slot], k_scr.at[slot], v_scr.at[slot], ctx_scr.at[slot], grad_scr, expo_scr,
            inverse_scr.at[slot], dq_scr, dk_ref, dv_ref, s_scr, before, after,
        )

    last = step == steps - 1

    @pl.when(last)
    def _():
        late.wait()
        outs = []

        def back(span):
            grad = normalize_back(
                normal_scr[span], scale1_ref[span, 0:1], gain1_ref[...] * total_scr[span]
            )
            total_scr[span] = grad
            low_scr[span] = grad.astype(BF16)
            copies = moved(
                [(total_scr.at[span], sum_ref.at[span]), (low_scr.at[span], sum_low_ref.at[span])],
                out_sems.at[pl.ds(len(outs), 2)],
            )
            start_all(copies)
            outs.extend(copies)

        add(spans[0])
        for before_span, span in zip(spans, spans[1:]):
            add(span)
            back(before_span)
        back(spans[-1])
        wait_all(outs)


def self_backward_kernel(
    at, cross_at,
    g_ref, low_ref, cdk_ref, cdv_ref, attn_ref, q_ref, k_ref, v_ref, ctx_ref, expo_ref, inverse_ref,
    out_ref, states_ref,
    total_scr, states_scr, start_scr, low_scr, grad_scr, dq_scr, dk_scr, dv_scr, s_scr, expo_scr,
    in_sems, out_sems, expo_sems,
    wo_scr, wq_scr, wk_scr, wv_scr, q_scr, k_scr, v_scr, ctx_scr, inverse_scr,
    cdk_scr, cdv_scr, cwk_scr, cwv_scr, group_sems,
):
    width = low_ref.shape[1]
    spans = parts_of(low_ref.shape[0])
    step, steps = pl.program_id(0), pl.num_programs(0)
    slot = lax.rem(step, 2)
    load, low_load = moved([(g_ref, start_scr), (low_ref, low_scr)], in_sems)
    begin, before, after = expo_loads(expo_ref, expo_scr, expo_sems, step, steps)
    start_group, wait_group = group_loads(
        [
            (row_group(attn_ref, at[0] * width, width), wo_scr),
            (column_group(cdk_ref), cdk_scr),
            (column_group(attn_ref, cross_at[2] * width), cwk_scr),
            (column_group(cdv_ref), cdv_scr),
            (column_group(attn_ref, cross_at[3] * width), cwv_scr),
            (column_group(q_ref), q_scr),
            (column_group(k_ref), k_scr),
            (column_group(v_ref), v_scr),
            (column_group(ctx_ref), ctx_scr),
            (column_group(inverse_ref), inverse_scr),
            (column_group(attn_ref, at[1] * width), wq_scr),
            (column_group(attn_ref, at[2] * width), wk_scr),
            (column_group(attn_ref, at[3] * width), wv_scr),
        ],
        group_sems,
    )

    @pl.when(step == 0)
    def _():
        low_load.start()
        start_group(0)
        begin()
        total_scr[...] = jnp.zeros_like(total_scr)
        states_scr[...] = jnp.zeros_like(states_scr)

    pl.when(step == 1)(load.start)

    pl.when(step == 0)(low_load.wait)
    wait_group(step, slice(None))
    pl.when(step < steps - 1)(functools.partial(start_group, step + 1))
    for span in spans:
        grad_scr[span] = dot(low_scr[span], wo_scr[slot], 1, 1).astype(BF16)
    for span in parts_of(states_scr.shape[0]):
        states_scr[span] += dot(cdk_scr[slot, span], cwk_scr[slot], 1, 1) + dot(
            cdv_scr[slot, span], cwv_scr[slot], 1, 1
        )
    attend_backward(
        True, q_scr.at[slot], k_scr.at[slot], v_scr.at[slot], ctx_scr.at[slot], grad_scr, expo_scr,
        inverse_scr.at[slot], dq_scr, dk_scr, dv_scr, s_scr, before, after,
    )

    def back(span):
        return (
            dot(dq_scr[span], wq_scr[slot], 1, 1)
            + dot(dk_scr[span], wk_scr[slot], 1, 1)
            + dot(dv_scr[span], wv_scr[slot], 1, 1)
        )

    last = step == steps - 1

    @pl.when(jnp.logical_not(last))
    def _():
        for span in spans:
            total_scr[span] += back(span)

    @pl.when(last)
    def _():
        load.wait()
        outs = [pltpu.make_async_copy(states_scr, states_ref, out_sems.at[len(spans)])]
        outs[0].start()
        for index, span in enumerate(spans):
            total_scr[span] += start_scr[span] + back(span)
            outs.append(
                pltpu.make_async_copy(total_scr.at[span], out_ref.at[span], out_sems.at[index])
            )
            outs[-1].start()
        wait_all(outs)


def attend_scratch(rows, keys):
    return [
        pltpu.VMEM((2, rows, keys), BF16),
        pltpu.VMEM((GROUP, rows, keys), BF16),
        pltpu.SemaphoreType.DMA((3,)),
        pltpu.SemaphoreType.DMA((2 * rows // CHUNK,)),
        pltpu.SemaphoreType.DMA((GROUP // 2,)),
    ]


def group_scratch(rows, keys, width, weights):
    group = GROUP * SIZE
    return (
        [pltpu.VMEM((2, group, width), BF16)]
        + [pltpu.VMEM((2, width, group), BF16)] * weights
        + [pltpu.VMEM((2, rows, group), BF16)]
        + [pltpu.VMEM((2, keys, group), BF16)] * 2
        + [pltpu.VMEM((2, rows, group), BF16), pltpu.VMEM((2, rows, group), F32)]
    )


def ffn_cross_backward(
    grads, ffn_w, w2_at, w1_at, slope, start, normal2, scale2, gain2, normal1, scale1, gain1, attn_w, at, saved,
    held,
):
    rows, width = grads.shape
    keys = saved[1].shape[0]
    wide = slope.shape[1]
    groups = wide // width
    block = FFN_BACK_STEP
    steps = wide // block
    group = GROUP * SIZE

    def unit(i):
        return jnp.minimum(i, steps - 1)

    def out(i):
        return (0, jnp.maximum(i - steps, 0))

    return call(
        functools.partial(ffn_cross_backward_kernel, held, steps, at),
        "ffn_cross_backward",
        (steps + width // group,),
        [
            whole((rows, width)),
            pl.BlockSpec((width, block), lambda i: (0, unit(i) + w1_at // block)),
            pl.BlockSpec((block // groups, wide), lambda i: (unit(i), w2_at // wide)),
            pl.BlockSpec((rows, block), lambda i: (0, unit(i))),
            anywhere(),
            anywhere(),
            whole((rows, 128)),
            whole((1, width)),
            anywhere(),
            whole((rows, 128)),
            whole((1, width)),
        ]
        + [anywhere()] * 7,
        [anywhere()] * 2 + [pl.BlockSpec((keys, group), out)] * 2,
        [
            jax.ShapeDtypeStruct((rows, width), F32),
            jax.ShapeDtypeStruct((rows, width), BF16),
            jax.ShapeDtypeStruct((keys, width), BF16),
            jax.ShapeDtypeStruct((keys, width), BF16),
        ],
        4 * rows * width * (width + wide) + 8 * rows * keys * width,
        48 * rows * width + 4 * width * (width + wide) + 2 * rows * wide + 32 * rows * keys,
        0,
        [pltpu.VMEM((rows, width), F32)] * 3
        + [pltpu.VMEM((rows, width), BF16)]
        + [pltpu.VMEM((rows, group), BF16)] * 2
        + attend_scratch(rows, keys)
        + group_scratch(rows, keys, width, 1)
        + [pltpu.SemaphoreType.DMA((7, 2))],
    )(
        grads, ffn_w, ffn_w, slope, start, normal2, scale2, gain2, normal1, scale1, gain1, attn_w, *saved
    )


def self_backward(grads, low, cross_grads, weights, at, cross_at, saved):
    rows, width = grads.shape
    keys = cross_grads[0].shape[0]
    group = GROUP * SIZE
    return call(
        functools.partial(self_backward_kernel, at, cross_at),
        "self_backward",
        (width // group,),
        [anywhere()] * 11,
        [anywhere()] * 2,
        [jax.ShapeDtypeStruct((rows, width), F32), jax.ShapeDtypeStruct((keys, width), F32)],
        8 * rows * width * width + 4 * keys * width * width + 4 * rows * rows * width,
        28 * rows * width + 12 * width * width + 32 * rows * rows,
        0,
        [pltpu.VMEM((rows, width), F32), pltpu.VMEM((keys, width), F32), pltpu.VMEM((rows, width), F32)]
        + [pltpu.VMEM((rows, width), BF16)]
        + [pltpu.VMEM((rows, group), BF16)] * 4
        + attend_scratch(rows, rows)
        + group_scratch(rows, rows, width, 3)
        + [pltpu.VMEM((2, keys, group), BF16)] * 2
        + [pltpu.VMEM((2, width, group), BF16)] * 2
        + [pltpu.SemaphoreType.DMA((13, 2))],
    )(grads, low, *cross_grads, weights, *saved)


def unpack_kernel(up_in, down_in, small_in, down_ref, up_ref, up_b_ref, gain_ref, shift_ref, down_b_ref):
    units = down_ref.shape[2]
    up_ref[...] = up_in[...].astype(F32)
    for at in range(down_ref.shape[0]):
        down_ref[at] = down_in[:, at * units : (at + 1) * units].astype(F32)

    @pl.when(pl.program_id(0) == 0)
    def _():
        small = small_in[...].astype(F32)
        per = up_b_ref.shape[1] // 128
        for at, ref in enumerate((up_b_ref, gain_ref, shift_ref, down_b_ref)):
            for part in range(ref.shape[1] // 128):
                row = at * per + part
                ref[:, part * 128 : (part + 1) * 128] = small[row : row + 1]


def unpack(grads, down_shape):
    width, units = down_shape
    halves = width // units
    steps = 2
    step = units // steps
    small = 4 * width // 128

    def fixed(shape):
        return pl.BlockSpec(shape, lambda i: (0, 0))

    down, *rest = call(
        unpack_kernel,
        "unpack",
        (steps,),
        [
            pl.BlockSpec((step, width), lambda i: (i, 0)),
            pl.BlockSpec((step, width), lambda i: (i + steps, 0)),
            pl.BlockSpec((small, 128), lambda i: (0, width // 128)),
        ],
        [
            pl.BlockSpec((halves, step, units), lambda i: (0, i, 0)),
            pl.BlockSpec((step, width), lambda i: (i, 0)),
        ]
        + [fixed((1, width))] * 3
        + [fixed((1, units))],
        [
            jax.ShapeDtypeStruct((halves, units, units), F32),
            jax.ShapeDtypeStruct((units, width), F32),
        ]
        + [jax.ShapeDtypeStruct((1, width), F32)] * 3
        + [jax.ShapeDtypeStruct((1, units), F32)],
        0,
        16 * width * units,
    )(grads, grads, grads)
    return down.reshape(down_shape), *rest


def join_kernel(first_ref, second_ref, out_ref, held_scr, in_sems, out_sems):
    rows = first_ref.shape[0]
    wide, more = first_ref.shape[1], second_ref.shape[1]
    parts = [pl.ds(at, rows // 2) for at in range(0, rows, rows // 2)]
    loads = []
    for at, part in enumerate(parts):
        loads.append(
            moved(
                [
                    (first_ref.at[part], held_scr.at[part, pl.ds(0, wide)]),
                    (second_ref.at[part], held_scr.at[part, pl.ds(wide, more)]),
                ],
                in_sems.at[at],
            )
        )
        start_all(loads[-1])
    held_scr[:, wide + more :] = jnp.zeros((rows, held_scr.shape[1] - wide - more), BF16)
    outs = moved([(held_scr.at[part], out_ref.at[part]) for part in parts], out_sems)
    for load, out in zip(loads, outs):
        wait_all(load)
        out.start()
    wait_all(outs)


def join(first, second, spare):
    rows = first.shape[0]
    shape = (rows, first.shape[1] + second.shape[1] + spare)
    return call(
        join_kernel,
        "join",
        (),
        [anywhere()] * 2,
        anywhere(),
        jax.ShapeDtypeStruct(shape, BF16),
        0,
        4 * rows * shape[1],
        0,
        [
            pltpu.VMEM(shape, BF16),
            pltpu.SemaphoreType.DMA((2, 2)),
            pltpu.SemaphoreType.DMA((2,)),
        ],
    )(first, second)


def gather(shard):
    return lax.all_gather(shard, "fsdp", axis=0, tiled=True)


def sum_over(part, axis):
    count = lax.axis_size(axis)
    total, travel = part.astype(F32), part
    for _ in range(count - 1):
        travel = lax.ppermute(travel, axis, [(at, (at + 1) % count) for at in range(count)])
        total = total + travel.astype(F32)
    return total.astype(part.dtype)


def local(
    inputs,
    encoder,
    grad_out,
    target_mask,
    source_lengths,
    step,
    attn_in,
    attn_out,
    ffn_in,
    ffn_in_bias,
    ffn_out,
    ffn_out_bias,
    attn_bias,
    norm_gain,
    norm_shift,
    adapter_down,
    adapter_down_bias,
    adapter_up,
    adapter_up_bias,
    adapter_gain,
    adapter_shift,
):
    sequences, row_count, width = inputs.shape
    held = attn_in.shape[0]
    groups = ffn_out.shape[0] // held
    wide = ffn_in.shape[1]
    pad = jnp.zeros((held, 128), BF16)
    attn_w = gather(join(attn_in, attn_out, 128))
    ffn_w = jnp.concatenate(
        [ffn_out[at * held : (at + 1) * held] for at in range(groups)] + [ffn_in, pad], 1
    )
    ffn_w = gather(ffn_w)
    w1_at, w2_at = wide, 0
    self_at, cross_at = (6, 0, 1, 2), (7, 3, 4, 5)

    ramp = (4.0 * step.astype(F32) / RAMP).reshape(1)
    bias = [attn_bias[at : at + 1] for at in range(6)]
    gain = [norm_gain[at : at + 1] for at in range(3)]
    shift = [norm_shift[at : at + 1] for at in range(3)]
    tokens, states = inputs.reshape(-1, width), encoder.reshape(-1, width)
    target_length = jnp.sum((target_mask > 0).astype(jnp.int32)).reshape(1)

    *self_saved, self_ctx, self_expo, self_inverse = self_forward(
        target_length, tokens, attn_w, bias[0], bias[1]
    )
    normal1, scale1, *cross_saved, cross_ctx, cross_expo, cross_inverse = cross_forward(
        source_lengths,
        tokens,
        self_ctx,
        states,
        attn_w,
        self_at[:1] + cross_at[1:],
        (bias[2], gain[0], shift[0], bias[3], bias[4]),
    )
    token_total = sequences * row_count * lax.axis_size("fsdp") * lax.axis_size("dp")
    normal2, hidden2, adapt_in, adapt_act, adapt_slope, base, scale2, scale_a = post_cross(
        ramp,
        normal1,
        cross_ctx,
        attn_w,
        cross_at[0],
        adapter_down,
        adapter_up,
        (bias[5], gain[0], shift[0], gain[1], shift[1], ffn_out_bias[None])
        + (adapter_gain[None], adapter_shift[None], adapter_up_bias[None]),
        adapter_down_bias[None],
    )
    slope, layer_out, grad_ffn, grad_rest, adapter_grads = middle(
        ramp,
        hidden2,
        ffn_w,
        w2_at,
        w1_at,
        ffn_in_bias[None],
        scale_a,
        (gain[2], shift[2], adapter_gain[None], adapter_shift[None]),
        (base, grad_out.reshape(-1, width), adapt_slope, adapter_up, adapt_act, adapter_down, adapt_in),
        held,
        1.0 / math.sqrt(token_total),
    )
    scattered = lax.psum_scatter(adapter_grads, "fsdp", scatter_dimension=0, tiled=True)
    grad_sum1, low_sum1, *cross_grads = ffn_cross_backward(
        grad_ffn,
        ffn_w,
        w2_at,
        w1_at,
        slope,
        grad_rest,
        normal2,
        scale2,
        gain[1],
        normal1,
        scale1,
        gain[0],
        attn_w,
        cross_at,
        (*cross_saved, cross_ctx, cross_expo, cross_inverse),
        held,
    )
    scattered, low_sum1 = lax.optimization_barrier((scattered, low_sum1))
    adapter_grads = gather(sum_over(scattered, "dp"))
    grad_input, grad_encoder = self_backward(
        grad_sum1,
        low_sum1,
        cross_grads,
        attn_w,
        self_at,
        cross_at,
        (*self_saved, self_ctx, self_expo, self_inverse),
    )
    grad_down, grad_up, up_bias, grad_gain, grad_shift, down_bias = unpack(
        adapter_grads, adapter_down.shape
    )
    return (
        layer_out.reshape(inputs.shape),
        grad_input.reshape(inputs.shape),
        grad_encoder.reshape(encoder.shape),
        grad_down,
        down_bias.reshape(-1),
        grad_up,
        up_bias.reshape(-1),
        grad_gain.reshape(-1),
        grad_shift.reshape(-1),
    )


def solution(mesh):
    batch = P(("fsdp", "dp"), None, None)
    split = P("fsdp", None)
    placed = (
        (batch,) * 3
        + (P(("fsdp", "dp"), None), P(("fsdp", "dp")), P())
        + (split, split, split, P(), split)
        + (P(),) * 10
    )
    return jax.shard_map(
        local,
        mesh=mesh,
        in_specs=placed,
        out_specs=(batch,) * 3 + (P(),) * 6,
        check_vma=False,
    )
```

```python
import functools
import math

import jax
import jax.numpy as jnp
from jax import lax
from jax.experimental import pallas as pl
from jax.experimental.pallas import tpu as pltpu
from jax.sharding import PartitionSpec as P

HEADS = 16
RAMP = 1000
EPS = 1e-05
F32 = jnp.float32
BF16 = jnp.bfloat16
VMEM_LIMIT = 58 * 2**20


def dot(left, right, left_dim, right_dim):
    return lax.dot_general(
        left, right, (((left_dim,), (right_dim,)), ((), ())), preferred_element_type=F32
    )


def call(kernel, name, grid, in_specs, out_specs, out_shape, flops, moved, exps=0, scratch=()):
    return pl.pallas_call(
        kernel,
        name=name,
        grid=grid,
        in_specs=in_specs,
        out_specs=out_specs,
        out_shape=out_shape,
        scratch_shapes=scratch,
        compiler_params=pltpu.CompilerParams(vmem_limit_bytes=VMEM_LIMIT),
        cost_estimate=pl.CostEstimate(
            flops=int(flops), bytes_accessed=int(moved), transcendentals=int(exps)
        ),
    )


def whole(shape):
    return pl.BlockSpec(shape, lambda *_: (0,) * len(shape), pipeline_mode=pl.Buffered(1))


def columns(rows, width, first=0):
    return pl.BlockSpec((rows, width), lambda i: (0, i + first))


def square(width, at):
    return pl.BlockSpec((width, width), lambda i: (0, at), pipeline_mode=pl.Buffered(1))


def normalize(values):
    center = values - jnp.mean(values, -1, keepdims=True)
    scale = lax.rsqrt(jnp.mean(center * center, -1, keepdims=True) + EPS)
    return center * scale, scale


def normalize_back(normal, scale, grad):
    return scale * (
        grad
        - jnp.mean(grad, -1, keepdims=True)
        - normal * jnp.mean(grad * normal, -1, keepdims=True)
    )


def split_three(values):
    high = values.astype(BF16).astype(F32)
    middle = (values - high).astype(BF16).astype(F32)
    return high, middle, values - high - middle


GROUP = 4
CHUNK = 256
SIZE = 64


def attend_forward(causal, ahead, q_ref, k_ref, v_ref, length, ctx_ref, expo_ref, inverse_ref):
    rows, keys = q_ref.shape[0], k_ref.shape[0]
    width = 2 * SIZE
    lane = lax.broadcasted_iota(jnp.int32, (rows, width), 1)
    key_lane = lax.broadcasted_iota(jnp.int32, (keys, width), 1)
    key_row = lax.broadcasted_iota(jnp.int32, (keys, width), 0)
    picks = jnp.where(lane % SIZE == 0, 1.0, 0.0).astype(BF16)
    extra = jnp.where(key_row < length, 0.0, -1e30).astype(BF16)
    one = jnp.asarray(1.0, BF16)
    left = lane[:CHUNK] < SIZE
    head_q, head_k, head_v = [], [], []
    for at in range(0, q_ref.shape[1], width):
        queries = q_ref[:, at : at + width]
        key_rows, value_rows = k_ref[:, at : at + width], v_ref[:, at : at + width]
        head_q += [jnp.where(lane < SIZE, queries, picks), jnp.where(lane < SIZE, picks, queries)]
        head_k += [
            jnp.where(key_lane < SIZE, key_rows, extra),
            jnp.where(key_lane < SIZE, extra, key_rows),
        ]
        head_v += [
            jnp.where(key_lane < SIZE, value_rows, one),
            jnp.where(key_lane < SIZE, one, value_rows),
        ]

    def scores(at, head):
        low, high = at * CHUNK, (at + 1) * CHUNK
        live = high if causal else keys
        found = dot(head_q[head][low:high], head_k[head][:live], 1, 1)
        if not causal:
            return found
        query_at = lax.broadcasted_iota(jnp.int32, (CHUNK, CHUNK), 0)
        key_at = lax.broadcasted_iota(jnp.int32, (CHUNK, CHUNK), 1)
        edge = jnp.where(key_at <= query_at, found[:, low:high], -1e30)
        return jnp.concatenate([found[:, :low], edge], 1) if low else edge

    done, waiting = {}, []

    def finish(at, head, found):
        low, high = at * CHUNK, (at + 1) * CHUNK
        live = found.shape[1]
        top = jnp.max(found, 1, keepdims=True)
        expo = jnp.exp(found - top).astype(BF16)
        expo_ref[head, low:high, :live] = expo
        done[head] = dot(expo, head_v[head][:live], 1, 0)
        if head % 2:
            first, second = done[head - 1], done[head]
            inverse = 1.0 / jnp.where(left, pltpu.roll(first, SIZE, 1), pltpu.roll(second, SIZE, 1))
            span = slice(head // 2 * width, (head // 2 + 1) * width)
            inverse_ref[low:high, span] = inverse.astype(BF16)
            ctx_ref[low:high, span] = (jnp.where(left, first, second) * inverse).astype(BF16)

    for pair in range(len(head_q) // 2):
        for at in range(rows // CHUNK):
            for head in (2 * pair, 2 * pair + 1):
                waiting.append((at, head, scores(at, head)))
                if len(waiting) > ahead:
                    finish(*waiting.pop(0))
    for unit in waiting:
        finish(*unit)


def attend_backward(
    causal, q_ref, k_ref, v_ref, ctx_ref, grad_ref, expo_ref, inverse_ref, dq_ref, dk_ref, dv_ref, s_scr,
    before, after,
):
    rows, keys = q_ref.shape[0], k_ref.shape[0]
    width = 2 * SIZE
    count = rows // CHUNK
    pairs = q_ref.shape[1] // width
    lane = lax.broadcasted_iota(jnp.int32, (rows, width), 1)
    key_lane = lax.broadcasted_iota(jnp.int32, (keys, width), 1)
    place, key_place = lane % SIZE, key_lane % SIZE
    ones = jnp.where((key_place >= 1) & (key_place <= 3), 1.0, 0.0).astype(BF16)
    from_lane = lax.broadcasted_iota(jnp.int32, (2 * width, width), 0) % width
    to_lane = lax.broadcasted_iota(jnp.int32, (2 * width, width), 1)
    swap = jnp.where((from_lane < SIZE) != (to_lane < SIZE), 1.0, 0.0).astype(BF16)

    def prepare(pair):
        span = slice(pair * width, (pair + 1) * width)
        value_rows = v_ref[:, span]
        grads = (grad_ref[:, span].astype(F32) * inverse_ref[:, span].astype(F32)).astype(BF16)
        products = grads.astype(F32) * ctx_ref[:, span].astype(F32)
        high = products.astype(BF16)
        low = (products - high.astype(F32)).astype(BF16)
        parts = split_three(-dot(jnp.concatenate([high, low], 1), swap, 1, 0))
        packed = jnp.zeros((rows, width), F32)
        for index, part in enumerate(parts):
            packed = jnp.where(place == index + 1, part, packed)
        packed = packed.astype(BF16)
        head_g = [jnp.where(lane < SIZE, grads, packed), jnp.where(lane < SIZE, packed, grads)]
        head_v = [
            jnp.where(key_lane < SIZE, value_rows, ones),
            jnp.where(key_lane < SIZE, ones, value_rows),
        ]
        return head_g, head_v, q_ref[:, span].T, grads.T

    def multiply(pair, head_g, head_v):
        span = slice(pair * width, (pair + 1) * width)
        key_rows = k_ref[:, span]
        grad_q, waiting = {}, []

        def finish(at, head, grad_p):
            low, high = at * CHUNK, (at + 1) * CHUNK
            live = grad_p.shape[1]
            expo = expo_ref[2 * pair + head, low:high, :live]
            grad_s = (expo.astype(F32) * grad_p).astype(BF16)
            s_scr[head, low:high, :live] = grad_s
            grad_q[head] = dot(grad_s, key_rows[:live], 1, 0)
            if head:
                both = jnp.where(lane[low:high] < SIZE, grad_q[0], grad_q[1])
                dq_ref[low:high, span] = (both * SIZE**-0.5).astype(BF16)

        for at in range(count):
            for head in range(2):
                low, high = at * CHUNK, (at + 1) * CHUNK
                live = high if causal else keys
                waiting.append((at, head, dot(head_g[head][low:high], head_v[head][:live], 1, 1)))
                if len(waiting) > 1:
                    finish(*waiting.pop(0))
        for unit in waiting:
            finish(*unit)

    def collect(pair, queries_t, grads_t):
        span = slice(pair * width, (pair + 1) * width)
        step = CHUNK if causal else keys
        for source, saved, first, to in (
            (grads_t, expo_ref, 2 * pair, dv_ref),
            (queries_t, s_scr, 0, dk_ref),
        ):
            for low in range(0, keys, step):
                start = low if causal else 0
                parts = [
                    dot(
                        source[head * SIZE : (head + 1) * SIZE, start:],
                        saved[first + head, start:, low : low + step],
                        1,
                        0,
                    )
                    for head in range(2)
                ]
                to[low : low + step, span] = jnp.concatenate(parts, 0).T.astype(BF16)

    ready = prepare(0)
    for pair in range(pairs):
        head_g, head_v, queries_t, grads_t = ready
        before(pair)
        multiply(pair, head_g, head_v)
        more = pair + 1 < pairs
        if causal and more:
            ready = prepare(pair + 1)
        collect(pair, queries_t, grads_t)
        if more and not causal:
            ready = prepare(pair + 1)
        after(pair)


def parts_of(rows):
    return [slice(at, at + CHUNK) for at in range(0, rows, CHUNK)]


def wide_scale(scale):
    return jnp.broadcast_to(scale, (scale.shape[0], 128))


def self_forward_kernel(
    length_ref, x_ref, wq_ref, wk_ref, wv_ref, bq_ref, bv_ref,
    q_ref, k_ref, v_ref, ctx_ref, expo_ref, inverse_ref,
):
    scale = jnp.asarray(SIZE**-0.5, BF16)
    for span in parts_of(x_ref.shape[0]):
        rows = x_ref[span]
        q_ref[span] = (dot(rows, wq_ref[...], 1, 0) + bq_ref[...]).astype(BF16) * scale
        k_ref[span] = dot(rows, wk_ref[...], 1, 0).astype(BF16)
        v_ref[span] = (dot(rows, wv_ref[...], 1, 0) + bv_ref[...]).astype(BF16)
    attend_forward(
        True, 2, q_ref, k_ref, v_ref, length_ref[0], ctx_ref, expo_ref, inverse_ref
    )


def anywhere():
    return pl.BlockSpec(memory_space=pl.ANY)


def scalar():
    return pl.BlockSpec(memory_space=pltpu.SMEM)


def attend_out(rows, keys, width):
    group = GROUP * SIZE
    heads = width // SIZE
    specs = (
        [columns(rows, group)]
        + [columns(keys, group)] * 2
        + [columns(rows, group)]
        + [pl.BlockSpec((GROUP, rows, keys), lambda i: (i, 0, 0)), columns(rows, group)]
    )
    shapes = (
        [jax.ShapeDtypeStruct((rows, width), BF16)]
        + [jax.ShapeDtypeStruct((keys, width), BF16)] * 2
        + [jax.ShapeDtypeStruct((rows, width), BF16)]
        + [
            jax.ShapeDtypeStruct((heads, rows, keys), BF16),
            jax.ShapeDtypeStruct((rows, width), BF16),
        ]
    )
    return specs, shapes


def self_forward(length, values, weights, q_bias, v_bias):
    rows, width = values.shape
    group = GROUP * SIZE
    per = width // group
    specs, shapes = attend_out(rows, rows, width)
    return call(
        self_forward_kernel,
        "self_forward",
        (per,),
        [scalar(), whole((rows, width))]
        + [columns(width, group, at * per) for at in range(3)]
        + [columns(1, group)] * 2,
        specs,
        shapes,
        6 * rows * width * width + 4 * rows * rows * width,
        18 * rows * width + 6 * width * width + 32 * rows * rows,
        rows * rows * HEADS,
    )(length, values, weights, weights, weights, q_bias, v_bias)


def cross_forward_kernel(
    length_ref, x_ref, sctx_ref, states_ref, wo_ref, wq_ref, wk_ref, wv_ref,
    bo_ref, gain_ref, shift_ref, bq_ref, bv_ref,
    normal_ref, scale_ref, q_ref, k_ref, v_ref, ctx_ref, expo_ref, inverse_ref, hidden_scr,
):
    spans = parts_of(x_ref.shape[0])

    @pl.when(pl.program_id(0) == 0)
    def _():
        sums = [
            x_ref[span].astype(F32) + dot(sctx_ref[span], wo_ref[...], 1, 0) + bo_ref[...]
            for span in spans
        ]
        for span, total in zip(spans, sums):
            normal, scale = normalize(total)
            normal_ref[span] = normal
            scale_ref[span] = wide_scale(scale)
            hidden_scr[span] = (normal * gain_ref[...] + shift_ref[...]).astype(BF16)

    size = jnp.asarray(SIZE**-0.5, BF16)
    for span in parts_of(states_ref.shape[0]):
        rows = states_ref[span]
        k_ref[span] = dot(rows, wk_ref[...], 1, 0).astype(BF16)
        v_ref[span] = (dot(rows, wv_ref[...], 1, 0) + bv_ref[...]).astype(BF16)
    for span in spans:
        q_ref[span] = (dot(hidden_scr[span], wq_ref[...], 1, 0) + bq_ref[...]).astype(BF16) * size
    attend_forward(
        False, 2, q_ref, k_ref, v_ref, length_ref[0], ctx_ref, expo_ref, inverse_ref
    )


def cross_forward(length, values, context, states, weights, at, vectors):
    rows, width = values.shape
    keys = states.shape[0]
    group = GROUP * SIZE
    per = width // group
    specs, shapes = attend_out(rows, keys, width)
    return call(
        cross_forward_kernel,
        "cross_forward",
        (per,),
        [scalar(), whole((rows, width)), whole((rows, width)), whole((keys, width))]
        + [square(width, at[0])]
        + [columns(width, group, first * per) for first in at[1:]]
        + [whole((1, width))] * 3
        + [columns(1, group)] * 2,
        [whole((rows, width)), whole((rows, 128))] + specs,
        [jax.ShapeDtypeStruct((rows, width), F32), jax.ShapeDtypeStruct((rows, 128), F32)] + shapes,
        8 * rows * width * width + 4 * rows * keys * width,
        26 * rows * width + 8 * width * width + 32 * rows * keys,
        rows * keys * HEADS,
        [pltpu.VMEM((rows, width), BF16)],
    )(length, values, context, states, weights, weights, weights, weights, *vectors)


FFN_STEP = 1024
FFN_BACK_STEP = 512


def second_block(w_ref, held, width):
    pieces = []
    for at in range(0, w_ref.shape[0], held):
        for group in range(w_ref.shape[1] // width):
            pieces.append(w_ref[at : at + held, group * width : (group + 1) * width])
    return jnp.concatenate(pieces, 0)


def in_turn(units, finish):
    waiting = None
    for first, span in units:
        value = first(span)
        if waiting is not None:
            finish(*waiting)
        waiting = (span, value)
    finish(*waiting)


def post_cross_kernel(
    ramp_ref, n1_ref, ctx_ref, wo_ref, down_ref, up_ref,
    bo_ref, gain1_ref, shift1_ref, gain2_ref, shift2_ref, b2_ref, gain_a_ref, shift_a_ref, up_b_ref,
    down_b_ref,
    normal_ref, hidden_ref, in_ref, act_ref, slope_ref, base_ref, scale_ref, scale_a_ref,
):
    spans = parts_of(n1_ref.shape[0])
    sums = [dot(ctx_ref[span], wo_ref[...], 1, 0) + bo_ref[...] for span in spans]
    for span, total in zip(spans, sums):
        normal, scale = normalize(total + (n1_ref[span] * gain1_ref[...] + shift1_ref[...]))
        normal_ref[span] = normal
        hidden = normal * gain2_ref[...] + shift2_ref[...]
        hidden_ref[span] = hidden.astype(BF16)
        base_ref[span] = hidden + b2_ref[...] + ramp_ref[0] * up_b_ref[...]
        normal_a, scale_a = normalize(hidden)
        in_ref[span] = (normal_a * gain_a_ref[...] + shift_a_ref[...]).astype(BF16)
        scale_ref[span] = wide_scale(scale)
        scale_a_ref[span] = wide_scale(scale_a)
    for span in spans:
        lower = dot(in_ref[span], down_ref[...], 1, 0) + down_b_ref[...]
        gate = 1.0 / (1.0 + jnp.exp(-lower))
        act_ref[span] = (lower * gate).astype(BF16)
        slope_ref[span] = (gate * (1.0 + lower * (1.0 - gate))).astype(BF16)
    for span in spans:
        base_ref[span] += ramp_ref[0] * dot(act_ref[span], up_ref[...], 1, 0)


def post_cross(ramp, normal1, context, weights, wo_at, down, up, vectors, down_bias):
    rows, width = normal1.shape
    units = down.shape[1]
    step = 512

    def block(wide):
        return pl.BlockSpec((step, wide), lambda i: (i, 0))

    return call(
        post_cross_kernel,
        "post_cross",
        (rows // step,),
        [scalar(), block(width), block(width), square(width, wo_at), whole(down.shape), whole(up.shape)]
        + [whole((1, width))] * 9
        + [whole((1, units))],
        [block(width)] * 3 + [block(units)] * 2 + [block(width)] + [block(128)] * 2,
        [
            jax.ShapeDtypeStruct((rows, width), F32),
            jax.ShapeDtypeStruct((rows, width), BF16),
            jax.ShapeDtypeStruct((rows, width), BF16),
            jax.ShapeDtypeStruct((rows, units), BF16),
            jax.ShapeDtypeStruct((rows, units), BF16),
            jax.ShapeDtypeStruct((rows, width), F32),
            jax.ShapeDtypeStruct((rows, 128), F32),
            jax.ShapeDtypeStruct((rows, 128), F32),
        ],
        2 * rows * width * width + 4 * rows * width * units,
        22 * rows * width,
        rows * units,
    )(ramp, normal1, context, weights, down, up, *vectors, down_bias)


def middle_kernel(
    held, factor, ramp_ref, hidden_ref, w1_ref, w2_ref, b1_ref, scale_a_ref,
    gain3_ref, shift3_ref, gain_a_ref, shift_a_ref,
    base_in, go_in, slope_in, up_in, act_in, down_in, in_in,
    slope_ref, out_out, gffn_out, rest_out, grads_out,
    base_scr, go_scr, slope_scr, up_scr, act_scr, down_scr, in_scr,
    total_scr, out_scr, gffn_scr, branch_scr, lower_scr, grads_scr, in_sems, out_sems,
):
    rows, width = hidden_ref.shape
    units = down_in.shape[1]
    spans = parts_of(rows)
    step = pl.program_id(0)
    loads = moved(
        [
            (base_in, base_scr), (go_in, go_scr), (slope_in, slope_scr), (up_in, up_scr),
            (act_in, act_scr), (down_in, down_scr), (in_in, in_scr),
        ],
        in_sems,
    )

    @pl.when(step == 0)
    def _():
        total_scr[...] = jnp.zeros_like(total_scr)

    for at, part in enumerate((loads[:1], loads[1:4], loads[4:])):
        pl.when(step == at + 1)(functools.partial(start_all, part))

    def first(span):
        return dot(hidden_ref[span], w1_ref[...], 1, 0) + b1_ref[...]

    def finish(span, pre):
        phi = 0.5 + 0.5 * lax.erf(pre * (0.5**0.5))
        act = (pre * phi).astype(BF16)
        slope = phi + pre * (jnp.exp(pre * pre * -0.5) * (1.0 / math.sqrt(2.0 * math.pi)))
        slope_ref[span] = slope.astype(BF16)
        total_scr[span] += dot(act, second_block(w2_ref, held, width), 1, 0)

    in_turn([(first, span) for span in spans], finish)

    @pl.when(step == pl.num_programs(0) - 1)
    def _():
        ramp = ramp_ref[0]
        wait_all(loads[:4])
        main, beside = pl.ds(0, width), pl.ds(width, 128)
        outs = moved(
            [
                (out_scr, out_out),
                (gffn_scr, gffn_out),
                (grads_scr.at[:, main], grads_out.at[:, main]),
            ],
            out_sems,
        )
        kind = grads_scr.dtype
        sums = [jnp.zeros((1, width), F32)] * 3 + [jnp.zeros((1, units), F32)]

        def norm_three(span):
            normal, scale = normalize(total_scr[span] + base_scr[span])
            out_scr[span] = (normal * gain3_ref[...] + shift3_ref[...]).astype(BF16)
            grad = normalize_back(normal, scale, gain3_ref[...] * go_scr[span].astype(F32))
            gffn_scr[span] = grad.astype(BF16)
            total_scr[span] = grad
            grad_branch = (ramp * grad).astype(BF16)
            branch_scr[span] = grad_branch
            sums[0] = sums[0] + jnp.sum(grad_branch.astype(F32), 0, keepdims=True)

        def adapter_back(span):
            grad_act = dot(branch_scr[span], up_scr[...], 1, 1).astype(BF16).astype(F32)
            grad_lower = (slope_scr[span].astype(F32) * grad_act).astype(BF16)
            lower_scr[span] = grad_lower
            sums[3] = sums[3] + jnp.sum(grad_lower.astype(F32), 0, keepdims=True)

        for span in spans:
            norm_three(span)
            adapter_back(span)
        start_all(outs[:2])
        wait_all(loads[4:])
        grads_scr[0:units, 0:width] = (dot(act_scr[...], branch_scr[...], 0, 0) * factor).astype(kind)
        for at, span in enumerate(spans):
            grad_adapt = dot(lower_scr[span], down_scr[...], 1, 1)
            normal_a = (in_scr[span].astype(F32) - shift_a_ref[...]) * (1.0 / gain_a_ref[...])
            scale_a = scale_a_ref[span, 0:1]
            total_scr[span] += normalize_back(normal_a, scale_a, gain_a_ref[...] * grad_adapt)
            outs.append(
                pltpu.make_async_copy(total_scr.at[span], rest_out.at[span], out_sems.at[3 + at])
            )
            outs[-1].start()
            sums[1] = sums[1] + jnp.sum(grad_adapt * normal_a, 0, keepdims=True)
            sums[2] = sums[2] + jnp.sum(grad_adapt, 0, keepdims=True)
        for at in range(0, width, units):
            grads_scr[units : 2 * units, at : at + units] = (
                dot(in_scr[:, at : at + units], lower_scr[...], 0, 0) * factor
            ).astype(kind)
        outs[2].start()
        vectors = []
        for row in sums:
            row = row * factor
            vectors += [row[:, low : low + 128] for low in range(0, row.shape[1], 128)]
        vectors += [jnp.zeros((1, 128), F32)] * (4 * width // 128 - len(vectors))
        small = jnp.concatenate(vectors, 0).astype(kind)
        lines = small.shape[0]
        grads_scr[0:lines, width:] = small
        grads_scr[lines:, width:] = jnp.zeros((2 * units - lines, 128), kind)
        outs.append(
            pltpu.make_async_copy(
                grads_scr.at[:, beside], grads_out.at[:, beside], out_sems.at[3 + len(spans)]
            )
        )
        outs[-1].start()
        wait_all(outs)


def middle(
    ramp, hidden, ffn_w, w2_at, w1_at, first_bias, scale_a, vectors, late, held, factor
):
    rows, width = hidden.shape
    wide = first_bias.shape[1]
    units = late[2].shape[1]
    step = FFN_STEP
    groups = wide // width
    return call(
        functools.partial(middle_kernel, held, factor),
        "middle",
        (wide // step,),
        [
            scalar(),
            whole((rows, width)),
            columns(width, step, w1_at // step),
            pl.BlockSpec((step // groups, wide), lambda i: (i, w2_at // wide)),
            columns(1, step),
            whole((rows, 128)),
        ]
        + [whole((1, width))] * 4
        + [anywhere()] * len(late),
        [columns(rows, step)] + [anywhere()] * 4,
        [
            jax.ShapeDtypeStruct((rows, wide), BF16),
            jax.ShapeDtypeStruct((rows, width), BF16),
            jax.ShapeDtypeStruct((rows, width), BF16),
            jax.ShapeDtypeStruct((rows, width), F32),
            jax.ShapeDtypeStruct((2 * units, width + 128), BF16),
        ],
        4 * rows * width * wide + 8 * rows * width * units,
        22 * rows * width + 4 * width * wide + 2 * rows * wide + 12 * width * units,
        2 * rows * wide,
        [pltpu.VMEM(value.shape, value.dtype) for value in late]
        + [
            pltpu.VMEM((rows, width), F32),
            pltpu.VMEM((rows, width), BF16),
            pltpu.VMEM((rows, width), BF16),
            pltpu.VMEM((rows, width), BF16),
            pltpu.VMEM((rows, units), BF16),
            pltpu.VMEM((2 * units, width + 128), BF16),
            pltpu.SemaphoreType.DMA((len(late),)),
            pltpu.SemaphoreType.DMA((4 + rows // CHUNK,)),
        ],
    )(ramp, hidden, ffn_w, ffn_w, first_bias, scale_a, *vectors, *late)


def moved(pairs, sems):
    return [
        pltpu.make_async_copy(source, target, sems.at[at])
        for at, (source, target) in enumerate(pairs)
    ]


def start_all(copies):
    for copy in copies:
        copy.start()


def wait_all(copies):
    for copy in copies:
        copy.wait()


def expo_loads(expo_ref, expo_scr, sems, group, count):
    def load(which, pair):
        heads = pl.ds(which * GROUP + 2 * pair, 2)
        return pltpu.make_async_copy(
            expo_ref.at[heads], expo_scr.at[pl.ds(2 * pair, 2)], sems.at[pair]
        )

    def begin():
        for pair in range(GROUP // 2):
            load(0, pair).start()

    def before(pair):
        load(group, pair).wait()

    def after(pair):
        @pl.when(group < count - 1)
        def _():
            load(group + 1, pair).start()

    return begin, before, after


def group_loads(pairs, sems):
    def copies(group, part):
        slot = lax.rem(group, 2)
        return [
            pltpu.make_async_copy(source(group), target.at[slot], sems.at[at, slot])
            for at, (source, target) in list(enumerate(pairs))[part]
        ]

    def start(group):
        start_all(copies(group, slice(None)))

    def wait(group, part):
        wait_all(copies(group, part))

    return start, wait


def column_group(ref, first=0):
    width = GROUP * SIZE
    return lambda group: ref.at[:, pl.ds(pl.multiple_of(group * width, width) + first, width)]


def row_group(ref, first, width):
    depth = GROUP * SIZE
    return lambda group: ref.at[
        pl.ds(pl.multiple_of(group * depth, depth), depth), pl.ds(first, width)
    ]


def ffn_cross_backward_kernel(
    held, ffn_steps, at,
    g_ref, w1_ref, w2_ref, slope_ref, start_ref, normal2_ref, scale2_ref, gain2_ref,
    normal1_ref, scale1_ref, gain1_ref, attn_ref, q_ref, k_ref, v_ref, ctx_ref, expo_ref, inverse_ref,
    sum_ref, sum_low_ref, dk_ref, dv_ref,
    total_scr, start_scr, normal_scr, low_scr, grad_scr, dq_scr, s_scr, expo_scr,
    in_sems, out_sems, expo_sems,
    wo_scr, wq_scr, q_scr, k_scr, v_scr, ctx_scr, inverse_scr, group_sems, scale2_scr, scale1_scr, scale_sems,
):
    rows, width = g_ref.shape
    spans = parts_of(rows)
    step, steps = pl.program_id(0), pl.num_programs(0)
    loads = moved([(start_ref, start_scr), (normal2_ref, normal_scr)], in_sems)
    late = pltpu.make_async_copy(normal1_ref, normal_scr, in_sems.at[2])
    scales = moved([(scale2_ref, scale2_scr), (scale1_ref, scale1_scr)], scale_sems)
    group, groups = step - ffn_steps, steps - ffn_steps
    begin, before, after = expo_loads(expo_ref, expo_scr, expo_sems, group, groups)
    start_group, wait_group = group_loads(
        [
            (row_group(attn_ref, at[0] * width, width), wo_scr),
            (column_group(q_ref), q_scr),
            (column_group(k_ref), k_scr),
            (column_group(v_ref), v_scr),
            (column_group(ctx_ref), ctx_scr),
            (column_group(inverse_ref), inverse_scr),
            (column_group(attn_ref, at[1] * width), wq_scr),
        ],
        group_sems,
    )

    @pl.when(step == 0)
    def _():
        total_scr[...] = jnp.zeros_like(total_scr)

    pl.when(step == 1)(loads[0].start)
    pl.when(step == ffn_steps // 2)(loads[1].start)
    pl.when(step == ffn_steps // 2 + 1)(functools.partial(start_all, scales))
    pl.when(step == ffn_steps - 2)(functools.partial(start_group, 0))

    def first(span):
        return dot(g_ref[span], second_block(w2_ref, held, width), 1, 1)

    def finish(span, grad_act):
        grad_pre = (slope_ref[span].astype(F32) * grad_act).astype(BF16)
        total_scr[span] += dot(grad_pre, w1_ref[...], 1, 1)

    @pl.when(step < ffn_steps - 1)
    def _():
        in_turn([(first, span) for span in spans], finish)

    @pl.when(step == ffn_steps - 1)
    def _():
        begin()
        wait_all(loads)
        wait_all(scales)

        def back(span):
            grad = normalize_back(
                normal_scr[span],
                scale2_scr[span, 0:1],
                gain2_ref[...] * (total_scr[span] + start_scr[span]),
            )
            total_scr[span] = grad
            low_scr[span] = grad.astype(BF16)

        held_act, done = None, []
        for span in [*spans, None]:
            grad_act = first(span) if span is not None else None
            if held_act is not None:
                finish(*held_act)
                done.append(held_act[0])
            held_act = (span, grad_act)
            if len(done) > 1:
                back(done.pop(0))
        back(done.pop(0))
        late.start()

    slot = lax.rem(step, 2) if ffn_steps % 2 == 0 else lax.rem(step + 1, 2)

    def add(span):
        total_scr[span] += dot(dq_scr[span], wq_scr[slot], 1, 1)

    @pl.when(step == ffn_steps)
    def _():
        dq_scr[...] = jnp.zeros_like(dq_scr)

    @pl.when(step >= ffn_steps)
    def _():
        wait_group(group, slice(None))
        for span in spans:
            grad_scr[span] = dot(low_scr[span], wo_scr[slot], 1, 1).astype(BF16)
        last_slot = jnp.where(group > 0, 1 - slot, slot)
        for span in spans:
            total_scr[span] += dot(dq_scr[span], wq_scr[last_slot], 1, 1)
        pl.when(group < groups - 1)(functools.partial(start_group, group + 1))
        attend_backward(
            False, q_scr.at[slot], k_scr.at[slot], v_scr.at[slot], ctx_scr.at[slot], grad_scr, expo_scr,
            inverse_scr.at[slot], dq_scr, dk_ref, dv_ref, s_scr, before, after,
        )

    last = step == steps - 1

    @pl.when(last)
    def _():
        late.wait()
        outs = []

        def back(span):
            grad = normalize_back(
                normal_scr[span], scale1_scr[span, 0:1], gain1_ref[...] * total_scr[span]
            )
            total_scr[span] = grad
            low_scr[span] = grad.astype(BF16)
            copies = moved(
                [(total_scr.at[span], sum_ref.at[span]), (low_scr.at[span], sum_low_ref.at[span])],
                out_sems.at[pl.ds(len(outs), 2)],
            )
            start_all(copies)
            outs.extend(copies)

        add(spans[0])
        for before_span, span in zip(spans, spans[1:]):
            add(span)
            back(before_span)
        back(spans[-1])
        wait_all(outs)


def self_backward_kernel(
    at, cross_at,
    g_ref, low_ref, cdk_ref, cdv_ref, attn_ref, q_ref, k_ref, v_ref, ctx_ref, expo_ref, inverse_ref,
    out_ref, states_ref,
    total_scr, states_scr, start_scr, low_scr, grad_scr, dq_scr, dk_scr, dv_scr, s_scr, expo_scr,
    in_sems, out_sems, expo_sems,
    wo_scr, wq_scr, wk_scr, wv_scr, q_scr, k_scr, v_scr, ctx_scr, inverse_scr,
    cdk_scr, cdv_scr, cwk_scr, cwv_scr, group_sems,
):
    width = low_ref.shape[1]
    spans = parts_of(low_ref.shape[0])
    step, steps = pl.program_id(0), pl.num_programs(0)
    slot = lax.rem(step, 2)
    load, low_load = moved([(g_ref, start_scr), (low_ref, low_scr)], in_sems)
    begin, before, after = expo_loads(expo_ref, expo_scr, expo_sems, step, steps)
    start_group, wait_group = group_loads(
        [
            (row_group(attn_ref, at[0] * width, width), wo_scr),
            (column_group(cdk_ref), cdk_scr),
            (column_group(attn_ref, cross_at[2] * width), cwk_scr),
            (column_group(cdv_ref), cdv_scr),
            (column_group(attn_ref, cross_at[3] * width), cwv_scr),
            (column_group(q_ref), q_scr),
            (column_group(k_ref), k_scr),
            (column_group(v_ref), v_scr),
            (column_group(ctx_ref), ctx_scr),
            (column_group(inverse_ref), inverse_scr),
            (column_group(attn_ref, at[1] * width), wq_scr),
            (column_group(attn_ref, at[2] * width), wk_scr),
            (column_group(attn_ref, at[3] * width), wv_scr),
        ],
        group_sems,
    )

    @pl.when(step == 0)
    def _():
        low_load.start()
        start_group(0)
        begin()
        total_scr[...] = jnp.zeros_like(total_scr)
        states_scr[...] = jnp.zeros_like(states_scr)

    pl.when(step == 1)(load.start)

    pl.when(step == 0)(low_load.wait)
    wait_group(step, slice(None))
    pl.when(step < steps - 1)(functools.partial(start_group, step + 1))
    for span in spans:
        grad_scr[span] = dot(low_scr[span], wo_scr[slot], 1, 1).astype(BF16)
    for span in parts_of(states_scr.shape[0]):
        states_scr[span] += dot(cdk_scr[slot, span], cwk_scr[slot], 1, 1) + dot(
            cdv_scr[slot, span], cwv_scr[slot], 1, 1
        )
    attend_backward(
        True, q_scr.at[slot], k_scr.at[slot], v_scr.at[slot], ctx_scr.at[slot], grad_scr, expo_scr,
        inverse_scr.at[slot], dq_scr, dk_scr, dv_scr, s_scr, before, after,
    )

    def back(span):
        return (
            dot(dq_scr[span], wq_scr[slot], 1, 1)
            + dot(dk_scr[span], wk_scr[slot], 1, 1)
            + dot(dv_scr[span], wv_scr[slot], 1, 1)
        )

    last = step == steps - 1

    @pl.when(jnp.logical_not(last))
    def _():
        for span in spans:
            total_scr[span] += back(span)

    @pl.when(last)
    def _():
        load.wait()
        outs = [pltpu.make_async_copy(states_scr, states_ref, out_sems.at[len(spans)])]
        outs[0].start()
        for index, span in enumerate(spans):
            total_scr[span] += start_scr[span] + back(span)
            outs.append(
                pltpu.make_async_copy(total_scr.at[span], out_ref.at[span], out_sems.at[index])
            )
            outs[-1].start()
        wait_all(outs)


def attend_scratch(rows, keys):
    return [
        pltpu.VMEM((2, rows, keys), BF16),
        pltpu.VMEM((GROUP, rows, keys), BF16),
        pltpu.SemaphoreType.DMA((3,)),
        pltpu.SemaphoreType.DMA((2 * rows // CHUNK,)),
        pltpu.SemaphoreType.DMA((GROUP // 2,)),
    ]


def group_scratch(rows, keys, width, weights):
    group = GROUP * SIZE
    return (
        [pltpu.VMEM((2, group, width), BF16)]
        + [pltpu.VMEM((2, width, group), BF16)] * weights
        + [pltpu.VMEM((2, rows, group), BF16)]
        + [pltpu.VMEM((2, keys, group), BF16)] * 2
        + [pltpu.VMEM((2, rows, group), BF16)] * 2
    )


def ffn_cross_backward(
    grads, ffn_w, w2_at, w1_at, slope, start, normal2, scale2, gain2, normal1, scale1, gain1, attn_w, at, saved,
    held,
):
    rows, width = grads.shape
    keys = saved[1].shape[0]
    wide = slope.shape[1]
    groups = wide // width
    block = FFN_BACK_STEP
    steps = wide // block
    group = GROUP * SIZE

    def unit(i):
        return jnp.minimum(i, steps - 1)

    def out(i):
        return (0, jnp.maximum(i - steps, 0))

    return call(
        functools.partial(ffn_cross_backward_kernel, held, steps, at),
        "ffn_cross_backward",
        (steps + width // group,),
        [
            whole((rows, width)),
            pl.BlockSpec((width, block), lambda i: (0, unit(i) + w1_at // block)),
            pl.BlockSpec((block // groups, wide), lambda i: (unit(i), w2_at // wide)),
            pl.BlockSpec((rows, block), lambda i: (0, unit(i))),
            anywhere(),
            anywhere(),
            anywhere(),
            whole((1, width)),
            anywhere(),
            anywhere(),
            whole((1, width)),
        ]
        + [anywhere()] * 7,
        [anywhere()] * 2 + [pl.BlockSpec((keys, group), out)] * 2,
        [
            jax.ShapeDtypeStruct((rows, width), F32),
            jax.ShapeDtypeStruct((rows, width), BF16),
            jax.ShapeDtypeStruct((keys, width), BF16),
            jax.ShapeDtypeStruct((keys, width), BF16),
        ],
        4 * rows * width * (width + wide) + 8 * rows * keys * width,
        48 * rows * width + 4 * width * (width + wide) + 2 * rows * wide + 32 * rows * keys,
        0,
        [pltpu.VMEM((rows, width), F32)] * 3
        + [pltpu.VMEM((rows, width), BF16)]
        + [pltpu.VMEM((rows, group), BF16)] * 2
        + attend_scratch(rows, keys)
        + group_scratch(rows, keys, width, 1)
        + [pltpu.SemaphoreType.DMA((7, 2))]
        + [pltpu.VMEM((rows, 128), F32)] * 2
        + [pltpu.SemaphoreType.DMA((2,))],
    )(
        grads, ffn_w, ffn_w, slope, start, normal2, scale2, gain2, normal1, scale1, gain1, attn_w, *saved
    )


def self_backward(grads, low, cross_grads, weights, at, cross_at, saved):
    rows, width = grads.shape
    keys = cross_grads[0].shape[0]
    group = GROUP * SIZE
    return call(
        functools.partial(self_backward_kernel, at, cross_at),
        "self_backward",
        (width // group,),
        [anywhere()] * 11,
        [anywhere()] * 2,
        [jax.ShapeDtypeStruct((rows, width), F32), jax.ShapeDtypeStruct((keys, width), F32)],
        8 * rows * width * width + 4 * keys * width * width + 4 * rows * rows * width,
        28 * rows * width + 12 * width * width + 32 * rows * rows,
        0,
        [pltpu.VMEM((rows, width), F32), pltpu.VMEM((keys, width), F32), pltpu.VMEM((rows, width), F32)]
        + [pltpu.VMEM((rows, width), BF16)]
        + [pltpu.VMEM((rows, group), BF16)] * 4
        + attend_scratch(rows, rows)
        + group_scratch(rows, rows, width, 3)
        + [pltpu.VMEM((2, keys, group), BF16)] * 2
        + [pltpu.VMEM((2, width, group), BF16)] * 2
        + [pltpu.SemaphoreType.DMA((13, 2))],
    )(grads, low, *cross_grads, weights, *saved)


def unpack_kernel(up_in, down_in, small_in, down_ref, up_ref, up_b_ref, gain_ref, shift_ref, down_b_ref):
    units = down_ref.shape[2]
    up_ref[...] = up_in[...].astype(F32)
    for at in range(down_ref.shape[0]):
        down_ref[at] = down_in[:, at * units : (at + 1) * units].astype(F32)

    @pl.when(pl.program_id(0) == 0)
    def _():
        small = small_in[...].astype(F32)
        per = up_b_ref.shape[1] // 128
        for at, ref in enumerate((up_b_ref, gain_ref, shift_ref, down_b_ref)):
            for part in range(ref.shape[1] // 128):
                row = at * per + part
                ref[:, part * 128 : (part + 1) * 128] = small[row : row + 1]


def unpack(grads, down_shape):
    width, units = down_shape
    halves = width // units
    steps = 2
    step = units // steps
    small = 4 * width // 128

    def fixed(shape):
        return pl.BlockSpec(shape, lambda i: (0, 0))

    down, *rest = call(
        unpack_kernel,
        "unpack",
        (steps,),
        [
            pl.BlockSpec((step, width), lambda i: (i, 0)),
            pl.BlockSpec((step, width), lambda i: (i + steps, 0)),
            pl.BlockSpec((small, 128), lambda i: (0, width // 128)),
        ],
        [
            pl.BlockSpec((halves, step, units), lambda i: (0, i, 0)),
            pl.BlockSpec((step, width), lambda i: (i, 0)),
        ]
        + [fixed((1, width))] * 3
        + [fixed((1, units))],
        [
            jax.ShapeDtypeStruct((halves, units, units), F32),
            jax.ShapeDtypeStruct((units, width), F32),
        ]
        + [jax.ShapeDtypeStruct((1, width), F32)] * 3
        + [jax.ShapeDtypeStruct((1, units), F32)],
        0,
        16 * width * units,
    )(grads, grads, grads)
    return down.reshape(down_shape), *rest


def join_kernel(first_ref, second_ref, out_ref, held_scr, in_sems, out_sems):
    rows = first_ref.shape[0]
    wide, more = first_ref.shape[1], second_ref.shape[1]
    parts = [pl.ds(at, rows // 2) for at in range(0, rows, rows // 2)]
    loads = []
    for at, part in enumerate(parts):
        loads.append(
            moved(
                [
                    (first_ref.at[part], held_scr.at[part, pl.ds(0, wide)]),
                    (second_ref.at[part], held_scr.at[part, pl.ds(wide, more)]),
                ],
                in_sems.at[at],
            )
        )
        start_all(loads[-1])
    held_scr[:, wide + more :] = jnp.zeros((rows, held_scr.shape[1] - wide - more), BF16)
    outs = moved([(held_scr.at[part], out_ref.at[part]) for part in parts], out_sems)
    for load, out in zip(loads, outs):
        wait_all(load)
        out.start()
    wait_all(outs)


def join(first, second, spare):
    rows = first.shape[0]
    shape = (rows, first.shape[1] + second.shape[1] + spare)
    return call(
        join_kernel,
        "join",
        (),
        [anywhere()] * 2,
        anywhere(),
        jax.ShapeDtypeStruct(shape, BF16),
        0,
        4 * rows * shape[1],
        0,
        [
            pltpu.VMEM(shape, BF16),
            pltpu.SemaphoreType.DMA((2, 2)),
            pltpu.SemaphoreType.DMA((2,)),
        ],
    )(first, second)


def gather(shard):
    return lax.all_gather(shard, "fsdp", axis=0, tiled=True)


def sum_over(part, axis):
    count = lax.axis_size(axis)
    total, travel = part.astype(F32), part
    for _ in range(count - 1):
        travel = lax.ppermute(travel, axis, [(at, (at + 1) % count) for at in range(count)])
        total = total + travel.astype(F32)
    return total.astype(part.dtype)


def local(
    inputs,
    encoder,
    grad_out,
    target_mask,
    source_lengths,
    step,
    attn_in,
    attn_out,
    ffn_in,
    ffn_in_bias,
    ffn_out,
    ffn_out_bias,
    attn_bias,
    norm_gain,
    norm_shift,
    adapter_down,
    adapter_down_bias,
    adapter_up,
    adapter_up_bias,
    adapter_gain,
    adapter_shift,
):
    sequences, row_count, width = inputs.shape
    held = attn_in.shape[0]
    groups = ffn_out.shape[0] // held
    wide = ffn_in.shape[1]
    pad = jnp.zeros((held, 128), BF16)
    attn_w = gather(join(attn_in, attn_out, 128))
    ffn_w = jnp.concatenate(
        [ffn_out[at * held : (at + 1) * held] for at in range(groups)] + [ffn_in, pad], 1
    )
    ffn_w = gather(ffn_w)
    w1_at, w2_at = wide, 0
    self_at, cross_at = (6, 0, 1, 2), (7, 3, 4, 5)

    ramp = (4.0 * step.astype(F32) / RAMP).reshape(1)
    bias = [attn_bias[at : at + 1] for at in range(6)]
    gain = [norm_gain[at : at + 1] for at in range(3)]
    shift = [norm_shift[at : at + 1] for at in range(3)]
    tokens, states = inputs.reshape(-1, width), encoder.reshape(-1, width)
    target_length = jnp.sum((target_mask > 0).astype(jnp.int32)).reshape(1)

    *self_saved, self_ctx, self_expo, self_inverse = self_forward(
        target_length, tokens, attn_w, bias[0], bias[1]
    )
    normal1, scale1, *cross_saved, cross_ctx, cross_expo, cross_inverse = cross_forward(
        source_lengths,
        tokens,
        self_ctx,
        states,
        attn_w,
        self_at[:1] + cross_at[1:],
        (bias[2], gain[0], shift[0], bias[3], bias[4]),
    )
    token_total = sequences * row_count * lax.axis_size("fsdp") * lax.axis_size("dp")
    normal2, hidden2, adapt_in, adapt_act, adapt_slope, base, scale2, scale_a = post_cross(
        ramp,
        normal1,
        cross_ctx,
        attn_w,
        cross_at[0],
        adapter_down,
        adapter_up,
        (bias[5], gain[0], shift[0], gain[1], shift[1], ffn_out_bias[None])
        + (adapter_gain[None], adapter_shift[None], adapter_up_bias[None]),
        adapter_down_bias[None],
    )
    slope, layer_out, grad_ffn, grad_rest, adapter_grads = middle(
        ramp,
        hidden2,
        ffn_w,
        w2_at,
        w1_at,
        ffn_in_bias[None],
        scale_a,
        (gain[2], shift[2], adapter_gain[None], adapter_shift[None]),
        (base, grad_out.reshape(-1, width), adapt_slope, adapter_up, adapt_act, adapter_down, adapt_in),
        held,
        1.0 / math.sqrt(token_total),
    )
    scattered = lax.psum_scatter(adapter_grads, "fsdp", scatter_dimension=0, tiled=True)
    grad_sum1, low_sum1, *cross_grads = ffn_cross_backward(
        grad_ffn,
        ffn_w,
        w2_at,
        w1_at,
        slope,
        grad_rest,
        normal2,
        scale2,
        gain[1],
        normal1,
        scale1,
        gain[0],
        attn_w,
        cross_at,
        (*cross_saved, cross_ctx, cross_expo, cross_inverse),
        held,
    )
    scattered, low_sum1 = lax.optimization_barrier((scattered, low_sum1))
    adapter_grads = gather(sum_over(scattered, "dp"))
    grad_input, grad_encoder = self_backward(
        grad_sum1,
        low_sum1,
        cross_grads,
        attn_w,
        self_at,
        cross_at,
        (*self_saved, self_ctx, self_expo, self_inverse),
    )
    grad_down, grad_up, up_bias, grad_gain, grad_shift, down_bias = unpack(
        adapter_grads, adapter_down.shape
    )
    return (
        layer_out.reshape(inputs.shape),
        grad_input.reshape(inputs.shape),
        grad_encoder.reshape(encoder.shape),
        grad_down,
        down_bias.reshape(-1),
        grad_up,
        up_bias.reshape(-1),
        grad_gain.reshape(-1),
        grad_shift.reshape(-1),
    )


def solution(mesh):
    batch = P(("fsdp", "dp"), None, None)
    split = P("fsdp", None)
    placed = (
        (batch,) * 3
        + (P(("fsdp", "dp"), None), P(("fsdp", "dp")), P())
        + (split, split, split, P(), split)
        + (P(),) * 10
    )
    return jax.shard_map(
        local,
        mesh=mesh,
        in_specs=placed,
        out_specs=(batch,) * 3 + (P(),) * 6,
        check_vma=False,
    )
```
